128 devices in a mesh: grp: 16 (over z, y_hi, core), blk: 8 (over y_lo, x).
Axes of the slice: x: 4, y: 4 (y_hi: 2, y_lo: 2; y = y_hi * 2 + y_lo), z: 4, core: 2. Of those that a mesh axis runs over, the one named last changes fastest.
Arguments:
- embed: bfloat16 [65536, 1024], P(('grp', 'blk')), may hold values from -6 to 6
- owner: int32 [65536, 1], P(('grp', 'blk')), may hold values from 0 to 15; in each aligned block of 512 rows (0 to 511, 512 to 1023, ...) at most 64 rows name the same one
- local_id: int32 [65536], P(('grp', 'blk')), may hold values from 0 to 127
- rank: int32 [65536], P(('grp', 'blk')), may hold values from 0 to 65535, each once
Outputs:
- highest: float32 [65536], P(('grp', 'blk'))
The draws below stay inside these ranges and needn't reach their ends.
Inputs may be any that keep to these rules, and one draw needn't show every extreme that they name: `owner`: among the 512 rows of one device, at most 64 name one group. `rank`: every value appears exactly once.
All inputs are finite; a program needn't handle non-finite values.
Results may differ from the reference program's by a relative error of at most 0.00068.
Values may be sent and summed in bfloat16 or wider, within the bound.
No kernel may reach another device: no remote copies, remote signals or barrier semaphores. Data moves between devices by JAX's collectives and lax.ppermute only.
A program may use at most 64 MiB of HBM per device.

```python
import math
import jax
import jax.numpy as jnp
import numpy as np
from jax import lax

D = 1024
ROWS_DEV = 512
CAP = 64
CL_GRP = 128
ROWS = 65536
N_GRP = 16
N_BLK = 8


def set_ends(entries, own_key, low, high):
    place = [jax.random.randint(jax.random.fold_in(own_key, axis), (), 0, length) for axis, length in enumerate(entries.shape)]
    widest = entries.shape.index(max(entries.shape))
    beside = place[:widest] + [(place[widest] + 1) % entries.shape[widest]] + place[widest + 1:]
    return entries.at[tuple(place)].set(low).at[tuple(beside)].set(high)


def block_scale(rng, extent, pieces, smallest, top_value):
    def one(dim, shards_of):
        steps = jax.random.uniform(jax.random.fold_in(jax.random.fold_in(rng, 6), dim), (shards_of,), jnp.float32, smallest / len(pieces), top_value / len(pieces))
        return jnp.repeat(jnp.exp(steps), extent[dim] // shards_of).reshape((-1,) + (1,) * (len(extent) - dim - 1))

    gain = one(*pieces[0])
    for cut in pieces[1:]:
        gain = gain * one(*cut)
    return gain


def rank_table(count, lean):
    weights = [(1 << 20) // math.isqrt(rank ** lean) + 1 for rank in range(1, count + 1)]
    scale = 1 + sum(weights) // (1 << 30)
    return np.cumsum(np.array([max(1, weight // scale) for weight in weights]))


def ranked_ids(rng, shape, count, slope):
    grid = rank_table(count, slope)
    pick = jax.random.randint(jax.random.fold_in(rng, 1), shape, 0, int(grid[count - 1]))
    grade = jnp.searchsorted(jnp.asarray(grid, jnp.int32), pick, side="right")
    return jax.random.permutation(jax.random.fold_in(rng, 2), count)[grade].astype(jnp.int32)


def shared_out(key, own, number, rows, amount, top, most, lean):
    order = jax.random.permutation(key, amount)
    packed, usual = shares(amount, rows * top, most, lean, True), shares(amount, rows * top, most, lean, False)
    places = jnp.arange(amount)

    def named(sizes, rotation):
        used = int((sizes > 0).sum())
        fixed = max(1, used // 4)
        moved = fixed + (places - fixed + rotation * (used - fixed)) % max(1, amount - fixed)
        return jnp.zeros((amount,), jnp.int32).at[order[jnp.where(places < fixed, places, moved)]].set(jnp.asarray(sizes, jnp.int32))

    sizes = jnp.where(number % 4 == 0, named(packed, number // 4), named(usual, number - number // 4 - 1))
    mixed = jax.random.permutation(jax.random.fold_in(own, 3), amount)
    giver, receiver = mixed[0:amount // 2 * 2:2], mixed[1:amount // 2 * 2:2]
    slack = jnp.minimum(sizes[giver] - 1, most - sizes[receiver]) // 2
    slack = jnp.where((giver == order[0]) | (receiver == order[0]) | (sizes[receiver] == 0), 0, jnp.maximum(slack, 0))
    moved = jax.random.randint(jax.random.fold_in(own, 4), (amount // 2,), 0, 1 << 20) % (slack + 1)
    sizes = sizes.at[giver].add(-moved).at[receiver].add(moved)
    items = jnp.searchsorted(jnp.cumsum(sizes), jnp.arange(rows * top), side="right").astype(jnp.int32)
    table = items.reshape(top, rows).T
    table = table[jax.random.permutation(jax.random.fold_in(own, 1), rows)]
    rotation = jax.random.randint(jax.random.fold_in(own, 2), (rows, 1), 0, top)
    return jnp.take_along_axis(table, (jnp.arange(top)[None, :] + rotation) % top, axis=1)


def shares(count, total, bound, lean, full):
    portions = [(1 << 20) // math.isqrt(standing ** lean) + 1 for standing in range(1, count + 1)]
    largest = bound if full else min(bound, max(-(-total // count), total * portions[0] // sum(portions)))
    least = 1 if total - largest >= count - 1 else 0
    holding, rest = [largest] + [least] * (count - 1), total - largest - least * (count - 1)
    while rest > 0:
        candidates = [i for i in range(1, count) if holding[i] < largest] or [i for i in range(1, count) if holding[i] < bound]
        whole, budget = sum([portions[i] for i in candidates]), rest
        for i in candidates:
            more = min(bound - holding[i], max(1, budget * portions[i] // whole), rest)
            holding[i] = holding[i] + more
            rest = rest - more
    return np.array(holding)


def noise(rng, shape, scale, most, cuts=(), kind=jnp.bfloat16):
    drawn = jax.random.normal(rng, shape, jnp.float32) * scale
    if len(cuts) > 0:
        drawn = block_scale(rng, shape, cuts, -0.22, 0.18) * drawn
    return jnp.clip(drawn, min=-most, max=most).astype(kind)


def setup_inputs(seed: int = 0) -> dict:
    keys = jax.random.split(jax.random.key(seed), 5)
    embed = noise(keys[0], (ROWS, D), 1.0, 6.0, ((0, 128),))
    owner_keys = jax.random.split(jax.random.fold_in(keys[1], 1), ROWS // ROWS_DEV)
    owner_turns = jax.random.permutation(jax.random.fold_in(keys[1], 3), ROWS // ROWS_DEV)
    owner = jax.vmap(lambda own, number: shared_out(jax.random.fold_in(keys[1], 2), own, number, ROWS_DEV, N_GRP, 1, CAP, 2))(owner_keys, owner_turns).reshape((ROWS, 1))
    local_id = set_ends(ranked_ids(keys[2], (ROWS,), CL_GRP, 2), jax.random.fold_in(keys[2], 3), 0, CL_GRP - 1).astype(jnp.int32)
    rank = jax.random.permutation(keys[3], ROWS).astype(jnp.int32)
    return dict(embed=embed, owner=owner, local_id=local_id, rank=rank)


EPS = 1e-06

def reference(embed, owner, local_id, rank):
    wide = embed.astype(jnp.float32)
    unit = (wide * lax.rsqrt(lax.optimization_barrier(jnp.sum(wide * wide, 1, keepdims=True)) + EPS)).astype(jnp.bfloat16)
    target = owner[:, 0].astype(jnp.int32)
    index = jnp.arange(ROWS, dtype=jnp.int32)
    width = N_GRP * CAP
    limit = N_BLK * width

    def per_group(group):
        order_key = jnp.where(target == group, 0, ROWS).astype(jnp.int32) + index
        chosen = jnp.argsort(order_key, stable=True)[:limit].astype(jnp.int32)
        valid = target[chosen] == group
        group_unit = unit[chosen]
        group_tag = jnp.where(valid, local_id[chosen], -1).astype(jnp.int32)
        group_rank = rank[chosen].astype(jnp.int32)

        def per_block(block_no):
            start = (block_no * width).astype(jnp.int32)
            query = lax.dynamic_slice_in_dim(group_unit, start, width, 0)
            query_tag = lax.dynamic_slice_in_dim(group_tag, start, width, 0)
            query_rank = lax.dynamic_slice_in_dim(group_rank, start, width, 0)
            scores = lax.dot_general(query, group_unit, (((1,), (1,)), ((), ())), preferred_element_type=jnp.float32)
            allowed = (query_tag[:, None] == group_tag[None, :]) & (group_tag[None, :] >= 0) & (group_rank[None, :] < query_rank[:, None])
            return lax.optimization_barrier(jnp.max(jnp.where(allowed, scores, jnp.float32(-1.0)), axis=1))
        values = lax.map(per_block, jnp.arange(limit // width, dtype=jnp.int32)).reshape(limit)
        return (chosen, jnp.where(valid, values, jnp.float32(-1.0)))
    chosen, values = lax.map(per_group, jnp.arange(N_GRP, dtype=jnp.int32))
    result = jnp.full((ROWS,), -1.0, jnp.float32)
    return result.at[chosen.reshape(-1)].max(values.reshape(-1))
```

```python
import math

import jax
import jax.numpy as jnp
from jax import lax
from jax.experimental import pallas as pl
from jax.experimental.pallas import tpu as pltpu
from jax.sharding import PartitionSpec as P

EPS = 1e-06
BEYOND = 1073741824
BOTH = ("grp", "blk")
CHIPS = 64
DEVICES = 128
SLOTS = 16
EXTRA = 128
CHUNK = 128
TILE = 256
PACKED = 1536
ROOM = PACKED + CHUNK
COLS = (((1,), (1,)), ((), ()))
F32 = jnp.float32
BF16 = jnp.bfloat16
I32 = jnp.int32


def iota(shape, dim):
    return lax.broadcasted_iota(I32, shape, dim)


def hot(mask):
    return jnp.where(mask, jnp.float32(1), jnp.float32(0)).astype(BF16)


def dot(a, b, dims=(((1,), (0,)), ((), ()))):
    return lax.dot_general(a, b, dims, preferred_element_type=F32)


def thirds(x):
    high = x.astype(BF16)
    rest = x - high.astype(F32)
    middle = rest.astype(BF16)
    return high, middle, (rest - middle.astype(F32)).astype(BF16)


def send_kernel(embed, owner, local, rank, out, place, unit, extra, slot, rounds):
    rows, width = unit.shape
    step = pl.program_id(0)
    block = out.shape[0]

    @pl.when(step == 0)
    def _():
        wide = embed[...].astype(F32)
        scale = lax.rsqrt(jnp.sum(wide * wide, 1, keepdims=True) + EPS)
        unit[...] = (wide * scale).astype(BF16)
        group, number, order = owner[...], local[...], rank[...]
        chip = (number & (CHIPS - 1)) ^ (group * 4)
        own = iota((CHIPS, rows), 0) == chip
        before = hot(iota((rows, rows), 0) < iota((rows, rows), 1))
        ahead = dot(hot(own), before)
        position = jnp.sum(jnp.where(own, ahead, 0.0), 0, keepdims=True).astype(I32)
        most = jnp.max(jnp.sum(jnp.where(own, 1.0, 0.0), 1, keepdims=True), 0, keepdims=True)
        rounds[...] = jnp.broadcast_to(
            jnp.where(most > 2 * SLOTS, jnp.float32(1), jnp.float32(0)), rounds.shape
        )
        device = ((chip >> 3) << 4) + ((position & 1) << 3) + (chip & 7)
        seat = position >> 1
        slot[...] = jnp.where(seat < SLOTS, device * SLOTS + seat, -1)
        which = iota(place.shape, 0)
        place[...] = jnp.where(which == 0, device, seat)
        kind = iota(extra.shape, 0)
        fields = (number, group, order >> 8, order & 255, jnp.ones_like(order))
        table = jnp.zeros(extra.shape, I32)
        for at, field in enumerate(fields):
            table = jnp.where(kind == at, field, table)
        extra[...] = table.astype(F32).astype(BF16)

    pick = hot(iota((block, rows), 0) + step * block == slot[...])
    out[:, :width] = dot(pick, unit[...]).astype(BF16)
    lane = iota((block, EXTRA), 1)
    fields = dot(pick, extra[...], COLS)
    out[:, width:] = jnp.where(lane == 5, rounds[0:1, :], fields).astype(BF16)


def pack_kernel(taken, packed, spots, info, base):
    step = pl.program_id(0)
    width = packed.shape[1] - EXTRA

    @pl.when(step == 0)
    def _():
        base[0] = 0
        info[17] = 0
        packed[0:CHUNK, :] = jnp.zeros((CHUNK, packed.shape[1]), BF16)

    start = base[0]
    first = jnp.minimum((start >> 7) << 7, PACKED - CHUNK)
    first = pl.multiple_of(first, CHUNK)
    info[step] = first
    take = hot(iota((16, EXTRA), 0) == iota((16, EXTRA), 1))
    fields = dot(take, taken[:, width:], COLS)
    filled = fields[4:5, :]
    upto = hot(iota((CHUNK, CHUNK), 0) <= iota((CHUNK, CHUNK), 1))
    running = dot(jnp.broadcast_to(filled, (16, CHUNK)).astype(BF16), upto)[0:1, :]
    spot = jnp.where(filled > 0, running.astype(I32) + (start - 1), -1)
    spots[pl.ds(step, 1), :] = spot
    after = start + jnp.sum(filled).astype(I32)
    base[0] = after
    info[17] = jnp.maximum(info[17], jnp.max(fields[5:6, :]).astype(I32))
    pick = hot(iota((2 * CHUNK, CHUNK), 0) + first == spot)
    moved = dot(pick, taken[...])
    here = pl.ds(first, CHUNK)
    packed[here, :] = (packed[here, :].astype(F32) + moved[:CHUNK]).astype(BF16)
    packed[pl.ds(pl.multiple_of(first + CHUNK, CHUNK), CHUNK), :] = moved[CHUNK:].astype(BF16)

    @pl.when(step == pl.num_programs(0) - 1)
    def _():
        @pl.when(first + 3 * CHUNK <= ROOM)
        def _():
            tail = pl.ds(pl.multiple_of(first + 2 * CHUNK, CHUNK), CHUNK)
            packed[tail, :] = jnp.zeros((CHUNK, packed.shape[1]), BF16)

        tiles = jnp.minimum((after + TILE - 1) // TILE, PACKED // TILE)
        info[16] = tiles
        info[17] = jnp.where(after > PACKED, 1, info[17])
        mark = jnp.where(iota((16, EXTRA), 1) == 6, tiles.astype(F32), 0.0)
        corner = packed[0:16, width:].astype(F32)
        packed[0:16, width:] = (corner + mark).astype(BF16)


def score(queries, query_tiles, keys, key_tiles, best):
    width = queries.shape[1] - EXTRA
    take = hot(iota((16, EXTRA), 0) == iota((16, EXTRA), 1))

    def query_step(at, carry):
        rows = pl.ds(pl.multiple_of(at * TILE, TILE), TILE)
        fields = dot(take, queries[rows, width:], COLS).astype(I32)
        query_rank = fields[2:3, :] * 256 + fields[3:4, :]
        cluster = (fields[1:2, :] * 128 + fields[0:1, :] + fields[4:5, :]) * 65536
        query = queries[rows, :width]

        def key_step(other, found):
            span = pl.ds(pl.multiple_of(other * TILE, TILE), TILE)
            side = keys[span, width:].astype(F32).astype(I32)
            mark = (side[:, 1:2] * 128 + side[:, 0:1] + side[:, 4:5]) * 65536
            mark = mark + side[:, 2:3] * 256 + side[:, 3:4]
            scores = dot(keys[span, :width], query, COLS)
            earlier = (mark >= cluster) & (mark < cluster + query_rank)
            return jnp.maximum(
                found, jnp.max(jnp.where(earlier, scores, -1.0), 0, keepdims=True)
            )

        best[:, rows] = lax.fori_loop(0, key_tiles, key_step, best[:, rows])
        return carry

    lax.fori_loop(0, query_tiles, query_step, 0)


def own_kernel(info, packed, best):
    best[...] = jnp.full(best.shape, -1.0, F32)
    score(packed, info[16], packed, info[16], best)


def other_kernel(info, packed, other, best_in, spots, back, best):
    best[...] = best_in[...]
    width = packed.shape[1] - EXTRA
    corner = other[0:16, width:].astype(F32)
    tiles = jnp.max(jnp.where(iota((16, EXTRA), 1) == 6, corner, 0.0)).astype(I32)
    score(packed, info[16], other, tiles, best)
    flag = info[17].astype(F32)
    row = iota((16, TILE), 0)
    sub, lane = iota((8, CHUNK), 0), iota((8, CHUNK), 1) // SLOTS
    for step in range(DEVICES * SLOTS // CHUNK):
        first = pl.multiple_of(info[step], CHUNK)
        parts = thirds(best[:, pl.ds(first, TILE)])
        stack = jnp.zeros((16, TILE), F32)
        for at, part in enumerate(parts):
            stack = jnp.where(row == at, part.astype(F32), stack)
        pick = hot(iota((TILE, CHUNK), 0) + first == spots[step : step + 1, :])
        value = jnp.sum(dot(stack.astype(BF16), pick), 0, keepdims=True)
        line = jnp.where(lane == sub, value, jnp.where(lane == ((sub + 1) & 7), flag, 0.0))
        back[8 * step : 8 * step + 8, :] = line


def home_kernel(blk, back, place, highest, flag):
    rows = place.shape[1]
    device, seat = place[0:1, :], place[1:2, :]
    pick = hot(iota((DEVICES, rows), 0) == device)
    lines = back[...]
    total = jnp.zeros((CHUNK, rows), F32)
    for part in thirds(lines):
        total = total + dot(part, pick, (((0,), (0,)), ((), ())))
    mine = iota((CHUNK, rows), 0) == seat + blk[0] * SLOTS
    highest[...] = jnp.sum(jnp.where(mine, total, 0.0), 0, keepdims=True)
    marks = iota(lines.shape, 1) // SLOTS == ((blk[0] + 1) & 7)
    flag[0] = jnp.max(jnp.where(marks, lines, 0.0)).astype(I32)


def whole(shape):
    return pl.BlockSpec(shape, lambda *_: (0,) * len(shape))


SCALARS = pl.BlockSpec(memory_space=pltpu.SMEM)
PARAMS = pltpu.CompilerParams(vmem_limit_bytes=48 * 1024 * 1024)


def direct(embed, owner, local_id, rank):
    rows, width = embed.shape
    full = width + EXTRA
    slots = DEVICES * SLOTS
    block = 256
    sent, place = pl.pallas_call(
        send_kernel,
        grid=(slots // block,),
        in_specs=[whole((rows, width))] + [whole((1, rows))] * 3,
        out_specs=[pl.BlockSpec((block, full), lambda i: (i, 0)), whole((8, rows))],
        out_shape=[
            jax.ShapeDtypeStruct((slots, full), BF16),
            jax.ShapeDtypeStruct((8, rows), I32),
        ],
        scratch_shapes=[
            pltpu.VMEM((rows, width), BF16),
            pltpu.VMEM((EXTRA, rows), BF16),
            pltpu.VMEM((1, rows), I32),
            pltpu.VMEM((8, EXTRA), F32),
        ],
        compiler_params=PARAMS,
        name="send",
    )(embed, owner.reshape(1, rows), local_id.reshape(1, rows), rank.reshape(1, rows))
    taken = lax.all_to_all(
        sent.reshape(DEVICES, SLOTS, full), BOTH, split_axis=0, concat_axis=0, tiled=True
    ).reshape(slots, full)
    packed, spots, info = pl.pallas_call(
        pack_kernel,
        grid=(slots // CHUNK,),
        in_specs=[pl.BlockSpec((CHUNK, full), lambda i: (i, 0))],
        out_specs=[whole((ROOM, full)), whole((slots // CHUNK, CHUNK)), SCALARS],
        out_shape=[
            jax.ShapeDtypeStruct((ROOM, full), BF16),
            jax.ShapeDtypeStruct((slots // CHUNK, CHUNK), I32),
            jax.ShapeDtypeStruct((32,), I32),
        ],
        scratch_shapes=[pltpu.SMEM((1,), I32)],
        compiler_params=PARAMS,
        name="pack",
    )(taken)
    other = lax.ppermute(packed, "grp", [(i, i ^ 1) for i in range(16)])
    best = pl.pallas_call(
        own_kernel,
        in_specs=[SCALARS, whole((ROOM, full))],
        out_specs=whole((1, ROOM)),
        out_shape=jax.ShapeDtypeStruct((1, ROOM), F32),
        compiler_params=PARAMS,
        cost_estimate=pl.CostEstimate(
            flops=2 * 1024 * 1024 * width, bytes_accessed=2 * ROOM * full, transcendentals=0
        ),
        name="own",
    )(info, packed)
    back = pl.pallas_call(
        other_kernel,
        in_specs=[
            SCALARS,
            whole((ROOM, full)),
            whole((ROOM, full)),
            whole((1, ROOM)),
            whole((slots // CHUNK, CHUNK)),
        ],
        out_specs=whole((DEVICES, CHUNK)),
        out_shape=jax.ShapeDtypeStruct((DEVICES, CHUNK), F32),
        scratch_shapes=[pltpu.VMEM((1, ROOM), F32)],
        compiler_params=PARAMS,
        name="other",
    )(info, packed, other, best, spots)
    home = lax.all_to_all(back, BOTH, split_axis=0, concat_axis=0, tiled=True)
    highest, flag = pl.pallas_call(
        home_kernel,
        in_specs=[SCALARS, whole((DEVICES, CHUNK)), whole((8, rows))],
        out_specs=[whole((1, rows)), SCALARS],
        out_shape=[
            jax.ShapeDtypeStruct((1, rows), F32),
            jax.ShapeDtypeStruct((1,), I32),
        ],
        compiler_params=PARAMS,
        name="home",
    )(lax.axis_index("blk").astype(I32).reshape(1), home, place)
    return highest.reshape(rows), flag[0]


def pair_scores(query, query_tag, query_rank, keys, key_tag, key_rank):
    scores = lax.dot_general(
        query, keys, (((1,), (1,)), ((), ())), preferred_element_type=jnp.float32
    )
    same = (
        (query_tag[:, None] == key_tag[None, :])
        & (key_tag[None, :] >= 0)
        & (query_tag[:, None] >= 0)
    )
    row_side = jnp.where(
        same & (key_rank[None, :] < query_rank[:, None]), scores, jnp.float32(-1.0)
    )
    column_side = jnp.where(
        same & (query_rank[:, None] < key_rank[None, :]), scores, jnp.float32(-1.0)
    )
    return (jnp.max(row_side, axis=1), jnp.max(column_side, axis=0))


def tile_split(rows, tags, ranks, tile):
    count = rows.shape[0] // tile
    sort_key = jnp.where(tags >= 0, tags, BEYOND).reshape(count, tile)
    return (
        rows.reshape(count, tile, -1),
        tags.reshape(count, tile),
        ranks.reshape(count, tile),
        jnp.min(sort_key, 1),
        jnp.max(sort_key, 1),
    )


def tiled_scores(query, query_tag, query_rank, keys, key_tag, key_rank):
    tile = math.gcd(query.shape[0], 256)
    query_tiles = tile_split(query, query_tag, query_rank, tile)
    key_tiles = tile_split(keys, key_tag, key_rank, tile)
    empty = jnp.full((tile,), -1.0, jnp.float32)

    def outer(column_carry, query_block):
        q_rows, q_tag, q_rank, q_low, q_high = query_block

        def inner(row_carry, key_block):
            k_rows, k_tag, k_rank, k_low, k_high = key_block
            meet = (q_low <= k_high) & (k_low <= q_high) & (q_low < BEYOND) & (k_low < BEYOND)
            row_best, column_best = lax.cond(
                meet,
                lambda: pair_scores(q_rows, q_tag, q_rank, k_rows, k_tag, k_rank),
                lambda: (empty, empty),
            )
            return (jnp.maximum(row_carry, row_best), column_best)

        row_best, columns = lax.scan(inner, empty, key_tiles)
        return (jnp.maximum(column_carry, columns), row_best)

    start_columns = jnp.full((keys.shape[0] // tile, tile), -1.0, jnp.float32)
    columns, rows = lax.scan(outer, start_columns, query_tiles)
    return (rows.reshape(-1), columns.reshape(-1))


def by_group(embed, owner, local_id, rank):
    n_group = lax.axis_size("grp")
    row_count = embed.shape[0]
    capacity = row_count // 8
    width = n_group * capacity
    wide = embed.astype(jnp.float32)
    unit = (wide * lax.rsqrt(jnp.sum(wide * wide, 1, keepdims=True) + EPS)).astype(jnp.bfloat16)
    target = owner[:, 0]
    onehot = (target[:, None] == jnp.arange(n_group, dtype=jnp.int32)[None, :]).astype(jnp.int32)
    position = jnp.sum((jnp.cumsum(onehot, 0) - 1) * onehot, 1)
    slot_index = target * capacity + position
    send_unit = jnp.zeros((width, unit.shape[1]), jnp.bfloat16).at[slot_index].set(unit)
    send_tag = jnp.full((width,), -1, jnp.int32).at[slot_index].set(local_id)
    send_rank = jnp.zeros((width,), jnp.int32).at[slot_index].set(rank)
    routed, routed_tag, routed_rank = (
        lax.all_to_all(
            send_unit.reshape(n_group, capacity, -1), "grp", split_axis=0, concat_axis=0, tiled=True
        ),
        lax.all_to_all(
            send_tag.reshape(n_group, capacity), "grp", split_axis=0, concat_axis=0, tiled=True
        ),
        lax.all_to_all(
            send_rank.reshape(n_group, capacity), "grp", split_axis=0, concat_axis=0, tiled=True
        ),
    )
    routed_tag = routed_tag.reshape(width)
    ordering = jnp.argsort(jnp.where(routed_tag >= 0, routed_tag, BEYOND), stable=True)
    query = routed.reshape(width, -1)[ordering]
    query_tag = routed_tag[ordering]
    query_rank = routed_rank.reshape(width)[ordering]
    start_best = jnp.full((width,), -1.0, jnp.float32)
    keys = lax.all_gather(query, "blk", axis=0, tiled=True)
    key_tag = lax.all_gather(query_tag, "blk", axis=0, tiled=True)
    key_rank = lax.all_gather(query_rank, "blk", axis=0, tiled=True)
    row_best, unused = tiled_scores(query, query_tag, query_rank, keys, key_tag, key_rank)
    highest = jnp.maximum(start_best, row_best)
    in_slots = jnp.zeros((width,), jnp.float32).at[ordering].set(highest)
    home = lax.all_to_all(
        in_slots.reshape(n_group, capacity), "grp", split_axis=0, concat_axis=0, tiled=True
    )
    return home.reshape(width)[slot_index]


def per_device(embed, owner, local_id, rank):
    highest, flag = direct(embed, owner, local_id, rank)
    return lax.cond(
        flag > 0, lambda: by_group(embed, owner, local_id, rank), lambda: highest
    )


def solution(mesh):
    in_specs = (
        P(("grp", "blk"), None),
        P(("grp", "blk"), None),
        P(("grp", "blk")),
        P(("grp", "blk")),
    )
    out_specs = P(("grp", "blk"))
    return jax.shard_map(
        per_device, mesh=mesh, in_specs=in_specs, out_specs=out_specs, check_vma=False
    )
```

```python
import functools

import jax
import jax.numpy as jnp
from jax import lax
from jax.experimental import pallas as pl
from jax.experimental.pallas import tpu as pltpu
from jax.sharding import PartitionSpec as P

EPS = 1e-06
BOTH = ("grp", "blk")
CHIPS = 64
BLOCK = 24
SEATS = 23
EXTRA = 128
CHUNK = 8 * BLOCK
WINDOW = CHUNK + 16
TILE = 256
TILES = 6
PACKED = TILE * TILES
ROOM = PACKED
SPILL = 128
GROUPS = [[g * 8 + b for g in range(core, 16, 2) for b in range(8)] for core in range(2)]
COLS = (((1,), (1,)), ((), ()))
F32 = jnp.float32
BF16 = jnp.bfloat16
I32 = jnp.int32


def iota(shape, dim):
    return lax.broadcasted_iota(I32, shape, dim)


def hot(mask):
    return jnp.where(mask, jnp.float32(1), jnp.float32(0)).astype(BF16)


def dot(a, b, dims=(((1,), (0,)), ((), ()))):
    return lax.dot_general(a, b, dims, preferred_element_type=F32)


def thirds(x):
    high = x.astype(BF16)
    rest = x - high.astype(F32)
    middle = rest.astype(BF16)
    return high, middle, (rest - middle.astype(F32)).astype(BF16)


def fields_of(extra):
    return dot(hot(iota((16, EXTRA), 0) == iota((16, EXTRA), 1)), extra, COLS)


def send_kernel(me, embed, owner, local, rank, out, place, unit, slot, ends):
    rows, width = embed.shape
    step = pl.program_id(0)
    block = out.shape[0]

    @pl.when(step == 0)
    def _():
        wide = embed[...].astype(F32)
        scale = lax.rsqrt(jnp.sum(wide * wide, 1, keepdims=True) + EPS)
        unit[...] = (wide * scale).astype(BF16)
        group, number, order = owner[...], local[...], rank[...]
        chip = (number & (CHIPS - 1)) ^ (group * 4)
        own = iota((CHIPS, rows), 0) == chip
        near = iota((CHIPS, rows), 0) == (chip ^ 1)
        before = hot(iota((rows, rows), 0) < iota((rows, rows), 1))
        ahead = dot(hot(own), before)
        count = jnp.sum(jnp.where(own, 1.0, 0.0), 1, keepdims=True)
        position = jnp.sum(jnp.where(own, ahead, 0.0), 0, keepdims=True).astype(I32)
        beside = jnp.sum(jnp.where(near, count, 0.0), 0, keepdims=True).astype(I32)
        spilled = position >= SEATS
        seat = jnp.where(spilled, beside + position - SEATS, position)
        late = jnp.max(jnp.where(seat >= SEATS, 1.0, 0.0), 1, keepdims=True)
        goes = jnp.where(seat < SEATS, jnp.where(spilled, chip ^ 1, chip), -1)
        line = seat + jnp.where(spilled, 32, 0)
        slot[...] = jnp.where(goes >= 0, goes * BLOCK + seat, -1)
        place[...] = jnp.where(iota(place.shape, 0) == 0, chip, line)
        entries = (
            number,
            group,
            order >> 8,
            order & 255,
            jnp.ones_like(order),
            jnp.where(spilled, 1, 0),
            (line + (me[0] & 7) * BLOCK) & (EXTRA - 1),
            jnp.broadcast_to(me[0], order.shape),
        )
        there = iota((CHIPS, rows), 0) == goes
        tables = [jnp.where(there, entry.astype(F32), 0.0).astype(BF16) for entry in entries]
        seats = hot(iota((EXTRA, rows), 0) == seat)
        fields = dot(jnp.concatenate(tables, 0), seats, COLS)
        lane = iota((CHIPS, EXTRA), 1)
        for at in range(len(entries)):
            field = fields[CHIPS * at : CHIPS * (at + 1), :]
            if at == 0:
                field = jnp.where(lane == EXTRA - 1, late, field)
            ends[:, EXTRA * at : EXTRA * (at + 1)] = field

    pick = hot(iota((block, rows), 0) == slot[...] - step * block)
    moved = dot(pick, unit[...])
    end = ends[pl.ds(pl.multiple_of(step * 8, 8), 8), :]
    last = iota((8, width), 0) == 7
    pieces = []
    for at in range(block // BLOCK):
        top = at * BLOCK
        pieces.append(moved[top : top + 16, :])
        pieces.append(jnp.where(last, end[at : at + 1, :], moved[top + 16 : top + 24, :]))
    out[...] = jnp.concatenate(pieces, 0).astype(BF16)


def gather(spot, count, taken, rows, fields):
    pick = hot(iota((count, CHUNK), 0) == spot)
    return dot(pick, taken[rows, :]), dot(pick, fields, COLS)


def load_chunks(source, taken, copied):
    copies = []
    for at in range(taken.shape[0] // CHUNK):
        rows = pl.ds(at * CHUNK, CHUNK)
        copies.append(pltpu.make_async_copy(source.at[rows, :], taken.at[rows, :], copied.at[at]))
        copies[-1].start()
    return copies


def read_kernel(source, spill, spots, fields, info, taken, pile, strange, copied):
    chunks = taken.shape[0] // CHUNK
    width = taken.shape[1]
    copies = load_chunks(source, taken, copied)
    upto = hot(iota((CHUNK, CHUNK), 0) <= iota((CHUNK, CHUNK), 1))
    ends = hot(iota((16, CHUNK), 1) == iota((16, CHUNK), 0) * BLOCK + SEATS)
    place = iota((EXTRA, CHUNK), 1)
    sender = jnp.zeros(place.shape, I32)
    for at in range(1, 8):
        sender = sender + jnp.where(place >= at * BLOCK, 1, 0)
    spread = hot(place - sender * BLOCK == iota((EXTRA, CHUNK), 0))
    mine = (iota((64, CHUNK), 0) & 7) == sender[:64, :]
    spots[...] = jnp.full(spots.shape, -1, I32)
    start, start_strange = jnp.int32(0), jnp.int32(0)
    late = jnp.zeros((8, 1), F32)
    for at in range(chunks):
        copies[at].wait()
        rows = pl.ds(at * CHUNK, CHUNK)
        lines = dot(ends, taken[rows, :])[:8, :]
        late = jnp.maximum(late, lines[:, EXTRA - 1 : EXTRA])
        stack = [lines[:, EXTRA * f : EXTRA * (f + 1)] for f in range(8)]
        wide = dot(jnp.concatenate(stack, 0).astype(BF16), spread)
        wide = jnp.where(mine, wide, 0.0)
        found = [jnp.sum(wide[8 * f : 8 * f + 8, :], 0, keepdims=True) for f in range(8)]
        table = jnp.concatenate(found + [jnp.zeros((EXTRA - 8, CHUNK), F32)], 0)
        fields[at] = table.astype(BF16)
        foreign = found[5]
        native = found[4] - foreign
        both = jnp.where(iota((16, CHUNK), 0) == 0, native, foreign)
        running = dot(both.astype(BF16), upto).astype(I32)
        spots[at : at + 1, 0:CHUNK] = jnp.where(native > 0, running[0:1, :] + (start - 1), -1)
        strange[at : at + 1, :] = jnp.where(
            foreign > 0, running[1:2, :] + (start_strange - 1), -1
        )
        info[at] = (start >> 4) << 4
        start = start + jnp.sum(native).astype(I32)
        start_strange = start_strange + jnp.sum(foreign).astype(I32)
    full = (start > PACKED) | (start_strange > SPILL) | (jnp.max(late) > 0)
    info[16] = jnp.minimum((start + TILE - 1) // TILE, TILES)
    info[17] = jnp.where(full, 1, 0)
    pile[...] = jnp.zeros(pile.shape, F32)

    @pl.when(start_strange > 0)
    def _():
        def step(at, carry):
            rows = pl.ds(pl.multiple_of(at * CHUNK, CHUNK), CHUNK)
            rows_in, side = gather(strange[pl.ds(at, 1), :], SPILL, taken, rows, fields[at])
            pile[:, :width] += rows_in
            pile[:, width:] += side
            return carry

        lax.fori_loop(0, chunks, step, 0)

    spill[...] = pile[...].astype(BF16)


def pack_kernel(info, source, spots, fields, packed, taken, room, copied, placed):
    chunks = taken.shape[0] // CHUNK
    width = taken.shape[1]
    copies = load_chunks(source, taken, copied)
    tiles = info[16]
    room[0:16, :] = jnp.zeros((16, room.shape[1]), BF16)
    first = jnp.int32(0)
    for at in range(chunks):
        first = pl.multiple_of(jnp.minimum(info[at], ROOM - WINDOW), 16)
        spot = spots[at : at + 1, 0:CHUNK] - first
        copies[at].wait()
        rows_in, side = gather(spot, WINDOW, taken, pl.ds(at * CHUNK, CHUNK), fields[at])
        here = pl.ds(first, 16)
        after = pl.ds(pl.multiple_of(first + 16, 16), WINDOW - 16)
        for span, value in ((pl.ds(0, width), rows_in), (pl.ds(width, EXTRA), side)):
            room[here, span] = (room[here, span].astype(F32) + value[:16]).astype(BF16)
            room[after, span] = value[16:].astype(BF16)

    def clear(at, carry):
        room[pl.ds(pl.multiple_of(at * 16, 16), 16), :] = jnp.zeros((16, room.shape[1]), BF16)
        return carry

    lax.fori_loop((first + WINDOW) // 16, tiles * (TILE // 16), clear, 0)
    for wait in (False, True):
        for at in range(TILES):
            rows = pl.ds(at * TILE, TILE)
            copy = pltpu.make_async_copy(room.at[rows, :], packed.at[rows, :], placed.at[at])
            pl.when(at < tiles)(copy.wait if wait else copy.start)


def score(queries, low, high, keys, key_tiles, best, marks):
    width = queries.shape[1] - EXTRA

    def mark_step(at, carry):
        span = pl.ds(pl.multiple_of(at * TILE, TILE), TILE)
        side = keys[span, width:].astype(F32).astype(I32)
        mark = (side[:, 1:2] * 128 + side[:, 0:1] + side[:, 4:5]) * 65536
        mark = mark + side[:, 2:3] * 256 + side[:, 3:4]
        marks[span, :] = jnp.broadcast_to(mark, (TILE, TILE))
        return carry

    lax.fori_loop(0, key_tiles, mark_step, 0)

    def against(size):
        def query_step(at, carry):
            rows = pl.ds(pl.multiple_of(at * TILE, TILE), TILE)
            fields = fields_of(queries[rows, width:]).astype(I32)
            cluster = (fields[1:2, :] * 128 + fields[0:1, :] + fields[4:5, :]) * 65536
            upper = cluster + fields[2:3, :] * 256 + fields[3:4, :]
            mark = marks[:size, :]
            scores = dot(keys[:size, :width], queries[rows, :width], COLS)
            earlier = (mark >= cluster) & (mark < upper)
            found = jnp.max(jnp.where(earlier, scores, -1.0), 0, keepdims=True)
            best[:, rows] = jnp.maximum(best[:, rows], found)
            return carry

        lax.fori_loop(low, high, query_step, 0)

    if isinstance(key_tiles, int):
        against(key_tiles * TILE)
        return
    for tiles in range(1, keys.shape[0] // TILE + 1):
        pl.when(key_tiles == tiles)(functools.partial(against, tiles * TILE))


def fetch(source, target, tiles, sems):
    for at in range(TILES):
        rows = pl.ds(at * TILE, TILE)
        copy = pltpu.make_async_copy(source.at[rows, :], target.at[rows, :], sems.at[at])
        pl.when(at < tiles)(copy.start)


def fetched(source, target, tiles, sems):
    for at in range(TILES):
        rows = pl.ds(at * TILE, TILE)
        copy = pltpu.make_async_copy(source.at[rows, :], target.at[rows, :], sems.at[at])
        pl.when(at < tiles)(copy.wait)


def own_kernel(info, packed, best, mine, marks, sems):
    fetch(packed, mine, info[16], sems)
    best[...] = jnp.full(best.shape, -1.0, F32)
    fetched(packed, mine, info[16], sems)
    score(mine, 0, info[16], mine, info[16], best, marks)


def other_kernel(
    info, other_info, packed, other, near, cross, best_in, spots, back,
    mine, theirs, best, marks, sems, other_sems,
):
    tiles, other_tiles = info[16], other_info[16]
    width = mine.shape[1] - EXTRA
    fetch(packed, mine, tiles, sems)
    fetch(other, theirs, other_tiles, other_sems)
    best[:, :PACKED] = best_in[...]
    best[:, PACKED:] = jnp.full((1, best.shape[1] - PACKED), -1.0, F32)
    spilled = jnp.max(near[:, width:].astype(F32)[:, 4:5]) + jnp.max(
        cross[:, width:].astype(F32)[:, 4:5]
    )
    more = jnp.where(spilled > 0, 1, 0).astype(I32)
    fetched(packed, mine, tiles, sems)
    fetched(other, theirs, other_tiles, other_sems)
    extra_at = pl.multiple_of(tiles * TILE, TILE)
    extra_rows = pl.ds(extra_at, SPILL)

    @pl.when(more > 0)
    def _():
        mine[extra_rows, :] = near[...]
        rest = pl.ds(pl.multiple_of(extra_at + SPILL, SPILL), TILE - SPILL)
        mine[rest, :] = jnp.zeros((TILE - SPILL, mine.shape[1]), BF16)
        at = pl.multiple_of(other_tiles * TILE, TILE)
        theirs[pl.ds(at, SPILL), :] = near[...]
        theirs[pl.ds(pl.multiple_of(at + SPILL, SPILL), SPILL), :] = cross[...]
        best[:, pl.ds(extra_at, TILE)] = jnp.full((1, TILE), -1.0, F32)
        score(mine, tiles, tiles + 1, mine, tiles, best, marks)

    score(mine, 0, tiles + more, theirs, other_tiles + more, best, marks)
    flag = jnp.maximum(info[17], other_info[17]).astype(F32)
    reach = 384
    row = iota((16, reach), 0)
    sub, lane = iota((8, EXTRA), 0), iota((8, EXTRA), 1)
    lower = (lane >= sub * BLOCK) & (lane < sub * BLOCK + BLOCK)
    upper = (lane + EXTRA >= sub * BLOCK) & (lane + EXTRA < sub * BLOCK + BLOCK)
    empty = jnp.where(((lane - sub * BLOCK) & (EXTRA - 1)) >= 64, flag, 0.0)
    for step in range(CHIPS // 8):
        first = pl.multiple_of((info[step] >> 7) << 7, 128)
        parts = thirds(best[:, pl.ds(first, reach)])
        stack = jnp.zeros((16, reach), F32)
        for at, part in enumerate(parts):
            stack = jnp.where(row == at, part.astype(F32), stack)
        pick = hot(iota((reach, 2 * EXTRA), 0) + first == spots[step : step + 1, :])
        value = jnp.sum(dot(stack.astype(BF16), pick), 0, keepdims=True)
        line = jnp.where(upper, value[:, EXTRA:], jnp.where(lower, value[:, :EXTRA], empty))
        back[8 * step : 8 * step + 8, :] = line

    @pl.when(more > 0)
    def _():
        fields = fields_of(near[:, width:]).astype(I32)
        filled = fields[4:5, :] > 0
        source = iota((CHIPS, SPILL), 0) == fields[7:8, :]
        line = hot(iota((EXTRA, SPILL), 0) == fields[6:7, :])
        total = back[...]
        for part in thirds(best[:, extra_rows]):
            held = jnp.where(source & filled, part.astype(F32), 0.0).astype(BF16)
            total = total + dot(held, line, COLS)
        back[...] = total


def home_kernel(me, back, place, highest, flag):
    rows = place.shape[1]
    base = (me[0] & 7) * BLOCK
    pick = hot(iota((CHIPS, rows), 0) == place[0:1, :])
    lines = back[...]
    total = jnp.zeros((EXTRA, rows), F32)
    for part in thirds(lines):
        total = total + dot(part, pick, (((0,), (0,)), ((), ())))
    mine = iota((EXTRA, rows), 0) == ((place[1:2, :] + base) & (EXTRA - 1))
    highest[...] = jnp.sum(jnp.where(mine, total, 0.0), 0, keepdims=True)
    marks = ((iota(lines.shape, 1) - base) & (EXTRA - 1)) >= 64
    flag[0] = jnp.max(jnp.where(marks, lines, 0.0)).astype(I32)


def whole(shape):
    return pl.BlockSpec(shape, lambda *_: (0,) * len(shape))


SCALARS = pl.BlockSpec(memory_space=pltpu.SMEM)
PLACED = pl.BlockSpec(memory_space=pl.ANY)
PARAMS = pltpu.CompilerParams(vmem_limit_bytes=56 * 1024 * 1024)


def array(shape, dtype):
    return jax.ShapeDtypeStruct(shape, dtype)


def exchange(x):
    return lax.all_to_all(
        x, BOTH, split_axis=0, concat_axis=0, tiled=True, axis_index_groups=GROUPS
    )


def direct(embed, owner, local_id, rank):
    rows, width = embed.shape
    full = width + EXTRA
    lines = CHIPS * BLOCK
    chunks = lines // CHUNK
    me = ((lax.axis_index("grp") >> 1) * 8 + lax.axis_index("blk")).astype(I32).reshape(1)
    sent, place = pl.pallas_call(
        send_kernel,
        grid=(chunks,),
        in_specs=[SCALARS, whole((rows, width))] + [whole((1, rows))] * 3,
        out_specs=[pl.BlockSpec((CHUNK, width), lambda i: (i, 0)), whole((8, rows))],
        out_shape=[array((lines, width), BF16), array((8, rows), I32)],
        scratch_shapes=[
            pltpu.VMEM((rows, width), BF16),
            pltpu.VMEM((1, rows), I32),
            pltpu.VMEM((CHIPS, width), F32),
        ],
        compiler_params=PARAMS,
        name="send",
    )(me, embed, owner.reshape(1, rows), local_id.reshape(1, rows), rank.reshape(1, rows))
    taken = exchange(sent.reshape(CHIPS, BLOCK, width)).reshape(lines, width)
    spill, spots, fields, info = pl.pallas_call(
        read_kernel,
        in_specs=[PLACED],
        out_specs=[
            whole((SPILL, full)),
            whole((chunks, 2 * EXTRA)),
            whole((chunks, EXTRA, CHUNK)),
            SCALARS,
        ],
        out_shape=[
            array((SPILL, full), BF16),
            array((chunks, 2 * EXTRA), I32),
            array((chunks, EXTRA, CHUNK), BF16),
            array((32,), I32),
        ],
        scratch_shapes=[
            pltpu.VMEM((lines, width), BF16),
            pltpu.VMEM((SPILL, full), F32),
            pltpu.VMEM((chunks, CHUNK), I32),
            pltpu.SemaphoreType.DMA((chunks,)),
        ],
        compiler_params=PARAMS,
        name="read",
    )(taken)
    near = lax.ppermute(spill, BOTH, [(i, i ^ 1) for i in range(2 * CHIPS)])
    packed = pl.pallas_call(
        pack_kernel,
        in_specs=[SCALARS, PLACED, whole((chunks, 2 * EXTRA)), whole((chunks, EXTRA, CHUNK))],
        out_specs=PLACED,
        out_shape=array((PACKED, full), BF16),
        scratch_shapes=[
            pltpu.VMEM((lines, width), BF16),
            pltpu.VMEM((ROOM, full), BF16),
            pltpu.SemaphoreType.DMA((chunks,)),
            pltpu.SemaphoreType.DMA((TILES,)),
        ],
        compiler_params=PARAMS,
        cost_estimate=pl.CostEstimate(
            flops=2 * lines * WINDOW * full, bytes_accessed=4 * lines * full, transcendentals=0
        ),
        name="pack",
    )(info, taken, spots, fields)
    swap = [(i, i ^ 1) for i in range(16)]
    other_info = lax.ppermute(info, "grp", swap)
    other = lax.ppermute(packed, "grp", swap)
    cross = lax.ppermute(near, "grp", swap)
    best = pl.pallas_call(
        own_kernel,
        in_specs=[SCALARS, PLACED],
        out_specs=whole((1, PACKED)),
        out_shape=array((1, PACKED), F32),
        scratch_shapes=[
            pltpu.VMEM((PACKED, full), BF16),
            pltpu.VMEM((PACKED, TILE), I32),
            pltpu.SemaphoreType.DMA((TILES,)),
        ],
        compiler_params=PARAMS,
        cost_estimate=pl.CostEstimate(
            flops=2 * 1024 * 1024 * width, bytes_accessed=2 * PACKED * full, transcendentals=0
        ),
        name="own",
    )(info, packed)
    back = pl.pallas_call(
        other_kernel,
        in_specs=[SCALARS, SCALARS, PLACED, PLACED]
        + [whole((SPILL, full))] * 2
        + [whole((1, PACKED)), whole((chunks, 2 * EXTRA))],
        out_specs=whole((CHIPS, EXTRA)),
        out_shape=array((CHIPS, EXTRA), F32),
        scratch_shapes=[
            pltpu.VMEM((PACKED + TILE, full), BF16),
            pltpu.VMEM((PACKED + TILE, full), BF16),
            pltpu.VMEM((1, PACKED + 2 * TILE), F32),
            pltpu.VMEM((PACKED + TILE, TILE), I32),
            pltpu.SemaphoreType.DMA((TILES,)),
            pltpu.SemaphoreType.DMA((TILES,)),
        ],
        compiler_params=PARAMS,
        name="other",
    )(info, other_info, packed, other, near, cross, best, spots)
    home = exchange(back)
    highest, flag = pl.pallas_call(
        home_kernel,
        in_specs=[SCALARS, whole((CHIPS, EXTRA)), whole((8, rows))],
        out_specs=[whole((1, rows)), SCALARS],
        out_shape=[array((1, rows), F32), array((1,), I32)],
        compiler_params=PARAMS,
        name="home",
    )(me, home, place)
    return highest.reshape(rows), flag[0]


def group_kernel(queries, keys, best_in, best, marks):
    best[...] = best_in[...]
    tiles = keys.shape[0] // TILE
    score(queries, 0, tiles, keys, tiles, best, marks)


def by_group(embed, owner, local_id, rank):
    n_group, n_block = lax.axis_size("grp"), lax.axis_size("blk")
    row_count, columns = embed.shape
    capacity = row_count // 8
    width = n_group * capacity
    full = columns + EXTRA
    wide = embed.astype(F32)
    unit = (wide * lax.rsqrt(jnp.sum(wide * wide, 1, keepdims=True) + EPS)).astype(BF16)
    target = owner[:, 0]
    onehot = (target[:, None] == jnp.arange(n_group, dtype=I32)[None, :]).astype(I32)
    position = jnp.sum((jnp.cumsum(onehot, 0) - 1) * onehot, 1)
    slot_index = target * capacity + position
    fields = jnp.stack([local_id, target, rank >> 8, rank & 255, jnp.ones_like(rank)], 1)
    fields = jnp.pad(fields, ((0, 0), (0, EXTRA - 5))).astype(BF16)
    sent = jnp.zeros((width, full), BF16).at[slot_index].set(jnp.concatenate([unit, fields], 1))
    routed = lax.all_to_all(
        sent.reshape(n_group, capacity, full), "grp", split_axis=0, concat_axis=0, tiled=True
    ).reshape(width, full)
    best = jnp.full((1, width), -1.0, F32)
    for by in range(n_block):
        turn = [(i, (i + by) % n_block) for i in range(n_block)]
        best = pl.pallas_call(
            group_kernel,
            in_specs=[whole((width, full))] * 2 + [whole((1, width))],
            out_specs=whole((1, width)),
            out_shape=array((1, width), F32),
            scratch_shapes=[pltpu.VMEM((width, TILE), I32)],
            compiler_params=PARAMS,
            name="group",
        )(routed, lax.ppermute(routed, "blk", turn) if by else routed, best)
    home = lax.all_to_all(
        best.reshape(n_group, capacity), "grp", split_axis=0, concat_axis=0, tiled=True
    )
    return home.reshape(width)[slot_index]


def per_device(embed, owner, local_id, rank):
    highest, flag = direct(embed, owner, local_id, rank)
    return lax.cond(
        flag > 0, lambda: by_group(embed, owner, local_id, rank), lambda: highest
    )


def solution(mesh):
    in_specs = (
        P(("grp", "blk"), None),
        P(("grp", "blk"), None),
        P(("grp", "blk")),
        P(("grp", "blk")),
    )
    out_specs = P(("grp", "blk"))
    return jax.shard_map(
        per_device, mesh=mesh, in_specs=in_specs, out_specs=out_specs, check_vma=False
    )
```

```python
import functools

import jax
import jax.numpy as jnp
from jax import lax
from jax.experimental import pallas as pl
from jax.experimental.pallas import tpu as pltpu
from jax.sharding import PartitionSpec as P

EPS = 1e-06
BOTH = ("grp", "blk")
CHIPS = 64
BLOCK = 24
SEATS = 23
EXTRA = 128
CHUNK = 8 * BLOCK
WINDOW = CHUNK + 16
TILE = 256
TILES = 6
PACKED = TILE * TILES
ROOM = PACKED
SPILL = 128
GROUPS = [[g * 8 + b for g in range(core, 16, 2) for b in range(8)] for core in range(2)]
COLS = (((1,), (1,)), ((), ()))
F32 = jnp.float32
BF16 = jnp.bfloat16
I32 = jnp.int32


def iota(shape, dim):
    return lax.broadcasted_iota(I32, shape, dim)


def hot(mask):
    return jnp.where(mask, jnp.float32(1), jnp.float32(0)).astype(BF16)


def dot(a, b, dims=(((1,), (0,)), ((), ()))):
    return lax.dot_general(a, b, dims, preferred_element_type=F32)


def thirds(x):
    high = x.astype(BF16)
    rest = x - high.astype(F32)
    middle = rest.astype(BF16)
    return high, middle, (rest - middle.astype(F32)).astype(BF16)


def fields_of(extra):
    return dot(hot(iota((16, EXTRA), 0) == iota((16, EXTRA), 1)), extra, COLS)


def send_kernel(me, embed, owner, local, rank, out, place, unit, slot, ends):
    rows, width = embed.shape
    step = pl.program_id(0)
    block = out.shape[0]

    @pl.when(step == 0)
    def _():
        wide = embed[...].astype(F32)
        scale = lax.rsqrt(jnp.sum(wide * wide, 1, keepdims=True) + EPS)
        unit[...] = (wide * scale).astype(BF16)
        group, number, order = owner[...], local[...], rank[...]
        chip = (number & (CHIPS - 1)) ^ (group * 4)
        own = iota((CHIPS, rows), 0) == chip
        near = iota((CHIPS, rows), 0) == (chip ^ 1)
        before = hot(iota((rows, rows), 0) < iota((rows, rows), 1))
        ahead = dot(hot(own), before)
        count = jnp.sum(jnp.where(own, 1.0, 0.0), 1, keepdims=True)
        position = jnp.sum(jnp.where(own, ahead, 0.0), 0, keepdims=True).astype(I32)
        beside = jnp.sum(jnp.where(near, count, 0.0), 0, keepdims=True).astype(I32)
        spilled = position >= SEATS
        seat = jnp.where(spilled, beside + position - SEATS, position)
        late = jnp.max(jnp.where(seat >= SEATS, 1.0, 0.0), 1, keepdims=True)
        goes = jnp.where(seat < SEATS, jnp.where(spilled, chip ^ 1, chip), -1)
        line = seat + jnp.where(spilled, 32, 0)
        slot[...] = jnp.where(goes >= 0, goes * BLOCK + seat, -1)
        place[...] = jnp.where(iota(place.shape, 0) == 0, chip, line)
        entries = (
            number,
            group,
            order >> 8,
            order & 255,
            jnp.ones_like(order),
            jnp.where(spilled, 1, 0),
            (line + (me[0] & 7) * BLOCK) & (EXTRA - 1),
            jnp.broadcast_to(me[0], order.shape),
        )
        there = iota((CHIPS, rows), 0) == goes
        tables = [jnp.where(there, entry.astype(F32), 0.0).astype(BF16) for entry in entries]
        seats = hot(iota((EXTRA, rows), 0) == seat)
        fields = dot(jnp.concatenate(tables, 0), seats, COLS)
        lane = iota((CHIPS, EXTRA), 1)
        for at in range(len(entries)):
            field = fields[CHIPS * at : CHIPS * (at + 1), :]
            if at == 0:
                field = jnp.where(lane == EXTRA - 1, late, field)
            ends[:, EXTRA * at : EXTRA * (at + 1)] = field

    pick = hot(iota((block, rows), 0) == slot[...] - step * block)
    moved = dot(pick, unit[...])
    end = ends[pl.ds(pl.multiple_of(step * 8, 8), 8), :]
    last = iota((8, width), 0) == 7
    pieces = []
    for at in range(block // BLOCK):
        top = at * BLOCK
        pieces.append(moved[top : top + 16, :])
        pieces.append(jnp.where(last, end[at : at + 1, :], moved[top + 16 : top + 24, :]))
    out[...] = jnp.concatenate(pieces, 0).astype(BF16)


def gather(spot, count, taken, rows, fields):
    pick = hot(iota((count, CHUNK), 0) == spot)
    return dot(pick, taken[rows, :]), dot(pick, fields, COLS)


def load_chunks(source, taken, copied):
    copies = []
    for at in range(taken.shape[0] // CHUNK):
        rows = pl.ds(at * CHUNK, CHUNK)
        copies.append(pltpu.make_async_copy(source.at[rows, :], taken.at[rows, :], copied.at[at]))
        copies[-1].start()
    return copies


def read_kernel(source, spill, spots, fields, info, taken, pile, ends, strange, copied):
    chunks = taken.shape[0] // CHUNK
    width = taken.shape[1]
    copies = load_chunks(source, taken, copied)
    upto = hot(iota((CHUNK, CHUNK), 0) <= iota((CHUNK, CHUNK), 1))
    place = iota((EXTRA, CHUNK), 1)
    sender = jnp.zeros(place.shape, I32)
    for at in range(1, 8):
        sender = sender + jnp.where(place >= at * BLOCK, 1, 0)
    spread = hot(place - sender * BLOCK == iota((EXTRA, CHUNK), 0))
    mine = (iota((64, CHUNK), 0) & 7) == sender[:64, :]
    spots[...] = jnp.full(spots.shape, -1, I32)
    for copy in copies:
        copy.wait()
    for at in range(CHIPS):
        last = at * BLOCK + SEATS
        top = (last // 16) * 16
        tile = taken[top : top + 16, :].astype(F32)
        ends[at : at + 1, :] = tile[last - top : last - top + 1, :]
    late = jnp.max(ends[:, EXTRA - 1 : EXTRA])
    stack = [
        ends[8 * at : 8 * at + 8, EXTRA * f : EXTRA * (f + 1)]
        for at in range(chunks)
        for f in range(8)
    ]
    wide = dot(jnp.concatenate(stack, 0).astype(BF16), spread)
    natives, foreigns = [], []
    for at in range(chunks):
        part = jnp.where(mine, wide[64 * at : 64 * at + 64, :], 0.0)
        found = [jnp.sum(part[8 * f : 8 * f + 8, :], 0, keepdims=True) for f in range(8)]
        table = jnp.concatenate(found + [jnp.zeros((EXTRA - 8, CHUNK), F32)], 0)
        fields[at] = table.astype(BF16)
        natives.append(found[4] - found[5])
        foreigns.append(found[5])
    both = jnp.concatenate(natives + foreigns, 0)
    running = dot(both.astype(BF16), upto).astype(I32)
    start, start_strange = jnp.int32(0), jnp.int32(0)
    for at in range(chunks):
        native, foreign = natives[at], foreigns[at]
        spots[at : at + 1, 0:CHUNK] = jnp.where(
            native > 0, running[at : at + 1, :] + (start - 1), -1
        )
        strange[at : at + 1, :] = jnp.where(
            foreign > 0, running[chunks + at : chunks + at + 1, :] + (start_strange - 1), -1
        )
        info[at] = (start >> 4) << 4
        start = start + jnp.sum(native).astype(I32)
        start_strange = start_strange + jnp.sum(foreign).astype(I32)
    info[16] = (start + TILE - 1) // TILE
    info[17] = jnp.where((start_strange > SPILL) | (late > 0), 1, 0)
    info[18] = start
    pile[...] = jnp.zeros(pile.shape, F32)

    @pl.when(start_strange > 0)
    def _():
        def step(at, carry):
            rows = pl.ds(pl.multiple_of(at * CHUNK, CHUNK), CHUNK)
            rows_in, side = gather(strange[pl.ds(at, 1), :], SPILL, taken, rows, fields[at])
            pile[:, :width] += rows_in
            pile[:, width:] += side
            return carry

        lax.fori_loop(0, chunks, step, 0)

    spill[...] = pile[...].astype(BF16)


def pack_kernel(info, source, spots, fields, packed, taken, room, copied, placed):
    chunks = taken.shape[0] // CHUNK
    width = taken.shape[1]
    copies = load_chunks(source, taken, copied)
    tiles = info[16]
    room[0:16, :] = jnp.zeros((16, room.shape[1]), BF16)
    first = jnp.int32(0)
    for at in range(chunks):
        first = pl.multiple_of(jnp.minimum(info[at], ROOM - WINDOW), 16)
        spot = spots[at : at + 1, 0:CHUNK] - first
        copies[at].wait()
        rows_in, side = gather(spot, WINDOW, taken, pl.ds(at * CHUNK, CHUNK), fields[at])
        here = pl.ds(first, 16)
        after = pl.ds(pl.multiple_of(first + 16, 16), WINDOW - 16)
        for span, value in ((pl.ds(0, width), rows_in), (pl.ds(width, EXTRA), side)):
            room[here, span] = (room[here, span].astype(F32) + value[:16]).astype(BF16)
            room[after, span] = value[16:].astype(BF16)

    def clear(at, carry):
        room[pl.ds(pl.multiple_of(at * 16, 16), 16), :] = jnp.zeros((16, room.shape[1]), BF16)
        return carry

    lax.fori_loop((first + WINDOW) // 16, tiles * (TILE // 16), clear, 0)
    for wait in (False, True):
        for at in range(TILES):
            rows = pl.ds(at * TILE, TILE)
            copy = pltpu.make_async_copy(room.at[rows, :], packed.at[rows, :], placed.at[at])
            pl.when(at < tiles)(copy.wait if wait else copy.start)


def append_kernel(info, near, packed_in, packed, info_out, window, blank, sems):
    for at in range(20):
        info_out[at] = info[at]
    total, tiles = info[18], info[16]
    count = jnp.sum(near[:, packed.shape[1] - EXTRA :].astype(F32)[:, 4:5]).astype(I32)
    first = (total >> 4) << 4
    fits = (total + count <= PACKED) & (first + SPILL + 16 <= PACKED)

    @pl.when((count > 0) & jnp.logical_not(fits))
    def _():
        info_out[17] = 1

    @pl.when((count > 0) & fits)
    def _():
        more = (total + count + TILE - 1) // TILE
        info_out[16] = more
        begin = pl.multiple_of(first, 16)
        head = pltpu.make_async_copy(
            packed.at[pl.ds(begin, 16), :], window.at[pl.ds(0, 16), :], sems.at[0]
        )
        head.start()

        @pl.when(more > tiles)
        def _():
            blank[...] = jnp.zeros(blank.shape, BF16)

        shift = iota((SPILL + 16, SPILL), 0) - iota((SPILL + 16, SPILL), 1)
        moved = dot(hot(shift == total - first), near[...])
        head.wait()
        keep = iota((16, packed.shape[1]), 0) < total - first
        window[0:16, :] = jnp.where(
            keep, window[0:16, :].astype(F32), moved[:16]
        ).astype(BF16)
        window[16:, :] = moved[16:].astype(BF16)

        @pl.when(more > tiles)
        def _():
            at = pl.multiple_of(tiles * TILE, TILE)
            clear = pltpu.make_async_copy(blank, packed.at[pl.ds(at, TILE), :], sems.at[1])
            clear.start()
            clear.wait()

        put = pltpu.make_async_copy(
            window, packed.at[pl.ds(begin, SPILL + 16), :], sems.at[2]
        )
        put.start()
        put.wait()


def score(queries, low, high, keys, key_tiles, best, marks):
    width = queries.shape[1] - EXTRA

    def mark_step(at, carry):
        span = pl.ds(pl.multiple_of(at * TILE, TILE), TILE)
        side = keys[span, width:].astype(F32).astype(I32)
        mark = (side[:, 1:2] * 128 + side[:, 0:1] + side[:, 4:5]) * 65536
        mark = mark + side[:, 2:3] * 256 + side[:, 3:4]
        marks[span, :] = jnp.broadcast_to(mark, (TILE, TILE))
        return carry

    lax.fori_loop(0, key_tiles, mark_step, 0)

    def against(size):
        def query_step(at, carry):
            rows = pl.ds(pl.multiple_of(at * TILE, TILE), TILE)
            fields = fields_of(queries[rows, width:]).astype(I32)
            cluster = (fields[1:2, :] * 128 + fields[0:1, :] + fields[4:5, :]) * 65536
            upper = cluster + fields[2:3, :] * 256 + fields[3:4, :]
            mark = marks[:size, :]
            scores = dot(keys[:size, :width], queries[rows, :width], COLS)
            earlier = (mark >= cluster) & (mark < upper)
            found = jnp.max(jnp.where(earlier, scores, -1.0), 0, keepdims=True)
            best[:, rows] = jnp.maximum(best[:, rows], found)
            return carry

        lax.fori_loop(low, high, query_step, 0)

    if isinstance(key_tiles, int):
        against(key_tiles * TILE)
        return
    for tiles in range(1, keys.shape[0] // TILE + 1):
        pl.when(key_tiles == tiles)(functools.partial(against, tiles * TILE))


def fetch(source, target, tiles, sems):
    for at in range(TILES):
        rows = pl.ds(at * TILE, TILE)
        copy = pltpu.make_async_copy(source.at[rows, :], target.at[rows, :], sems.at[at])
        pl.when(at < tiles)(copy.start)


def fetched(source, target, tiles, sems):
    for at in range(TILES):
        rows = pl.ds(at * TILE, TILE)
        copy = pltpu.make_async_copy(source.at[rows, :], target.at[rows, :], sems.at[at])
        pl.when(at < tiles)(copy.wait)


def own_kernel(info, packed, best, mine, marks, sems):
    fetch(packed, mine, info[16], sems)
    best[...] = jnp.full(best.shape, -1.0, F32)
    fetched(packed, mine, info[16], sems)
    score(mine, 0, info[16], mine, info[16], best, marks)


def other_kernel(
    info, other_info, packed, other, near, best_in, spots, back,
    mine, theirs, best, marks, sems, other_sems,
):
    tiles, other_tiles = info[16], other_info[16]
    fetch(packed, mine, tiles, sems)
    fetch(other, theirs, other_tiles, other_sems)
    best[:, :PACKED] = best_in[...]
    best[:, PACKED:] = jnp.full((1, best.shape[1] - PACKED), -1.0, F32)
    fetched(packed, mine, tiles, sems)
    fetched(other, theirs, other_tiles, other_sems)
    score(mine, 0, tiles, theirs, other_tiles, best, marks)
    flag = jnp.maximum(info[17], other_info[17]).astype(F32)
    reach = 384
    row = iota((16, reach), 0)

    def stacked(first, count):
        parts = thirds(best[:, pl.ds(pl.multiple_of(first, 128), count)])
        stack = jnp.zeros((16, count), F32)
        for at, part in enumerate(parts):
            stack = jnp.where(row[:, :count] == at, part.astype(F32), stack)
        return stack.astype(BF16)

    sub, lane = iota((8, EXTRA), 0), iota((8, EXTRA), 1)
    lower = (lane >= sub * BLOCK) & (lane < sub * BLOCK + BLOCK)
    upper = (lane + EXTRA >= sub * BLOCK) & (lane + EXTRA < sub * BLOCK + BLOCK)
    empty = jnp.where(((lane - sub * BLOCK) & (EXTRA - 1)) >= 64, flag, 0.0)
    for step in range(CHIPS // 8):
        first = (info[step] >> 7) << 7
        pick = hot(iota((reach, 2 * EXTRA), 0) + first == spots[step : step + 1, :])
        value = jnp.sum(dot(stacked(first, reach), pick), 0, keepdims=True)
        line = jnp.where(upper, value[:, EXTRA:], jnp.where(lower, value[:, :EXTRA], empty))
        back[8 * step : 8 * step + 8, :] = line
    fields = fields_of(near[:, mine.shape[1] - EXTRA :]).astype(I32)
    filled = fields[4:5, :] > 0

    @pl.when(jnp.max(fields[4:5, :].astype(F32)) > 0)
    def _():
        total = info[18]
        first = (total >> 7) << 7
        shift = iota((2 * EXTRA, SPILL), 0) - iota((2 * EXTRA, SPILL), 1)
        pick = hot(shift == total - first)
        value = jnp.sum(dot(stacked(first, 2 * EXTRA), pick), 0, keepdims=True)
        source = (iota((CHIPS, SPILL), 0) == fields[7:8, :]) & filled
        line = hot(iota((EXTRA, SPILL), 0) == fields[6:7, :])
        total = back[...]
        for part in thirds(value):
            held = jnp.where(source, part.astype(F32), 0.0).astype(BF16)
            total = total + dot(held, line, COLS)
        back[...] = total


def home_kernel(me, back, place, highest, flag):
    rows = place.shape[1]
    base = (me[0] & 7) * BLOCK
    pick = hot(iota((CHIPS, rows), 0) == place[0:1, :])
    lines = back[...]
    total = jnp.zeros((EXTRA, rows), F32)
    for part in thirds(lines):
        total = total + dot(part, pick, (((0,), (0,)), ((), ())))
    mine = iota((EXTRA, rows), 0) == ((place[1:2, :] + base) & (EXTRA - 1))
    highest[...] = jnp.sum(jnp.where(mine, total, 0.0), 0, keepdims=True)
    marks = ((iota(lines.shape, 1) - base) & (EXTRA - 1)) >= 64
    flag[0] = jnp.max(jnp.where(marks, lines, 0.0)).astype(I32)


def whole(shape):
    return pl.BlockSpec(shape, lambda *_: (0,) * len(shape))


SCALARS = pl.BlockSpec(memory_space=pltpu.SMEM)
PLACED = pl.BlockSpec(memory_space=pl.ANY)
PARAMS = pltpu.CompilerParams(vmem_limit_bytes=63 * 1024 * 1024)


def array(shape, dtype):
    return jax.ShapeDtypeStruct(shape, dtype)


def exchange(x):
    return lax.all_to_all(
        x, BOTH, split_axis=0, concat_axis=0, tiled=True, axis_index_groups=GROUPS
    )


def direct(embed, owner, local_id, rank):
    rows, width = embed.shape
    full = width + EXTRA
    lines = CHIPS * BLOCK
    chunks = lines // CHUNK
    me = ((lax.axis_index("grp") >> 1) * 8 + lax.axis_index("blk")).astype(I32).reshape(1)
    sent, place = pl.pallas_call(
        send_kernel,
        grid=(chunks,),
        in_specs=[SCALARS, whole((rows, width))] + [whole((1, rows))] * 3,
        out_specs=[pl.BlockSpec((CHUNK, width), lambda i: (i, 0)), whole((8, rows))],
        out_shape=[array((lines, width), BF16), array((8, rows), I32)],
        scratch_shapes=[
            pltpu.VMEM((rows, width), BF16),
            pltpu.VMEM((1, rows), I32),
            pltpu.VMEM((CHIPS, width), F32),
        ],
        compiler_params=PARAMS,
        name="send",
    )(me, embed, owner.reshape(1, rows), local_id.reshape(1, rows), rank.reshape(1, rows))
    taken = exchange(sent.reshape(CHIPS, BLOCK, width)).reshape(lines, width)
    spill, spots, fields, info = pl.pallas_call(
        read_kernel,
        in_specs=[PLACED],
        out_specs=[
            whole((SPILL, full)),
            whole((chunks, 2 * EXTRA)),
            whole((chunks, EXTRA, CHUNK)),
            SCALARS,
        ],
        out_shape=[
            array((SPILL, full), BF16),
            array((chunks, 2 * EXTRA), I32),
            array((chunks, EXTRA, CHUNK), BF16),
            array((32,), I32),
        ],
        scratch_shapes=[
            pltpu.VMEM((lines, width), BF16),
            pltpu.VMEM((SPILL, full), F32),
            pltpu.VMEM((CHIPS, width), F32),
            pltpu.VMEM((chunks, CHUNK), I32),
            pltpu.SemaphoreType.DMA((chunks,)),
        ],
        compiler_params=PARAMS,
        name="read",
    )(taken)
    near = lax.ppermute(spill, BOTH, [(i, i ^ 1) for i in range(2 * CHIPS)])
    packed = pl.pallas_call(
        pack_kernel,
        in_specs=[SCALARS, PLACED, whole((chunks, 2 * EXTRA)), whole((chunks, EXTRA, CHUNK))],
        out_specs=PLACED,
        out_shape=array((PACKED, full), BF16),
        scratch_shapes=[
            pltpu.VMEM((lines, width), BF16),
            pltpu.VMEM((ROOM, full), BF16),
            pltpu.SemaphoreType.DMA((chunks,)),
            pltpu.SemaphoreType.DMA((TILES,)),
        ],
        compiler_params=PARAMS,
        cost_estimate=pl.CostEstimate(
            flops=2 * lines * WINDOW * full, bytes_accessed=4 * lines * full, transcendentals=0
        ),
        name="pack",
    )(info, taken, spots, fields)
    packed, info = pl.pallas_call(
        append_kernel,
        in_specs=[SCALARS, whole((SPILL, full)), PLACED],
        out_specs=[PLACED, SCALARS],
        out_shape=[array((PACKED, full), BF16), array((32,), I32)],
        scratch_shapes=[
            pltpu.VMEM((SPILL + 16, full), BF16),
            pltpu.VMEM((TILE, full), BF16),
            pltpu.SemaphoreType.DMA((3,)),
        ],
        input_output_aliases={2: 0},
        compiler_params=PARAMS,
        name="append",
    )(info, near, packed)
    swap = [(i, i ^ 1) for i in range(16)]
    other_info = lax.ppermute(info, "grp", swap)
    other = lax.ppermute(packed, "grp", swap)
    best = pl.pallas_call(
        own_kernel,
        in_specs=[SCALARS, PLACED],
        out_specs=whole((1, PACKED)),
        out_shape=array((1, PACKED), F32),
        scratch_shapes=[
            pltpu.VMEM((PACKED, full), BF16),
            pltpu.VMEM((PACKED, TILE), I32),
            pltpu.SemaphoreType.DMA((TILES,)),
        ],
        compiler_params=PARAMS,
        cost_estimate=pl.CostEstimate(
            flops=2 * 1024 * 1024 * width, bytes_accessed=2 * PACKED * full, transcendentals=0
        ),
        name="own",
    )(info, packed)
    back = pl.pallas_call(
        other_kernel,
        in_specs=[SCALARS, SCALARS, PLACED, PLACED]
        + [whole((SPILL, full)), whole((1, PACKED)), whole((chunks, 2 * EXTRA))],
        out_specs=whole((CHIPS, EXTRA)),
        out_shape=array((CHIPS, EXTRA), F32),
        scratch_shapes=[
            pltpu.VMEM((PACKED, full), BF16),
            pltpu.VMEM((PACKED, full), BF16),
            pltpu.VMEM((1, PACKED + 2 * TILE), F32),
            pltpu.VMEM((PACKED, TILE), I32),
            pltpu.SemaphoreType.DMA((TILES,)),
            pltpu.SemaphoreType.DMA((TILES,)),
        ],
        compiler_params=PARAMS,
        name="other",
    )(info, other_info, packed, other, near, best, spots)
    home = exchange(back)
    highest, flag = pl.pallas_call(
        home_kernel,
        in_specs=[SCALARS, whole((CHIPS, EXTRA)), whole((8, rows))],
        out_specs=[whole((1, rows)), SCALARS],
        out_shape=[array((1, rows), F32), array((1,), I32)],
        compiler_params=PARAMS,
        name="home",
    )(me, home, place)
    return highest.reshape(rows), flag[0]


def group_kernel(queries, keys, best_in, best, marks):
    best[...] = best_in[...]
    tiles = keys.shape[0] // TILE
    score(queries, 0, tiles, keys, tiles, best, marks)


def by_group(embed, owner, local_id, rank):
    n_group, n_block = lax.axis_size("grp"), lax.axis_size("blk")
    row_count, columns = embed.shape
    capacity = row_count // 8
    width = n_group * capacity
    full = columns + EXTRA
    wide = embed.astype(F32)
    unit = (wide * lax.rsqrt(jnp.sum(wide * wide, 1, keepdims=True) + EPS)).astype(BF16)
    target = owner[:, 0]
    onehot = (target[:, None] == jnp.arange(n_group, dtype=I32)[None, :]).astype(I32)
    position = jnp.sum((jnp.cumsum(onehot, 0) - 1) * onehot, 1)
    slot_index = target * capacity + position
    fields = jnp.stack([local_id, target, rank >> 8, rank & 255, jnp.ones_like(rank)], 1)
    fields = jnp.pad(fields, ((0, 0), (0, EXTRA - 5))).astype(BF16)
    sent = jnp.zeros((width, full), BF16).at[slot_index].set(jnp.concatenate([unit, fields], 1))
    routed = lax.all_to_all(
        sent.reshape(n_group, capacity, full), "grp", split_axis=0, concat_axis=0, tiled=True
    ).reshape(width, full)
    best = jnp.full((1, width), -1.0, F32)
    for by in range(n_block):
        turn = [(i, (i + by) % n_block) for i in range(n_block)]
        best = pl.pallas_call(
            group_kernel,
            in_specs=[whole((width, full))] * 2 + [whole((1, width))],
            out_specs=whole((1, width)),
            out_shape=array((1, width), F32),
            scratch_shapes=[pltpu.VMEM((width, TILE), I32)],
            compiler_params=PARAMS,
            name="group",
        )(routed, lax.ppermute(routed, "blk", turn) if by else routed, best)
    home = lax.all_to_all(
        best.reshape(n_group, capacity), "grp", split_axis=0, concat_axis=0, tiled=True
    )
    return home.reshape(width)[slot_index]


def per_device(embed, owner, local_id, rank):
    highest, flag = direct(embed, owner, local_id, rank)
    return lax.cond(
        flag > 0, lambda: by_group(embed, owner, local_id, rank), lambda: highest
    )


def solution(mesh):
    in_specs = (
        P(("grp", "blk"), None),
        P(("grp", "blk"), None),
        P(("grp", "blk")),
        P(("grp", "blk")),
    )
    out_specs = P(("grp", "blk"))
    return jax.shard_map(
        per_device, mesh=mesh, in_specs=in_specs, out_specs=out_specs, check_vma=False
    )
```

```python
import functools

import jax
import jax.numpy as jnp
from jax import lax
from jax.experimental import pallas as pl
from jax.experimental.pallas import tpu as pltpu
from jax.sharding import PartitionSpec as P

EPS = 1e-06
BOTH = ("grp", "blk")
CHIPS = 64
BLOCK = 24
SEATS = 23
EXTRA = 128
CHUNK = 8 * BLOCK
WINDOW = CHUNK + 16
TILE = 256
TILES = 6
PACKED = TILE * TILES
ROOM = PACKED
SPILL = 128
GROUPS = [[g * 8 + b for g in range(core, 16, 2) for b in range(8)] for core in range(2)]
COLS = (((1,), (1,)), ((), ()))
F32 = jnp.float32
BF16 = jnp.bfloat16
I32 = jnp.int32
LOWEST = -(2**31)


def iota(shape, dim):
    return lax.broadcasted_iota(I32, shape, dim)


def hot(mask):
    return jnp.where(mask, jnp.float32(1), jnp.float32(0)).astype(BF16)


def dot(a, b, dims=(((1,), (0,)), ((), ()))):
    return lax.dot_general(a, b, dims, preferred_element_type=F32)


def thirds(x):
    high = x.astype(BF16)
    rest = x - high.astype(F32)
    middle = rest.astype(BF16)
    return high, middle, (rest - middle.astype(F32)).astype(BF16)


def fields_of(extra):
    return dot(hot(iota((16, EXTRA), 0) == iota((16, EXTRA), 1)), extra, COLS)


def send_kernel(me, embed, owner, local, rank, out, place, unit, slot, ends):
    rows, width = embed.shape
    step = pl.program_id(0)
    block = out.shape[0]

    @pl.when(step == 0)
    def _():
        wide = embed[...].astype(F32)
        scale = lax.rsqrt(jnp.sum(wide * wide, 1, keepdims=True) + EPS)
        unit[...] = (wide * scale).astype(BF16)
        group, number, order = owner[...], local[...], rank[...]
        chip = (number & (CHIPS - 1)) ^ (group * 4)
        own = iota((CHIPS, rows), 0) == chip
        near = iota((CHIPS, rows), 0) == (chip ^ 1)
        before = hot(iota((rows, rows), 0) < iota((rows, rows), 1))
        ahead = dot(hot(own), before)
        count = jnp.sum(jnp.where(own, 1.0, 0.0), 1, keepdims=True)
        position = jnp.sum(jnp.where(own, ahead, 0.0), 0, keepdims=True).astype(I32)
        beside = jnp.sum(jnp.where(near, count, 0.0), 0, keepdims=True).astype(I32)
        spilled = position >= SEATS
        seat = jnp.where(spilled, beside + position - SEATS, position)
        late = jnp.max(jnp.where(seat >= SEATS, 1.0, 0.0), 1, keepdims=True)
        goes = jnp.where(seat < SEATS, jnp.where(spilled, chip ^ 1, chip), -1)
        line = seat + jnp.where(spilled, 32, 0)
        slot[...] = jnp.where(goes >= 0, goes * BLOCK + seat, -1)
        place[...] = jnp.where(iota(place.shape, 0) == 0, chip, line)
        entries = (
            number,
            group,
            order >> 8,
            order & 255,
            jnp.ones_like(order),
            jnp.where(spilled, 1, 0),
            (line + (me[0] & 7) * BLOCK) & (EXTRA - 1),
            jnp.broadcast_to(me[0], order.shape),
        )
        there = iota((CHIPS, rows), 0) == goes
        tables = [jnp.where(there, entry.astype(F32), 0.0).astype(BF16) for entry in entries]
        seats = hot(iota((EXTRA, rows), 0) == seat)
        fields = dot(jnp.concatenate(tables, 0), seats, COLS)
        lane = iota((CHIPS, EXTRA), 1)
        for at in range(len(entries)):
            field = fields[CHIPS * at : CHIPS * (at + 1), :]
            if at == 0:
                field = jnp.where(lane == EXTRA - 1, late, field)
            ends[:, EXTRA * at : EXTRA * (at + 1)] = field

    pick = hot(iota((block, rows), 0) == slot[...] - step * block)
    moved = dot(pick, unit[...])
    senders = block // BLOCK
    end = ends[pl.ds(pl.multiple_of(step * senders, 8), senders), :]
    last = iota((8, width), 0) == 7
    pieces = []
    for at in range(block // BLOCK):
        top = at * BLOCK
        pieces.append(moved[top : top + 16, :])
        pieces.append(jnp.where(last, end[at : at + 1, :], moved[top + 16 : top + 24, :]))
    out[...] = jnp.concatenate(pieces, 0).astype(BF16)


def gather(spot, count, taken, rows, fields):
    pick = hot(iota((count, CHUNK), 0) == spot)
    return dot(pick, taken[rows, :]), dot(pick, fields, COLS)


def load_chunks(source, taken, copied):
    copies = []
    for at in range(taken.shape[0] // CHUNK):
        rows = pl.ds(at * CHUNK, CHUNK)
        copies.append(pltpu.make_async_copy(source.at[rows, :], taken.at[rows, :], copied.at[at]))
        copies[-1].start()
    return copies


def read_kernel(source, spill, spots, fields, info, taken, pile, ends, strange, copied):
    chunks = taken.shape[0] // CHUNK
    width = taken.shape[1]
    copies = load_chunks(source, taken, copied)
    upto = hot(iota((CHUNK, CHUNK), 0) <= iota((CHUNK, CHUNK), 1))
    place = iota((EXTRA, CHUNK), 1)
    sender = jnp.zeros(place.shape, I32)
    for at in range(1, 8):
        sender = sender + jnp.where(place >= at * BLOCK, 1, 0)
    spread = hot(place - sender * BLOCK == iota((EXTRA, CHUNK), 0))
    mine = (iota((64, CHUNK), 0) & 7) == sender[:64, :]
    spots[...] = jnp.full(spots.shape, -1, I32)
    for copy in copies:
        copy.wait()
    for at in range(CHIPS):
        last = at * BLOCK + SEATS
        top = (last // 16) * 16
        tile = taken[top : top + 16, :].astype(F32)
        ends[at : at + 1, :] = tile[last - top : last - top + 1, :]
    late = jnp.max(ends[:, EXTRA - 1 : EXTRA])
    stack = [
        ends[8 * at : 8 * at + 8, EXTRA * f : EXTRA * (f + 1)]
        for at in range(chunks)
        for f in range(8)
    ]
    wide = dot(jnp.concatenate(stack, 0).astype(BF16), spread)
    natives, foreigns = [], []
    for at in range(chunks):
        part = jnp.where(mine, wide[64 * at : 64 * at + 64, :], 0.0)
        found = [jnp.sum(part[8 * f : 8 * f + 8, :], 0, keepdims=True) for f in range(8)]
        table = jnp.concatenate(found + [jnp.zeros((EXTRA - 8, CHUNK), F32)], 0)
        fields[at] = table.astype(BF16)
        natives.append(found[4] - found[5])
        foreigns.append(found[5])
    both = jnp.concatenate(natives + foreigns, 0)
    running = dot(both.astype(BF16), upto).astype(I32)
    start, start_strange = jnp.int32(0), jnp.int32(0)
    for at in range(chunks):
        native, foreign = natives[at], foreigns[at]
        spots[at : at + 1, 0:CHUNK] = jnp.where(
            native > 0, running[at : at + 1, :] + (start - 1), -1
        )
        strange[at : at + 1, :] = jnp.where(
            foreign > 0, running[chunks + at : chunks + at + 1, :] + (start_strange - 1), -1
        )
        info[at] = (start >> 4) << 4
        start = start + jnp.sum(native).astype(I32)
        start_strange = start_strange + jnp.sum(foreign).astype(I32)
    info[16] = (start + TILE - 1) // TILE
    info[17] = jnp.where((start_strange > SPILL) | (late > 0), 1, 0)
    info[18] = start
    pile[...] = jnp.zeros(pile.shape, F32)

    @pl.when(start_strange > 0)
    def _():
        def step(at, carry):
            rows = pl.ds(pl.multiple_of(at * CHUNK, CHUNK), CHUNK)
            rows_in, side = gather(strange[pl.ds(at, 1), :], SPILL, taken, rows, fields[at])
            pile[:, :width] += rows_in
            pile[:, width:] += side
            return carry

        lax.fori_loop(0, chunks, step, 0)

    spill[...] = pile[...].astype(BF16)


def pack_kernel(info, source, spots, fields, packed, taken, room, copied, placed):
    chunks = taken.shape[0] // CHUNK
    width = taken.shape[1]
    copies = load_chunks(source, taken, copied)
    tiles = info[16]
    room[0:16, :] = jnp.zeros((16, room.shape[1]), BF16)
    first = jnp.int32(0)
    done = jnp.int32(0)

    def put(at):
        rows = pl.ds(pl.multiple_of(at * TILE, TILE), TILE)
        return pltpu.make_async_copy(room.at[rows, :], packed.at[rows, :], placed.at[at])

    for at in range(chunks):
        first = pl.multiple_of(jnp.minimum(info[at], ROOM - WINDOW), 16)
        spot = spots[at : at + 1, 0:CHUNK] - first
        copies[at].wait()
        rows_in, side = gather(spot, WINDOW, taken, pl.ds(at * CHUNK, CHUNK), fields[at])
        here = pl.ds(first, 16)
        after = pl.ds(pl.multiple_of(first + 16, 16), WINDOW - 16)
        for span, value in ((pl.ds(0, width), rows_in), (pl.ds(width, EXTRA), side)):
            room[here, span] = (room[here, span].astype(F32) + value[:16]).astype(BF16)
            room[after, span] = value[16:].astype(BF16)
        if at + 1 < chunks:
            filled = info[at + 1] // TILE
            pl.when(filled > done)(put(done).start)
            done = filled

    def clear(at, carry):
        room[pl.ds(pl.multiple_of(at * 16, 16), 16), :] = jnp.zeros((16, room.shape[1]), BF16)
        return carry

    lax.fori_loop((first + WINDOW) // 16, tiles * (TILE // 16), clear, 0)
    for at in range(TILES):
        pl.when((at >= done) & (at < tiles))(put(at).start)
    for at in range(TILES):
        pl.when(at < tiles)(put(at).wait)


def append_kernel(info, near, packed_in, packed, info_out, window, blank, sems):
    for at in range(20):
        info_out[at] = info[at]
    total, tiles = info[18], info[16]
    count = jnp.sum(near[:, packed.shape[1] - EXTRA :].astype(F32)[:, 4:5]).astype(I32)
    first = (total >> 4) << 4
    fits = (total + count <= PACKED) & (first + SPILL + 16 <= PACKED)

    @pl.when((count > 0) & jnp.logical_not(fits))
    def _():
        info_out[17] = 1

    @pl.when((count > 0) & fits)
    def _():
        more = (total + count + TILE - 1) // TILE
        info_out[16] = more
        begin = pl.multiple_of(first, 16)
        head = pltpu.make_async_copy(
            packed.at[pl.ds(begin, 16), :], window.at[pl.ds(0, 16), :], sems.at[0]
        )
        head.start()

        @pl.when(more > tiles)
        def _():
            blank[...] = jnp.zeros(blank.shape, BF16)

        shift = iota((SPILL + 16, SPILL), 0) - iota((SPILL + 16, SPILL), 1)
        moved = dot(hot(shift == total - first), near[...])
        head.wait()
        keep = iota((16, packed.shape[1]), 0) < total - first
        window[0:16, :] = jnp.where(
            keep, window[0:16, :].astype(F32), moved[:16]
        ).astype(BF16)
        window[16:, :] = moved[16:].astype(BF16)

        @pl.when(more > tiles)
        def _():
            at = pl.multiple_of(tiles * TILE, TILE)
            clear = pltpu.make_async_copy(blank, packed.at[pl.ds(at, TILE), :], sems.at[1])
            clear.start()
            clear.wait()

        put = pltpu.make_async_copy(
            window, packed.at[pl.ds(begin, SPILL + 16), :], sems.at[2]
        )
        put.start()
        put.wait()


def score(queries, query_tiles, keys, key_tiles, best, marks, bounds):
    width = queries.shape[1] - EXTRA
    fields = fields_of(queries[:, width:]).astype(I32)
    bounds[0:1, :] = (fields[1:2, :] * 128 + fields[0:1, :] + fields[4:5, :]) * 65536
    bounds[1:2, :] = fields[2:3, :] * 256 + fields[3:4, :] + LOWEST

    def mark_step(at, carry):
        span = pl.ds(pl.multiple_of(at * TILE, TILE), TILE)
        side = keys[span, width:].astype(F32).astype(I32)
        mark = (side[:, 1:2] * 128 + side[:, 0:1] + side[:, 4:5]) * 65536
        mark = mark + side[:, 2:3] * 256 + side[:, 3:4] + LOWEST
        marks[span, :] = jnp.broadcast_to(mark, (TILE, EXTRA))
        return carry

    lax.fori_loop(0, key_tiles, mark_step, 0)

    def against(size):
        def query_step(at, carry):
            rows = pl.ds(pl.multiple_of(at * TILE, TILE), TILE)
            mark = marks[:size, :]
            mark = jnp.concatenate([mark] * (TILE // EXTRA), 1)
            scores = dot(keys[:size, :width], queries[rows, :width], COLS)
            earlier = mark - bounds[0:1, rows] < bounds[1:2, rows]
            found = jnp.max(jnp.where(earlier, scores, -1.0), 0, keepdims=True)
            best[:, rows] = jnp.maximum(best[:, rows], found)
            return carry

        lax.fori_loop(0, query_tiles, query_step, 0)

    if isinstance(key_tiles, int):
        against(key_tiles * TILE)
        return
    for tiles in range(1, keys.shape[0] // TILE + 1):
        pl.when(key_tiles == tiles)(functools.partial(against, tiles * TILE))


def fetch(source, target, tiles, sems):
    for at in range(TILES):
        rows = pl.ds(at * TILE, TILE)
        copy = pltpu.make_async_copy(source.at[rows, :], target.at[rows, :], sems.at[at])
        pl.when(at < tiles)(copy.start)


def fetched(source, target, tiles, sems):
    for at in range(TILES):
        rows = pl.ds(at * TILE, TILE)
        copy = pltpu.make_async_copy(source.at[rows, :], target.at[rows, :], sems.at[at])
        pl.when(at < tiles)(copy.wait)


def own_kernel(info, packed, best, mine, marks, bounds, sems):
    fetch(packed, mine, info[16], sems)
    best[...] = jnp.full(best.shape, -1.0, F32)
    fetched(packed, mine, info[16], sems)
    score(mine, info[16], mine, info[16], best, marks, bounds)


def other_kernel(
    info, other_info, packed, other, near, best_in, spots, back,
    mine, theirs, best, split, marks, bounds, sems, other_sems,
):
    tiles, other_tiles = info[16], other_info[16]
    fetch(packed, mine, tiles, sems)
    fetch(other, theirs, other_tiles, other_sems)
    best[:, :PACKED] = best_in[...]
    best[:, PACKED:] = jnp.full((1, best.shape[1] - PACKED), -1.0, F32)
    fetched(packed, mine, tiles, sems)
    fetched(other, theirs, other_tiles, other_sems)
    score(mine, tiles, theirs, other_tiles, best, marks, bounds)
    flag = jnp.maximum(info[17], other_info[17]).astype(F32)
    reach = 384
    row = iota((16, best.shape[1]), 0)
    stack = jnp.zeros(row.shape, F32)
    for at, part in enumerate(thirds(best[...])):
        stack = jnp.where(row == at, part.astype(F32), stack)
    split[...] = stack.astype(BF16)

    def stacked(first, count):
        return split[:, pl.ds(pl.multiple_of(first, 128), count)]

    sub, lane = iota((8, EXTRA), 0), iota((8, EXTRA), 1)
    lower = (lane >= sub * BLOCK) & (lane < sub * BLOCK + BLOCK)
    upper = (lane + EXTRA >= sub * BLOCK) & (lane + EXTRA < sub * BLOCK + BLOCK)
    empty = jnp.where(((lane - sub * BLOCK) & (EXTRA - 1)) >= 64, flag, 0.0)
    for step in range(CHIPS // 8):
        first = (info[step] >> 7) << 7
        pick = hot(iota((reach, 2 * EXTRA), 0) + first == spots[step : step + 1, :])
        value = jnp.sum(dot(stacked(first, reach), pick), 0, keepdims=True)
        line = jnp.where(upper, value[:, EXTRA:], jnp.where(lower, value[:, :EXTRA], empty))
        back[8 * step : 8 * step + 8, :] = line
    fields = fields_of(near[:, mine.shape[1] - EXTRA :]).astype(I32)
    filled = fields[4:5, :] > 0

    @pl.when(jnp.max(fields[4:5, :].astype(F32)) > 0)
    def _():
        total = info[18]
        first = (total >> 7) << 7
        shift = iota((2 * EXTRA, SPILL), 0) - iota((2 * EXTRA, SPILL), 1)
        pick = hot(shift == total - first)
        value = jnp.sum(dot(stacked(first, 2 * EXTRA), pick), 0, keepdims=True)
        source = (iota((CHIPS, SPILL), 0) == fields[7:8, :]) & filled
        line = hot(iota((EXTRA, SPILL), 0) == fields[6:7, :])
        total = back[...]
        for part in thirds(value):
            held = jnp.where(source, part.astype(F32), 0.0).astype(BF16)
            total = total + dot(held, line, COLS)
        back[...] = total


def home_kernel(me, back, place, highest, flag):
    rows = place.shape[1]
    base = (me[0] & 7) * BLOCK
    pick = hot(iota((CHIPS, rows), 0) == place[0:1, :])
    lines = back[...]
    total = jnp.zeros((EXTRA, rows), F32)
    for part in thirds(lines):
        total = total + dot(part, pick, (((0,), (0,)), ((), ())))
    mine = iota((EXTRA, rows), 0) == ((place[1:2, :] + base) & (EXTRA - 1))
    highest[...] = jnp.sum(jnp.where(mine, total, 0.0), 0, keepdims=True)
    marks = ((iota(lines.shape, 1) - base) & (EXTRA - 1)) >= 64
    flag[0] = jnp.max(jnp.where(marks, lines, 0.0)).astype(I32)


def whole(shape):
    return pl.BlockSpec(shape, lambda *_: (0,) * len(shape))


SCALARS = pl.BlockSpec(memory_space=pltpu.SMEM)
PLACED = pl.BlockSpec(memory_space=pl.ANY)
PARAMS = pltpu.CompilerParams(vmem_limit_bytes=63 * 1024 * 1024)
LESS = pltpu.CompilerParams(vmem_limit_bytes=28 * 1024 * 1024)


def array(shape, dtype):
    return jax.ShapeDtypeStruct(shape, dtype)


def exchange(x):
    return lax.all_to_all(
        x, BOTH, split_axis=0, concat_axis=0, tiled=True, axis_index_groups=GROUPS
    )


def direct(embed, owner, local_id, rank):
    rows, width = embed.shape
    full = width + EXTRA
    lines = CHIPS * BLOCK
    chunks = lines // CHUNK
    me = ((lax.axis_index("grp") >> 1) * 8 + lax.axis_index("blk")).astype(I32).reshape(1)
    sent, place = pl.pallas_call(
        send_kernel,
        grid=(chunks // 2,),
        in_specs=[SCALARS, whole((rows, width))] + [whole((1, rows))] * 3,
        out_specs=[pl.BlockSpec((2 * CHUNK, width), lambda i: (i, 0)), whole((8, rows))],
        out_shape=[array((lines, width), BF16), array((8, rows), I32)],
        scratch_shapes=[
            pltpu.VMEM((rows, width), BF16),
            pltpu.VMEM((1, rows), I32),
            pltpu.VMEM((CHIPS, width), F32),
        ],
        compiler_params=PARAMS,
        name="send",
    )(me, embed, owner.reshape(1, rows), local_id.reshape(1, rows), rank.reshape(1, rows))
    taken = exchange(sent.reshape(CHIPS, BLOCK, width)).reshape(lines, width)
    spill, spots, fields, info = pl.pallas_call(
        read_kernel,
        in_specs=[PLACED],
        out_specs=[
            whole((SPILL, full)),
            whole((chunks, 2 * EXTRA)),
            whole((chunks, EXTRA, CHUNK)),
            SCALARS,
        ],
        out_shape=[
            array((SPILL, full), BF16),
            array((chunks, 2 * EXTRA), I32),
            array((chunks, EXTRA, CHUNK), BF16),
            array((32,), I32),
        ],
        scratch_shapes=[
            pltpu.VMEM((lines, width), BF16),
            pltpu.VMEM((SPILL, full), F32),
            pltpu.VMEM((CHIPS, width), F32),
            pltpu.VMEM((chunks, CHUNK), I32),
            pltpu.SemaphoreType.DMA((chunks,)),
        ],
        compiler_params=PARAMS,
        name="read",
    )(taken)
    near = lax.ppermute(spill, BOTH, [(i, i ^ 1) for i in range(2 * CHIPS)])
    packed = pl.pallas_call(
        pack_kernel,
        in_specs=[SCALARS, PLACED, whole((chunks, 2 * EXTRA)), whole((chunks, EXTRA, CHUNK))],
        out_specs=PLACED,
        out_shape=array((PACKED, full), BF16),
        scratch_shapes=[
            pltpu.VMEM((lines, width), BF16),
            pltpu.VMEM((ROOM, full), BF16),
            pltpu.SemaphoreType.DMA((chunks,)),
            pltpu.SemaphoreType.DMA((TILES,)),
        ],
        compiler_params=PARAMS,
        cost_estimate=pl.CostEstimate(
            flops=2 * lines * WINDOW * full, bytes_accessed=4 * lines * full, transcendentals=0
        ),
        name="pack",
    )(info, taken, spots, fields)
    packed, info = pl.pallas_call(
        append_kernel,
        in_specs=[SCALARS, whole((SPILL, full)), PLACED],
        out_specs=[PLACED, SCALARS],
        out_shape=[array((PACKED, full), BF16), array((32,), I32)],
        scratch_shapes=[
            pltpu.VMEM((SPILL + 16, full), BF16),
            pltpu.VMEM((TILE, full), BF16),
            pltpu.SemaphoreType.DMA((3,)),
        ],
        input_output_aliases={2: 0},
        compiler_params=LESS,
        name="append",
    )(info, near, packed)
    swap = [(i, i ^ 1) for i in range(16)]
    other_info = lax.ppermute(info, "grp", swap)
    other = lax.ppermute(packed, "grp", swap)
    best = pl.pallas_call(
        own_kernel,
        in_specs=[SCALARS, PLACED],
        out_specs=whole((1, PACKED)),
        out_shape=array((1, PACKED), F32),
        scratch_shapes=[
            pltpu.VMEM((PACKED, full), BF16),
            pltpu.VMEM((PACKED, EXTRA), I32),
            pltpu.VMEM((8, PACKED), I32),
            pltpu.SemaphoreType.DMA((TILES,)),
        ],
        compiler_params=LESS,
        cost_estimate=pl.CostEstimate(
            flops=2 * 1024 * 1024 * width, bytes_accessed=2 * PACKED * full, transcendentals=0
        ),
        name="own",
    )(info, packed)
    back = pl.pallas_call(
        other_kernel,
        in_specs=[SCALARS, SCALARS, PLACED, PLACED]
        + [whole((SPILL, full)), whole((1, PACKED)), whole((chunks, 2 * EXTRA))],
        out_specs=whole((CHIPS, EXTRA)),
        out_shape=array((CHIPS, EXTRA), F32),
        scratch_shapes=[
            pltpu.VMEM((PACKED, full), BF16),
            pltpu.VMEM((PACKED, full), BF16),
            pltpu.VMEM((1, PACKED + 2 * TILE), F32),
            pltpu.VMEM((16, PACKED + 2 * TILE), BF16),
            pltpu.VMEM((PACKED, EXTRA), I32),
            pltpu.VMEM((8, PACKED), I32),
            pltpu.SemaphoreType.DMA((TILES,)),
            pltpu.SemaphoreType.DMA((TILES,)),
        ],
        compiler_params=LESS,
        name="other",
    )(info, other_info, packed, other, near, best, spots)
    home = exchange(back)
    highest, flag = pl.pallas_call(
        home_kernel,
        in_specs=[SCALARS, whole((CHIPS, EXTRA)), whole((8, rows))],
        out_specs=[whole((1, rows)), SCALARS],
        out_shape=[array((1, rows), F32), array((1,), I32)],
        compiler_params=LESS,
        name="home",
    )(me, home, place)
    return highest.reshape(rows), flag[0]


def group_kernel(queries, keys, best_in, best, marks, bounds):
    best[...] = best_in[...]
    tiles = keys.shape[0] // TILE
    score(queries, tiles, keys, tiles, best, marks, bounds)


def by_group(embed, owner, local_id, rank):
    n_group, n_block = lax.axis_size("grp"), lax.axis_size("blk")
    row_count, columns = embed.shape
    capacity = row_count // 8
    width = n_group * capacity
    full = columns + EXTRA
    wide = embed.astype(F32)
    unit = (wide * lax.rsqrt(jnp.sum(wide * wide, 1, keepdims=True) + EPS)).astype(BF16)
    target = owner[:, 0]
    onehot = (target[:, None] == jnp.arange(n_group, dtype=I32)[None, :]).astype(I32)
    position = jnp.sum((jnp.cumsum(onehot, 0) - 1) * onehot, 1)
    slot_index = target * capacity + position
    fields = jnp.stack([local_id, target, rank >> 8, rank & 255, jnp.ones_like(rank)], 1)
    fields = jnp.pad(fields, ((0, 0), (0, EXTRA - 5))).astype(BF16)
    sent = jnp.zeros((width, full), BF16).at[slot_index].set(jnp.concatenate([unit, fields], 1))
    routed = lax.all_to_all(
        sent.reshape(n_group, capacity, full), "grp", split_axis=0, concat_axis=0, tiled=True
    ).reshape(width, full)
    best = jnp.full((1, width), -1.0, F32)
    for by in range(n_block):
        turn = [(i, (i + by) % n_block) for i in range(n_block)]
        best = pl.pallas_call(
            group_kernel,
            in_specs=[whole((width, full))] * 2 + [whole((1, width))],
            out_specs=whole((1, width)),
            out_shape=array((1, width), F32),
            scratch_shapes=[pltpu.VMEM((width, EXTRA), I32), pltpu.VMEM((8, width), I32)],
            compiler_params=PARAMS,
            name="group",
        )(routed, lax.ppermute(routed, "blk", turn) if by else routed, best)
    home = lax.all_to_all(
        best.reshape(n_group, capacity), "grp", split_axis=0, concat_axis=0, tiled=True
    )
    return home.reshape(width)[slot_index]


def per_device(embed, owner, local_id, rank):
    highest, flag = direct(embed, owner, local_id, rank)
    return lax.cond(
        flag > 0, lambda: by_group(embed, owner, local_id, rank), lambda: highest
    )


def solution(mesh):
    in_specs = (
        P(("grp", "blk"), None),
        P(("grp", "blk"), None),
        P(("grp", "blk")),
        P(("grp", "blk")),
    )
    out_specs = P(("grp", "blk"))
    return jax.shard_map(
        per_device, mesh=mesh, in_specs=in_specs, out_specs=out_specs, check_vma=False
    )
```

```python
import functools

import jax
import jax.numpy as jnp
from jax import lax
from jax.experimental import pallas as pl
from jax.experimental.pallas import tpu as pltpu
from jax.sharding import PartitionSpec as P

EPS = 1e-06
BOTH = ("grp", "blk")
CHIPS = 64
BLOCK = 24
SEATS = 23
EXTRA = 128
CHUNK = 8 * BLOCK
WINDOW = CHUNK + 16
TILE = 256
TILES = 6
PACKED = TILE * TILES
ROOM = PACKED
SPILL = 128
GROUPS = [[g * 8 + b for g in range(core, 16, 2) for b in range(8)] for core in range(2)]
COLS = (((1,), (1,)), ((), ()))
F32 = jnp.float32
BF16 = jnp.bfloat16
I32 = jnp.int32
LOWEST = -(2**31)


def iota(shape, dim):
    return lax.broadcasted_iota(I32, shape, dim)


def hot(mask):
    return jnp.where(mask, jnp.float32(1), jnp.float32(0)).astype(BF16)


def dot(a, b, dims=(((1,), (0,)), ((), ()))):
    return lax.dot_general(a, b, dims, preferred_element_type=F32)


def thirds(x):
    high = x.astype(BF16)
    rest = x - high.astype(F32)
    middle = rest.astype(BF16)
    return high, middle, (rest - middle.astype(F32)).astype(BF16)


def fields_of(extra):
    return dot(hot(iota((16, EXTRA), 0) == iota((16, EXTRA), 1)), extra, COLS)


def send_kernel(me, embed, owner, local, rank, out, place, unit, slot, ends):
    rows, width = embed.shape
    step = pl.program_id(0)
    block = out.shape[0]

    @pl.when(step == 0)
    def _():
        wide = embed[...].astype(F32)
        scale = lax.rsqrt(jnp.sum(wide * wide, 1, keepdims=True) + EPS)
        unit[...] = (wide * scale).astype(BF16)
        group, number, order = owner[...], local[...], rank[...]
        chip = (number & (CHIPS - 1)) ^ (group * 4)
        own = iota((CHIPS, rows), 0) == chip
        near = iota((CHIPS, rows), 0) == (chip ^ 1)
        before = hot(iota((rows, rows), 0) < iota((rows, rows), 1))
        ahead = dot(hot(own), before)
        count = jnp.sum(jnp.where(own, 1.0, 0.0), 1, keepdims=True)
        position = jnp.sum(jnp.where(own, ahead, 0.0), 0, keepdims=True).astype(I32)
        beside = jnp.sum(jnp.where(near, count, 0.0), 0, keepdims=True).astype(I32)
        spilled = position >= SEATS
        seat = jnp.where(spilled, beside + position - SEATS, position)
        late = jnp.max(jnp.where(seat >= SEATS, 1.0, 0.0), 1, keepdims=True)
        goes = jnp.where(seat < SEATS, jnp.where(spilled, chip ^ 1, chip), -1)
        line = seat + jnp.where(spilled, 32, 0)
        slot[...] = jnp.where(goes >= 0, goes * BLOCK + seat, -1)
        place[...] = jnp.where(iota(place.shape, 0) == 0, chip, line)
        entries = (
            number,
            group,
            order >> 8,
            order & 255,
            jnp.ones_like(order),
            jnp.where(spilled, 1, 0),
            (line + (me[0] & 7) * BLOCK) & (EXTRA - 1),
            jnp.broadcast_to(me[0], order.shape),
        )
        there = iota((CHIPS, rows), 0) == goes
        tables = [jnp.where(there, entry.astype(F32), 0.0).astype(BF16) for entry in entries]
        seats = hot(iota((EXTRA, rows), 0) == seat)
        fields = dot(jnp.concatenate(tables, 0), seats, COLS)
        lane = iota((CHIPS, EXTRA), 1)
        for at in range(len(entries)):
            field = fields[CHIPS * at : CHIPS * (at + 1), :]
            if at == 0:
                field = jnp.where(lane == EXTRA - 1, late, field)
            ends[:, EXTRA * at : EXTRA * (at + 1)] = field

    pick = hot(iota((block, rows), 0) == slot[...] - step * block)
    moved = dot(pick, unit[...])
    senders = block // BLOCK
    end = ends[pl.ds(pl.multiple_of(step * senders, 8), senders), :]
    last = iota((8, width), 0) == 7
    pieces = []
    for at in range(block // BLOCK):
        top = at * BLOCK
        pieces.append(moved[top : top + 16, :])
        pieces.append(jnp.where(last, end[at : at + 1, :], moved[top + 16 : top + 24, :]))
    out[...] = jnp.concatenate(pieces, 0).astype(BF16)


def gather(spot, count, taken, rows, fields):
    pick = hot(iota((count, CHUNK), 0) == spot)
    return dot(pick, taken[rows, :]), dot(pick, fields, COLS)


def load_chunks(source, taken, copied):
    copies = []
    for at in range(taken.shape[0] // CHUNK):
        rows = pl.ds(at * CHUNK, CHUNK)
        copies.append(pltpu.make_async_copy(source.at[rows, :], taken.at[rows, :], copied.at[at]))
        copies[-1].start()
    return copies


def read_kernel(source, spill, spots, fields, info, taken, pile, ends, strange, copied):
    chunks = taken.shape[0] // CHUNK
    width = taken.shape[1]
    copies = load_chunks(source, taken, copied)
    upto = hot(iota((CHUNK, CHUNK), 0) <= iota((CHUNK, CHUNK), 1))
    place = iota((EXTRA, CHUNK), 1)
    sender = jnp.zeros(place.shape, I32)
    for at in range(1, 8):
        sender = sender + jnp.where(place >= at * BLOCK, 1, 0)
    spread = hot(place - sender * BLOCK == iota((EXTRA, CHUNK), 0))
    mine = (iota((64, CHUNK), 0) & 7) == sender[:64, :]
    spots[...] = jnp.full(spots.shape, -1, I32)
    for copy in copies:
        copy.wait()
    for at in range(CHIPS):
        last = at * BLOCK + SEATS
        top = (last // 16) * 16
        tile = taken[top : top + 16, :].astype(F32)
        ends[at : at + 1, :] = tile[last - top : last - top + 1, :]
    late = jnp.max(ends[:, EXTRA - 1 : EXTRA])
    stack = [
        ends[8 * at : 8 * at + 8, EXTRA * f : EXTRA * (f + 1)]
        for at in range(chunks)
        for f in range(8)
    ]
    wide = dot(jnp.concatenate(stack, 0).astype(BF16), spread)
    natives, foreigns = [], []
    for at in range(chunks):
        part = jnp.where(mine, wide[64 * at : 64 * at + 64, :], 0.0)
        found = [jnp.sum(part[8 * f : 8 * f + 8, :], 0, keepdims=True) for f in range(8)]
        table = jnp.concatenate(found + [jnp.zeros((EXTRA - 8, CHUNK), F32)], 0)
        fields[at] = table.astype(BF16)
        natives.append(found[4] - found[5])
        foreigns.append(found[5])
    both = jnp.concatenate(natives + foreigns, 0)
    running = dot(both.astype(BF16), upto).astype(I32)
    start, start_strange = jnp.int32(0), jnp.int32(0)
    for at in range(chunks):
        native, foreign = natives[at], foreigns[at]
        spots[at : at + 1, 0:CHUNK] = jnp.where(
            native > 0, running[at : at + 1, :] + (start - 1), -1
        )
        strange[at : at + 1, :] = jnp.where(
            foreign > 0, running[chunks + at : chunks + at + 1, :] + (start_strange - 1), -1
        )
        info[at] = (start >> 4) << 4
        start = start + jnp.sum(native).astype(I32)
        start_strange = start_strange + jnp.sum(foreign).astype(I32)
    info[16] = (start + TILE - 1) // TILE
    info[17] = jnp.where((start_strange > SPILL) | (late > 0), 1, 0)
    info[18] = start
    pile[...] = jnp.zeros(pile.shape, F32)

    @pl.when(start_strange > 0)
    def _():
        def step(at, carry):
            rows = pl.ds(pl.multiple_of(at * CHUNK, CHUNK), CHUNK)
            rows_in, side = gather(strange[pl.ds(at, 1), :], SPILL, taken, rows, fields[at])
            pile[:, :width] += rows_in
            pile[:, width:] += side
            return carry

        lax.fori_loop(0, chunks, step, 0)

    spill[...] = pile[...].astype(BF16)


def pack_kernel(info, source, spots, fields, packed, taken, room, copied, placed):
    chunks = taken.shape[0] // CHUNK
    width = taken.shape[1]
    copies = load_chunks(source, taken, copied)
    tiles = info[16]
    room[0:16, :] = jnp.zeros((16, room.shape[1]), BF16)
    first = jnp.int32(0)
    done = jnp.int32(0)

    def put(at):
        rows = pl.ds(pl.multiple_of(at * TILE, TILE), TILE)
        return pltpu.make_async_copy(room.at[rows, :], packed.at[rows, :], placed.at[at])

    for at in range(chunks):
        first = pl.multiple_of(jnp.minimum(info[at], ROOM - WINDOW), 16)
        spot = spots[at : at + 1, 0:CHUNK] - first
        copies[at].wait()
        rows_in, side = gather(spot, WINDOW, taken, pl.ds(at * CHUNK, CHUNK), fields[at])
        here = pl.ds(first, 16)
        after = pl.ds(pl.multiple_of(first + 16, 16), WINDOW - 16)
        for span, value in ((pl.ds(0, width), rows_in), (pl.ds(width, EXTRA), side)):
            room[here, span] = (room[here, span].astype(F32) + value[:16]).astype(BF16)
            room[after, span] = value[16:].astype(BF16)
        if at + 1 < chunks:
            filled = info[at + 1] // TILE
            pl.when(filled > done)(put(done).start)
            done = filled

    def clear(at, carry):
        room[pl.ds(pl.multiple_of(at * 16, 16), 16), :] = jnp.zeros((16, room.shape[1]), BF16)
        return carry

    lax.fori_loop((first + WINDOW) // 16, tiles * (TILE // 16), clear, 0)
    for at in range(TILES):
        pl.when((at >= done) & (at < tiles))(put(at).start)
    for at in range(TILES):
        pl.when(at < tiles)(put(at).wait)


def append_kernel(info, near, packed_in, packed, info_out, window, blank, sems):
    for at in range(20):
        info_out[at] = info[at]
    total, tiles = info[18], info[16]
    count = jnp.sum(near[:, packed.shape[1] - EXTRA :].astype(F32)[:, 4:5]).astype(I32)
    first = (total >> 4) << 4
    fits = (total + count <= PACKED) & (first + SPILL + 16 <= PACKED)

    @pl.when((count > 0) & jnp.logical_not(fits))
    def _():
        info_out[17] = 1

    @pl.when((count > 0) & fits)
    def _():
        more = (total + count + TILE - 1) // TILE
        info_out[16] = more
        begin = pl.multiple_of(first, 16)
        head = pltpu.make_async_copy(
            packed.at[pl.ds(begin, 16), :], window.at[pl.ds(0, 16), :], sems.at[0]
        )
        head.start()

        @pl.when(more > tiles)
        def _():
            blank[...] = jnp.zeros(blank.shape, BF16)

        shift = iota((SPILL + 16, SPILL), 0) - iota((SPILL + 16, SPILL), 1)
        moved = dot(hot(shift == total - first), near[...])
        head.wait()
        keep = iota((16, packed.shape[1]), 0) < total - first
        window[0:16, :] = jnp.where(
            keep, window[0:16, :].astype(F32), moved[:16]
        ).astype(BF16)
        window[16:, :] = moved[16:].astype(BF16)

        @pl.when(more > tiles)
        def _():
            at = pl.multiple_of(tiles * TILE, TILE)
            clear = pltpu.make_async_copy(blank, packed.at[pl.ds(at, TILE), :], sems.at[1])
            clear.start()
            clear.wait()

        put = pltpu.make_async_copy(
            window, packed.at[pl.ds(begin, SPILL + 16), :], sems.at[2]
        )
        put.start()
        put.wait()


def score(queries, query_tiles, keys, key_tiles, best, marks, bounds):
    width = queries.shape[1] - EXTRA
    fields = fields_of(queries[:, width:]).astype(I32)
    bounds[0:1, :] = (fields[1:2, :] * 128 + fields[0:1, :] + fields[4:5, :]) * 65536
    bounds[1:2, :] = fields[2:3, :] * 256 + fields[3:4, :] + LOWEST

    def mark_step(at, carry):
        span = pl.ds(pl.multiple_of(at * TILE, TILE), TILE)
        side = keys[span, width:].astype(F32).astype(I32)
        mark = (side[:, 1:2] * 128 + side[:, 0:1] + side[:, 4:5]) * 65536
        mark = mark + side[:, 2:3] * 256 + side[:, 3:4] + LOWEST
        marks[span, :] = jnp.broadcast_to(mark, (TILE, EXTRA))
        return carry

    lax.fori_loop(0, key_tiles, mark_step, 0)

    def against(size):
        def query_step(at, carry):
            rows = pl.ds(pl.multiple_of(at * TILE, TILE), TILE)
            mark = marks[:size, :]
            mark = jnp.concatenate([mark] * (TILE // EXTRA), 1)
            scores = dot(keys[:size, :width], queries[rows, :width], COLS)
            earlier = mark - bounds[0:1, rows] < bounds[1:2, rows]
            found = jnp.max(jnp.where(earlier, scores, -1.0), 0, keepdims=True)
            best[:, rows] = jnp.maximum(best[:, rows], found)
            return carry

        lax.fori_loop(0, query_tiles, query_step, 0)

    if isinstance(key_tiles, int):
        against(key_tiles * TILE)
        return
    for tiles in range(1, keys.shape[0] // TILE + 1):
        pl.when(key_tiles == tiles)(functools.partial(against, tiles * TILE))


def fetch(source, target, tiles, sems):
    for at in range(TILES):
        rows = pl.ds(at * TILE, TILE)
        copy = pltpu.make_async_copy(source.at[rows, :], target.at[rows, :], sems.at[at])
        pl.when(at < tiles)(copy.start)


def fetched(source, target, tiles, sems):
    for at in range(TILES):
        rows = pl.ds(at * TILE, TILE)
        copy = pltpu.make_async_copy(source.at[rows, :], target.at[rows, :], sems.at[at])
        pl.when(at < tiles)(copy.wait)


def own_kernel(info, packed, best, mine, marks, bounds, sems):
    fetch(packed, mine, info[16], sems)
    best[...] = jnp.full(best.shape, -1.0, F32)
    fetched(packed, mine, info[16], sems)
    score(mine, info[16], mine, info[16], best, marks, bounds)


def other_kernel(
    info, other_info, packed, other, near, best_in, spots, back,
    mine, theirs, best, split, marks, bounds, sems, other_sems,
):
    tiles, other_tiles = info[16], other_info[16]
    fetch(packed, mine, tiles, sems)
    fetch(other, theirs, other_tiles, other_sems)
    best[:, :PACKED] = best_in[...]
    best[:, PACKED:] = jnp.full((1, best.shape[1] - PACKED), -1.0, F32)
    fetched(packed, mine, tiles, sems)
    fetched(other, theirs, other_tiles, other_sems)
    score(mine, tiles, theirs, other_tiles, best, marks, bounds)
    flag = jnp.maximum(info[17], other_info[17]).astype(F32)
    reach = 384
    row = iota((16, best.shape[1]), 0)
    stack = jnp.zeros(row.shape, F32)
    for at, part in enumerate(thirds(best[...])):
        stack = jnp.where(row == at, part.astype(F32), stack)
    split[...] = stack.astype(BF16)

    def stacked(first, count):
        return split[:, pl.ds(pl.multiple_of(first, 128), count)]

    sub, lane = iota((8, EXTRA), 0), iota((8, EXTRA), 1)
    lower = (lane >= sub * BLOCK) & (lane < sub * BLOCK + BLOCK)
    upper = (lane + EXTRA >= sub * BLOCK) & (lane + EXTRA < sub * BLOCK + BLOCK)
    empty = jnp.where(((lane - sub * BLOCK) & (EXTRA - 1)) >= 64, flag, 0.0)
    for step in range(CHIPS // 8):
        first = (info[step] >> 7) << 7
        pick = hot(iota((reach, 2 * EXTRA), 0) + first == spots[step : step + 1, :])
        value = jnp.sum(dot(stacked(first, reach), pick), 0, keepdims=True)
        line = jnp.where(upper, value[:, EXTRA:], jnp.where(lower, value[:, :EXTRA], empty))
        back[8 * step : 8 * step + 8, :] = line
    fields = fields_of(near[:, mine.shape[1] - EXTRA :]).astype(I32)
    filled = fields[4:5, :] > 0

    @pl.when(jnp.max(fields[4:5, :].astype(F32)) > 0)
    def _():
        total = info[18]
        first = (total >> 7) << 7
        shift = iota((2 * EXTRA, SPILL), 0) - iota((2 * EXTRA, SPILL), 1)
        pick = hot(shift == total - first)
        value = jnp.sum(dot(stacked(first, 2 * EXTRA), pick), 0, keepdims=True)
        source = (iota((CHIPS, SPILL), 0) == fields[7:8, :]) & filled
        line = hot(iota((EXTRA, SPILL), 0) == fields[6:7, :])
        total = back[...]
        for part in thirds(value):
            held = jnp.where(source, part.astype(F32), 0.0).astype(BF16)
            total = total + dot(held, line, COLS)
        back[...] = total


def home_kernel(me, back, place, highest, flag):
    rows = place.shape[1]
    base = (me[0] & 7) * BLOCK
    pick = hot(iota((CHIPS, rows), 0) == place[0:1, :])
    lines = back[...]
    total = jnp.zeros((EXTRA, rows), F32)
    for part in thirds(lines):
        total = total + dot(part, pick, (((0,), (0,)), ((), ())))
    mine = iota((EXTRA, rows), 0) == ((place[1:2, :] + base) & (EXTRA - 1))
    highest[...] = jnp.sum(jnp.where(mine, total, 0.0), 0, keepdims=True)
    marks = ((iota(lines.shape, 1) - base) & (EXTRA - 1)) >= 64
    flag[0] = jnp.max(jnp.where(marks, lines, 0.0)).astype(I32)


def whole(shape):
    return pl.BlockSpec(shape, lambda *_: (0,) * len(shape))


SCALARS = pl.BlockSpec(memory_space=pltpu.SMEM)
PLACED = pl.BlockSpec(memory_space=pl.ANY)

LESS = pltpu.CompilerParams(vmem_limit_bytes=28 * 1024 * 1024)


def array(shape, dtype):
    return jax.ShapeDtypeStruct(shape, dtype)


def exchange(x):
    return lax.all_to_all(
        x, BOTH, split_axis=0, concat_axis=0, tiled=True, axis_index_groups=GROUPS
    )


def direct(embed, owner, local_id, rank):
    rows, width = embed.shape
    full = width + EXTRA
    lines = CHIPS * BLOCK
    chunks = lines // CHUNK
    me = ((lax.axis_index("grp") >> 1) * 8 + lax.axis_index("blk")).astype(I32).reshape(1)
    sent, place = pl.pallas_call(
        send_kernel,
        grid=(chunks // 2,),
        in_specs=[SCALARS, whole((rows, width))] + [whole((1, rows))] * 3,
        out_specs=[pl.BlockSpec((2 * CHUNK, width), lambda i: (i, 0)), whole((8, rows))],
        out_shape=[array((lines, width), BF16), array((8, rows), I32)],
        scratch_shapes=[
            pltpu.VMEM((rows, width), BF16),
            pltpu.VMEM((1, rows), I32),
            pltpu.VMEM((CHIPS, width), F32),
        ],
        compiler_params=LESS,
        name="send",
    )(me, embed, owner.reshape(1, rows), local_id.reshape(1, rows), rank.reshape(1, rows))
    taken = exchange(sent.reshape(CHIPS, BLOCK, width)).reshape(lines, width)
    spill, spots, fields, info = pl.pallas_call(
        read_kernel,
        in_specs=[PLACED],
        out_specs=[
            whole((SPILL, full)),
            whole((chunks, 2 * EXTRA)),
            whole((chunks, EXTRA, CHUNK)),
            SCALARS,
        ],
        out_shape=[
            array((SPILL, full), BF16),
            array((chunks, 2 * EXTRA), I32),
            array((chunks, EXTRA, CHUNK), BF16),
            array((32,), I32),
        ],
        scratch_shapes=[
            pltpu.VMEM((lines, width), BF16),
            pltpu.VMEM((SPILL, full), F32),
            pltpu.VMEM((CHIPS, width), F32),
            pltpu.VMEM((chunks, CHUNK), I32),
            pltpu.SemaphoreType.DMA((chunks,)),
        ],
        compiler_params=LESS,
        name="read",
    )(taken)
    near = lax.ppermute(spill, BOTH, [(i, i ^ 1) for i in range(2 * CHIPS)])
    packed = pl.pallas_call(
        pack_kernel,
        in_specs=[SCALARS, PLACED, whole((chunks, 2 * EXTRA)), whole((chunks, EXTRA, CHUNK))],
        out_specs=PLACED,
        out_shape=array((PACKED, full), BF16),
        scratch_shapes=[
            pltpu.VMEM((lines, width), BF16),
            pltpu.VMEM((ROOM, full), BF16),
            pltpu.SemaphoreType.DMA((chunks,)),
            pltpu.SemaphoreType.DMA((TILES,)),
        ],
        compiler_params=LESS,
        cost_estimate=pl.CostEstimate(
            flops=2 * lines * WINDOW * full, bytes_accessed=4 * lines * full, transcendentals=0
        ),
        name="pack",
    )(info, taken, spots, fields)
    packed, info = pl.pallas_call(
        append_kernel,
        in_specs=[SCALARS, whole((SPILL, full)), PLACED],
        out_specs=[PLACED, SCALARS],
        out_shape=[array((PACKED, full), BF16), array((32,), I32)],
        scratch_shapes=[
            pltpu.VMEM((SPILL + 16, full), BF16),
            pltpu.VMEM((TILE, full), BF16),
            pltpu.SemaphoreType.DMA((3,)),
        ],
        input_output_aliases={2: 0},
        compiler_params=LESS,
        name="append",
    )(info, near, packed)
    swap = [(i, i ^ 1) for i in range(16)]
    other_info = lax.ppermute(info, "grp", swap)
    other = lax.ppermute(packed, "grp", swap)
    best = pl.pallas_call(
        own_kernel,
        in_specs=[SCALARS, PLACED],
        out_specs=whole((1, PACKED)),
        out_shape=array((1, PACKED), F32),
        scratch_shapes=[
            pltpu.VMEM((PACKED, full), BF16),
            pltpu.VMEM((PACKED, EXTRA), I32),
            pltpu.VMEM((8, PACKED), I32),
            pltpu.SemaphoreType.DMA((TILES,)),
        ],
        compiler_params=LESS,
        cost_estimate=pl.CostEstimate(
            flops=2 * 1024 * 1024 * width, bytes_accessed=2 * PACKED * full, transcendentals=0
        ),
        name="own",
    )(info, packed)
    back = pl.pallas_call(
        other_kernel,
        in_specs=[SCALARS, SCALARS, PLACED, PLACED]
        + [whole((SPILL, full)), whole((1, PACKED)), whole((chunks, 2 * EXTRA))],
        out_specs=whole((CHIPS, EXTRA)),
        out_shape=array((CHIPS, EXTRA), F32),
        scratch_shapes=[
            pltpu.VMEM((PACKED, full), BF16),
            pltpu.VMEM((PACKED, full), BF16),
            pltpu.VMEM((1, PACKED + 2 * TILE), F32),
            pltpu.VMEM((16, PACKED + 2 * TILE), BF16),
            pltpu.VMEM((PACKED, EXTRA), I32),
            pltpu.VMEM((8, PACKED), I32),
            pltpu.SemaphoreType.DMA((TILES,)),
            pltpu.SemaphoreType.DMA((TILES,)),
        ],
        compiler_params=LESS,
        name="other",
    )(info, other_info, packed, other, near, best, spots)
    home = exchange(back)
    highest, flag = pl.pallas_call(
        home_kernel,
        in_specs=[SCALARS, whole((CHIPS, EXTRA)), whole((8, rows))],
        out_specs=[whole((1, rows)), SCALARS],
        out_shape=[array((1, rows), F32), array((1,), I32)],
        compiler_params=LESS,
        name="home",
    )(me, home, place)
    return highest.reshape(rows), flag[0]


def group_kernel(queries, keys, best_in, best, marks, bounds):
    best[...] = best_in[...]
    tiles = keys.shape[0] // TILE
    score(queries, tiles, keys, tiles, best, marks, bounds)


def by_group(embed, owner, local_id, rank):
    n_group, n_block = lax.axis_size("grp"), lax.axis_size("blk")
    row_count, columns = embed.shape
    capacity = row_count // 8
    width = n_group * capacity
    full = columns + EXTRA
    wide = embed.astype(F32)
    unit = (wide * lax.rsqrt(jnp.sum(wide * wide, 1, keepdims=True) + EPS)).astype(BF16)
    target = owner[:, 0]
    onehot = (target[:, None] == jnp.arange(n_group, dtype=I32)[None, :]).astype(I32)
    position = jnp.sum((jnp.cumsum(onehot, 0) - 1) * onehot, 1)
    slot_index = target * capacity + position
    fields = jnp.stack([local_id, target, rank >> 8, rank & 255, jnp.ones_like(rank)], 1)
    fields = jnp.pad(fields, ((0, 0), (0, EXTRA - 5))).astype(BF16)
    sent = jnp.zeros((width, full), BF16).at[slot_index].set(jnp.concatenate([unit, fields], 1))
    routed = lax.all_to_all(
        sent.reshape(n_group, capacity, full), "grp", split_axis=0, concat_axis=0, tiled=True
    ).reshape(width, full)
    best = jnp.full((1, width), -1.0, F32)
    for by in range(n_block):
        turn = [(i, (i + by) % n_block) for i in range(n_block)]
        best = pl.pallas_call(
            group_kernel,
            in_specs=[whole((width, full))] * 2 + [whole((1, width))],
            out_specs=whole((1, width)),
            out_shape=array((1, width), F32),
            scratch_shapes=[pltpu.VMEM((width, EXTRA), I32), pltpu.VMEM((8, width), I32)],
            compiler_params=LESS,
            name="group",
        )(routed, lax.ppermute(routed, "blk", turn) if by else routed, best)
    home = lax.all_to_all(
        best.reshape(n_group, capacity), "grp", split_axis=0, concat_axis=0, tiled=True
    )
    return home.reshape(width)[slot_index]


def per_device(embed, owner, local_id, rank):
    highest, flag = direct(embed, owner, local_id, rank)
    return lax.cond(
        flag > 0, lambda: by_group(embed, owner, local_id, rank), lambda: highest
    )


def solution(mesh):
    in_specs = (
        P(("grp", "blk"), None),
        P(("grp", "blk"), None),
        P(("grp", "blk")),
        P(("grp", "blk")),
    )
    out_specs = P(("grp", "blk"))
    return jax.shard_map(
        per_device, mesh=mesh, in_specs=in_specs, out_specs=out_specs, check_vma=False
    )
```

```python
import functools

import jax
import jax.numpy as jnp
from jax import lax
from jax.experimental import pallas as pl
from jax.experimental.pallas import tpu as pltpu
from jax.sharding import PartitionSpec as P

EPS = 1e-06
BOTH = ("grp", "blk")
CHIPS = 64
BLOCK = 24
SEATS = 23
EXTRA = 128
CHUNK = 8 * BLOCK
WINDOW = CHUNK + 16
TILE = 256
TILES = 6
PACKED = TILE * TILES
SPILL = 128
GROUPS = [[g * 8 + b for g in range(core, 16, 2) for b in range(8)] for core in range(2)]
COLS = (((1,), (1,)), ((), ()))
F32 = jnp.float32
BF16 = jnp.bfloat16
I32 = jnp.int32
LOWEST = -(2**31)


def iota(shape, dim):
    return lax.broadcasted_iota(I32, shape, dim)


def hot(mask):
    return jnp.where(mask, jnp.float32(1), jnp.float32(0)).astype(BF16)


def dot(a, b, dims=(((1,), (0,)), ((), ()))):
    return lax.dot_general(a, b, dims, preferred_element_type=F32)


def thirds(x):
    high = x.astype(BF16)
    rest = x - high.astype(F32)
    middle = rest.astype(BF16)
    return high, middle, (rest - middle.astype(F32)).astype(BF16)


def fields_of(extra):
    return dot(hot(iota((16, EXTRA), 0) == iota((16, EXTRA), 1)), extra, COLS)


def send_kernel(me, embed, owner, local, rank, out, place, unit, slot, ends):
    rows, width = embed.shape
    step = pl.program_id(0)
    block = out.shape[0]

    @pl.when(step == 0)
    def _():
        wide = embed[...].astype(F32)
        scale = lax.rsqrt(jnp.sum(wide * wide, 1, keepdims=True) + EPS)
        unit[...] = (wide * scale).astype(BF16)
        group, number, order = owner[...], local[...], rank[...]
        chip = (number & (CHIPS - 1)) ^ (group * 4)
        own = iota((CHIPS, rows), 0) == chip
        near = iota((CHIPS, rows), 0) == (chip ^ 1)
        before = hot(iota((rows, rows), 0) < iota((rows, rows), 1))
        ahead = dot(hot(own), before)
        count = jnp.sum(jnp.where(own, 1.0, 0.0), 1, keepdims=True)
        position = jnp.sum(jnp.where(own, ahead, 0.0), 0, keepdims=True).astype(I32)
        beside = jnp.sum(jnp.where(near, count, 0.0), 0, keepdims=True).astype(I32)
        spilled = position >= SEATS
        seat = jnp.where(spilled, beside + position - SEATS, position)
        late = jnp.max(jnp.where(seat >= SEATS, 1.0, 0.0), 1, keepdims=True)
        goes = jnp.where(seat < SEATS, jnp.where(spilled, chip ^ 1, chip), -1)
        line = seat + jnp.where(spilled, 32, 0)
        slot[...] = jnp.where(goes >= 0, goes * BLOCK + seat, -1)
        place[...] = jnp.where(iota(place.shape, 0) == 0, chip, line)
        entries = (
            number,
            group,
            order >> 8,
            order & 255,
            jnp.ones_like(order),
            jnp.where(spilled, 1, 0),
            (line + (me[0] & 7) * BLOCK) & (EXTRA - 1),
            jnp.broadcast_to(me[0], order.shape),
        )
        there = iota((CHIPS, rows), 0) == goes
        tables = [jnp.where(there, entry.astype(F32), 0.0).astype(BF16) for entry in entries]
        seats = hot(iota((EXTRA, rows), 0) == seat)
        fields = dot(jnp.concatenate(tables, 0), seats, COLS)
        lane = iota((CHIPS, EXTRA), 1)
        for at in range(len(entries)):
            field = fields[CHIPS * at : CHIPS * (at + 1), :]
            if at == 0:
                field = jnp.where(lane == EXTRA - 1, late, field)
            ends[:, EXTRA * at : EXTRA * (at + 1)] = field

    pick = hot(iota((block, rows), 0) == slot[...] - step * block)
    moved = dot(pick, unit[...])
    senders = block // BLOCK
    end = ends[pl.ds(pl.multiple_of(step * senders, 8), senders), :]
    last = iota((8, width), 0) == 7
    pieces = []
    for at in range(block // BLOCK):
        top = at * BLOCK
        pieces.append(moved[top : top + 16, :])
        pieces.append(jnp.where(last, end[at : at + 1, :], moved[top + 16 : top + 24, :]))
    out[...] = jnp.concatenate(pieces, 0).astype(BF16)


def gather(spot, count, taken, rows, fields):
    pick = hot(iota((count, CHUNK), 0) == spot)
    return dot(pick, taken[rows, :]), dot(pick, fields, COLS)


def read_kernel(taken, spill, spots, fields, info, pile, ends, strange):
    chunks = taken.shape[0] // CHUNK
    width = taken.shape[1]
    upto = hot(iota((CHUNK, CHUNK), 0) <= iota((CHUNK, CHUNK), 1))
    place = iota((EXTRA, CHUNK), 1)
    sender = jnp.zeros(place.shape, I32)
    for at in range(1, 8):
        sender = sender + jnp.where(place >= at * BLOCK, 1, 0)
    spread = hot(place - sender * BLOCK == iota((EXTRA, CHUNK), 0))
    mine = (iota((64, CHUNK), 0) & 7) == sender[:64, :]
    spots[...] = jnp.full(spots.shape, -1, I32)
    for at in range(CHIPS):
        last = at * BLOCK + SEATS
        top = (last // 16) * 16
        tile = taken[top : top + 16, :].astype(F32)
        ends[at : at + 1, :] = tile[last - top : last - top + 1, :]
    late = jnp.max(ends[:, EXTRA - 1 : EXTRA])
    stack = [
        ends[8 * at : 8 * at + 8, EXTRA * f : EXTRA * (f + 1)]
        for at in range(chunks)
        for f in range(8)
    ]
    wide = dot(jnp.concatenate(stack, 0).astype(BF16), spread)
    natives, foreigns = [], []
    for at in range(chunks):
        part = jnp.where(mine, wide[64 * at : 64 * at + 64, :], 0.0)
        found = [jnp.sum(part[8 * f : 8 * f + 8, :], 0, keepdims=True) for f in range(8)]
        table = jnp.concatenate(found + [jnp.zeros((EXTRA - 8, CHUNK), F32)], 0)
        fields[at] = table.astype(BF16)
        natives.append(found[4] - found[5])
        foreigns.append(found[5])
    both = jnp.concatenate(natives + foreigns, 0)
    running = dot(both.astype(BF16), upto).astype(I32)
    start, start_strange = jnp.int32(0), jnp.int32(0)
    for at in range(chunks):
        native, foreign = natives[at], foreigns[at]
        spots[at : at + 1, 0:CHUNK] = jnp.where(
            native > 0, running[at : at + 1, :] + (start - 1), -1
        )
        strange[at : at + 1, :] = jnp.where(
            foreign > 0, running[chunks + at : chunks + at + 1, :] + (start_strange - 1), -1
        )
        info[at] = (start >> 4) << 4
        start = start + jnp.sum(native).astype(I32)
        start_strange = start_strange + jnp.sum(foreign).astype(I32)
    info[16] = (start + TILE - 1) // TILE
    info[17] = jnp.where((start_strange > SPILL) | (late > 0), 1, 0)
    info[18] = start
    pile[...] = jnp.zeros(pile.shape, F32)

    @pl.when(start_strange > 0)
    def _():
        def step(at, carry):
            rows = pl.ds(pl.multiple_of(at * CHUNK, CHUNK), CHUNK)
            rows_in, side = gather(strange[pl.ds(at, 1), :], SPILL, taken, rows, fields[at])
            pile[:, :width] += rows_in
            pile[:, width:] += side
            return carry

        lax.fori_loop(0, chunks, step, 0)

    spill[...] = pile[...].astype(BF16)


def pack_kernel(info, taken, spots, fields, packed):
    width = taken.shape[1]
    tiles = info[16]
    packed[0:16, :] = jnp.zeros((16, packed.shape[1]), BF16)
    first = jnp.int32(0)
    for at in range(taken.shape[0] // CHUNK):
        first = pl.multiple_of(jnp.minimum(info[at], PACKED - WINDOW), 16)
        spot = spots[at : at + 1, 0:CHUNK] - first
        rows_in, side = gather(spot, WINDOW, taken, pl.ds(at * CHUNK, CHUNK), fields[at])
        here = pl.ds(first, 16)
        after = pl.ds(pl.multiple_of(first + 16, 16), WINDOW - 16)
        for span, value in ((pl.ds(0, width), rows_in), (pl.ds(width, EXTRA), side)):
            packed[here, span] = (packed[here, span].astype(F32) + value[:16]).astype(BF16)
            packed[after, span] = value[16:].astype(BF16)
    clear(packed, (first + WINDOW) // 16, tiles * (TILE // 16))


def clear(rows, low, high):
    def step(at, carry):
        rows[pl.ds(pl.multiple_of(at * 16, 16), 16), :] = jnp.zeros((16, rows.shape[1]), BF16)
        return carry

    lax.fori_loop(low, high, step, 0)


def append_kernel(info, near, packed_in, packed, info_out):
    for at in range(20):
        info_out[at] = info[at]
    total, tiles = info[18], info[16]
    count = jnp.sum(near[:, packed.shape[1] - EXTRA :].astype(F32)[:, 4:5]).astype(I32)
    first = (total >> 4) << 4
    fits = (total + count <= PACKED) & (first + SPILL + 16 <= PACKED)

    @pl.when((count > 0) & jnp.logical_not(fits))
    def _():
        info_out[17] = 1

    @pl.when((count > 0) & fits)
    def _():
        more = (total + count + TILE - 1) // TILE
        info_out[16] = more
        clear(packed, tiles * (TILE // 16), more * (TILE // 16))
        shift = iota((SPILL + 16, SPILL), 0) - iota((SPILL + 16, SPILL), 1)
        moved = dot(hot(shift == total - first), near[...])
        keep = iota((16, packed.shape[1]), 0) < total - first
        here = pl.ds(pl.multiple_of(first, 16), 16)
        after = pl.ds(pl.multiple_of(first + 16, 16), SPILL)
        held = packed[here, :].astype(F32)
        packed[here, :] = jnp.where(keep, held, moved[:16]).astype(BF16)
        packed[after, :] = moved[16:].astype(BF16)


def score(queries, query_tiles, keys, key_tiles, best, marks, bounds):
    width = queries.shape[1] - EXTRA
    fields = fields_of(queries[:, width:]).astype(I32)
    bounds[0:1, :] = (fields[1:2, :] * 128 + fields[0:1, :] + fields[4:5, :]) * 65536
    bounds[1:2, :] = fields[2:3, :] * 256 + fields[3:4, :] + LOWEST

    def mark_step(at, carry):
        span = pl.ds(pl.multiple_of(at * TILE, TILE), TILE)
        side = keys[span, width:].astype(F32).astype(I32)
        mark = (side[:, 1:2] * 128 + side[:, 0:1] + side[:, 4:5]) * 65536
        mark = mark + side[:, 2:3] * 256 + side[:, 3:4] + LOWEST
        marks[span, :] = jnp.broadcast_to(mark, (TILE, EXTRA))
        return carry

    lax.fori_loop(0, key_tiles, mark_step, 0)

    def against(size):
        def query_step(at, carry):
            rows = pl.ds(pl.multiple_of(at * TILE, TILE), TILE)
            mark = marks[:size, :]
            mark = jnp.concatenate([mark] * (TILE // EXTRA), 1)
            scores = dot(keys[:size, :width], queries[rows, :width], COLS)
            earlier = mark - bounds[0:1, rows] < bounds[1:2, rows]
            found = jnp.max(jnp.where(earlier, scores, -1.0), 0, keepdims=True)
            best[:, rows] = jnp.maximum(best[:, rows], found)
            return carry

        lax.fori_loop(0, query_tiles, query_step, 0)

    if isinstance(key_tiles, int):
        against(key_tiles * TILE)
        return
    for tiles in range(1, keys.shape[0] // TILE + 1):
        pl.when(key_tiles == tiles)(functools.partial(against, tiles * TILE))


def own_kernel(info, packed, best, marks, bounds):
    best[...] = jnp.full(best.shape, -1.0, F32)
    score(packed, info[16], packed, info[16], best, marks, bounds)


def other_kernel(
    info, other_info, mine, theirs, near, best_in, spots, back, best, split, marks, bounds
):
    best[:, :PACKED] = best_in[...]
    best[:, PACKED:] = jnp.full((1, best.shape[1] - PACKED), -1.0, F32)
    score(mine, info[16], theirs, other_info[16], best, marks, bounds)
    flag = jnp.maximum(info[17], other_info[17]).astype(F32)
    reach = 384
    row = iota((16, best.shape[1]), 0)
    stack = jnp.zeros(row.shape, F32)
    for at, part in enumerate(thirds(best[...])):
        stack = jnp.where(row == at, part.astype(F32), stack)
    split[...] = stack.astype(BF16)

    def stacked(first, count):
        return split[:, pl.ds(pl.multiple_of(first, 128), count)]

    sub, lane = iota((8, EXTRA), 0), iota((8, EXTRA), 1)
    lower = (lane >= sub * BLOCK) & (lane < sub * BLOCK + BLOCK)
    upper = (lane + EXTRA >= sub * BLOCK) & (lane + EXTRA < sub * BLOCK + BLOCK)
    empty = jnp.where(((lane - sub * BLOCK) & (EXTRA - 1)) >= 64, flag, 0.0)
    for step in range(CHIPS // 8):
        first = (info[step] >> 7) << 7
        pick = hot(iota((reach, 2 * EXTRA), 0) + first == spots[step : step + 1, :])
        value = jnp.sum(dot(stacked(first, reach), pick), 0, keepdims=True)
        line = jnp.where(upper, value[:, EXTRA:], jnp.where(lower, value[:, :EXTRA], empty))
        back[8 * step : 8 * step + 8, :] = line
    fields = fields_of(near[:, mine.shape[1] - EXTRA :]).astype(I32)
    filled = fields[4:5, :] > 0

    @pl.when(jnp.max(fields[4:5, :].astype(F32)) > 0)
    def _():
        total = info[18]
        first = (total >> 7) << 7
        shift = iota((2 * EXTRA, SPILL), 0) - iota((2 * EXTRA, SPILL), 1)
        pick = hot(shift == total - first)
        value = jnp.sum(dot(stacked(first, 2 * EXTRA), pick), 0, keepdims=True)
        source = (iota((CHIPS, SPILL), 0) == fields[7:8, :]) & filled
        line = hot(iota((EXTRA, SPILL), 0) == fields[6:7, :])
        total = back[...]
        for part in thirds(value):
            held = jnp.where(source, part.astype(F32), 0.0).astype(BF16)
            total = total + dot(held, line, COLS)
        back[...] = total


def home_kernel(me, back, place, highest, flag):
    rows = place.shape[1]
    base = (me[0] & 7) * BLOCK
    pick = hot(iota((CHIPS, rows), 0) == place[0:1, :])
    lines = back[...]
    total = jnp.zeros((EXTRA, rows), F32)
    for part in thirds(lines):
        total = total + dot(part, pick, (((0,), (0,)), ((), ())))
    mine = iota((EXTRA, rows), 0) == ((place[1:2, :] + base) & (EXTRA - 1))
    highest[...] = jnp.sum(jnp.where(mine, total, 0.0), 0, keepdims=True)
    marks = ((iota(lines.shape, 1) - base) & (EXTRA - 1)) >= 64
    flag[0] = jnp.max(jnp.where(marks, lines, 0.0)).astype(I32)


def whole(shape):
    return pl.BlockSpec(shape, lambda *_: (0,) * len(shape))


SCALARS = pl.BlockSpec(memory_space=pltpu.SMEM)
HELD = pl.BlockSpec(memory_space=pltpu.VMEM)

LESS = pltpu.CompilerParams(vmem_limit_bytes=28 * 1024 * 1024)


def held(x):
    return pltpu.with_memory_space_constraint(x, pltpu.VMEM)


def array(shape, dtype):
    return jax.ShapeDtypeStruct(shape, dtype)


def exchange(x):
    return lax.all_to_all(
        x, BOTH, split_axis=0, concat_axis=0, tiled=True, axis_index_groups=GROUPS
    )


def direct(embed, owner, local_id, rank):
    rows, width = embed.shape
    full = width + EXTRA
    lines = CHIPS * BLOCK
    chunks = lines // CHUNK
    me = ((lax.axis_index("grp") >> 1) * 8 + lax.axis_index("blk")).astype(I32).reshape(1)
    sent, place = pl.pallas_call(
        send_kernel,
        grid=(chunks // 2,),
        in_specs=[SCALARS, whole((rows, width))] + [whole((1, rows))] * 3,
        out_specs=[pl.BlockSpec((2 * CHUNK, width), lambda i: (i, 0)), whole((8, rows))],
        out_shape=[array((lines, width), BF16), array((8, rows), I32)],
        scratch_shapes=[
            pltpu.VMEM((rows, width), BF16),
            pltpu.VMEM((1, rows), I32),
            pltpu.VMEM((CHIPS, width), F32),
        ],
        compiler_params=LESS,
        name="send",
    )(me, embed, owner.reshape(1, rows), local_id.reshape(1, rows), rank.reshape(1, rows))
    taken = exchange(sent.reshape(CHIPS, BLOCK, width)).reshape(lines, width)
    spill, spots, fields, info = pl.pallas_call(
        read_kernel,
        in_specs=[HELD],
        out_specs=[HELD, HELD, HELD, SCALARS],
        out_shape=[
            pltpu.VMEM((SPILL, full), BF16),
            pltpu.VMEM((chunks, 2 * EXTRA), I32),
            pltpu.VMEM((chunks, EXTRA, CHUNK), BF16),
            array((32,), I32),
        ],
        scratch_shapes=[
            pltpu.VMEM((SPILL, full), F32),
            pltpu.VMEM((CHIPS, width), F32),
            pltpu.VMEM((chunks, CHUNK), I32),
        ],
        compiler_params=LESS,
        name="read",
    )(held(taken))
    near = lax.ppermute(spill, BOTH, [(i, i ^ 1) for i in range(2 * CHIPS)])
    packed = pl.pallas_call(
        pack_kernel,
        in_specs=[SCALARS, HELD, HELD, HELD],
        out_specs=HELD,
        out_shape=pltpu.VMEM((PACKED, full), BF16),
        compiler_params=LESS,
        cost_estimate=pl.CostEstimate(
            flops=2 * lines * WINDOW * full, bytes_accessed=4 * lines * full, transcendentals=0
        ),
        name="pack",
    )(info, held(taken), held(spots), held(fields))
    packed, info = pl.pallas_call(
        append_kernel,
        in_specs=[SCALARS, HELD, HELD],
        out_specs=[HELD, SCALARS],
        out_shape=[pltpu.VMEM((PACKED, full), BF16), array((32,), I32)],
        input_output_aliases={2: 0},
        compiler_params=LESS,
        name="append",
    )(info, held(near), held(packed))
    swap = [(i, i ^ 1) for i in range(16)]
    other_info = lax.ppermute(info, "grp", swap)
    other = lax.ppermute(packed, "grp", swap)
    best = pl.pallas_call(
        own_kernel,
        in_specs=[SCALARS, HELD],
        out_specs=HELD,
        out_shape=pltpu.VMEM((1, PACKED), F32),
        scratch_shapes=[pltpu.VMEM((PACKED, EXTRA), I32), pltpu.VMEM((8, PACKED), I32)],
        compiler_params=LESS,
        cost_estimate=pl.CostEstimate(
            flops=2 * 1024 * 1024 * width, bytes_accessed=2 * PACKED * full, transcendentals=0
        ),
        name="own",
    )(info, held(packed))
    back = pl.pallas_call(
        other_kernel,
        in_specs=[SCALARS, SCALARS] + [HELD] * 5,
        out_specs=HELD,
        out_shape=pltpu.VMEM((CHIPS, EXTRA), F32),
        scratch_shapes=[
            pltpu.VMEM((1, PACKED + 2 * TILE), F32),
            pltpu.VMEM((16, PACKED + 2 * TILE), BF16),
            pltpu.VMEM((PACKED, EXTRA), I32),
            pltpu.VMEM((8, PACKED), I32),
        ],
        compiler_params=LESS,
        name="other",
    )(info, other_info, held(packed), held(other), held(near), held(best), held(spots))
    home = exchange(back)
    highest, flag = pl.pallas_call(
        home_kernel,
        in_specs=[SCALARS, whole((CHIPS, EXTRA)), whole((8, rows))],
        out_specs=[whole((1, rows)), SCALARS],
        out_shape=[array((1, rows), F32), array((1,), I32)],
        compiler_params=LESS,
        name="home",
    )(me, home, place)
    return highest.reshape(rows), flag[0]


def group_kernel(queries, keys, best_in, best, marks, bounds):
    best[...] = best_in[...]
    tiles = keys.shape[0] // TILE
    score(queries, tiles, keys, tiles, best, marks, bounds)


def by_group(embed, owner, local_id, rank):
    n_group, n_block = lax.axis_size("grp"), lax.axis_size("blk")
    row_count, columns = embed.shape
    capacity = row_count // 8
    width = n_group * capacity
    full = columns + EXTRA
    wide = embed.astype(F32)
    unit = (wide * lax.rsqrt(jnp.sum(wide * wide, 1, keepdims=True) + EPS)).astype(BF16)
    target = owner[:, 0]
    onehot = (target[:, None] == jnp.arange(n_group, dtype=I32)[None, :]).astype(I32)
    position = jnp.sum((jnp.cumsum(onehot, 0) - 1) * onehot, 1)
    slot_index = target * capacity + position
    fields = jnp.stack([local_id, target, rank >> 8, rank & 255, jnp.ones_like(rank)], 1)
    fields = jnp.pad(fields, ((0, 0), (0, EXTRA - 5))).astype(BF16)
    sent = jnp.zeros((width, full), BF16).at[slot_index].set(jnp.concatenate([unit, fields], 1))
    routed = lax.all_to_all(
        sent.reshape(n_group, capacity, full), "grp", split_axis=0, concat_axis=0, tiled=True
    ).reshape(width, full)
    best = jnp.full((1, width), -1.0, F32)
    for by in range(n_block):
        turn = [(i, (i + by) % n_block) for i in range(n_block)]
        best = pl.pallas_call(
            group_kernel,
            in_specs=[whole((width, full))] * 2 + [whole((1, width))],
            out_specs=whole((1, width)),
            out_shape=array((1, width), F32),
            scratch_shapes=[pltpu.VMEM((width, EXTRA), I32), pltpu.VMEM((8, width), I32)],
            compiler_params=LESS,
            name="group",
        )(routed, lax.ppermute(routed, "blk", turn) if by else routed, best)
    home = lax.all_to_all(
        best.reshape(n_group, capacity), "grp", split_axis=0, concat_axis=0, tiled=True
    )
    return home.reshape(width)[slot_index]


def per_device(embed, owner, local_id, rank):
    highest, flag = direct(embed, owner, local_id, rank)
    return lax.cond(
        flag > 0, lambda: by_group(embed, owner, local_id, rank), lambda: highest
    )


def solution(mesh):
    in_specs = (
        P(("grp", "blk"), None),
        P(("grp", "blk"), None),
        P(("grp", "blk")),
        P(("grp", "blk")),
    )
    out_specs = P(("grp", "blk"))
    return jax.shard_map(
        per_device, mesh=mesh, in_specs=in_specs, out_specs=out_specs, check_vma=False
    )
```

```python
import functools

import jax
import jax.numpy as jnp
from jax import lax
from jax.experimental import pallas as pl
from jax.experimental.pallas import tpu as pltpu
from jax.sharding import PartitionSpec as P

EPS = 1e-06
BOTH = ("grp", "blk")
CHIPS = 64
BLOCK = 24
SEATS = 23
EXTRA = 128
CHUNK = 8 * BLOCK
WINDOW = CHUNK + 16
TILE = 256
TILES = 6
PACKED = TILE * TILES
SPILL = 128
GROUPS = [[g * 8 + b for g in range(core, 16, 2) for b in range(8)] for core in range(2)]
COLS = (((1,), (1,)), ((), ()))
F32 = jnp.float32
BF16 = jnp.bfloat16
I32 = jnp.int32
LOWEST = -(2**31)


def iota(shape, dim):
    return lax.broadcasted_iota(I32, shape, dim)


def hot(mask):
    return jnp.where(mask, jnp.float32(1), jnp.float32(0)).astype(BF16)


def dot(a, b, dims=(((1,), (0,)), ((), ()))):
    return lax.dot_general(a, b, dims, preferred_element_type=F32)


def thirds(x):
    high = x.astype(BF16)
    rest = x - high.astype(F32)
    middle = rest.astype(BF16)
    return high, middle, (rest - middle.astype(F32)).astype(BF16)


def fields_of(extra):
    return dot(hot(iota((16, EXTRA), 0) == iota((16, EXTRA), 1)), extra, COLS)


def chip_of(group, number, attempt):
    if attempt == 0:
        return (number >> 1) ^ (group * 4)
    turned = ((number >> 3) | (number << 4)) & (CHIPS - 1)
    return turned ^ (((group * 5 + 2) & 15) * 4)


def send_kernel(attempt, me, embed, owner, local, rank, out, place, unit, slot, ends):
    rows, width = embed.shape
    step = pl.program_id(0)
    block = out.shape[0]

    @pl.when(step == 0)
    def _():
        wide = embed[...].astype(F32)
        scale = lax.rsqrt(jnp.sum(wide * wide, 1, keepdims=True) + EPS)
        unit[...] = (wide * scale).astype(BF16)
        group, number, order = owner[...], local[...], rank[...]
        chip = chip_of(group, number, attempt)
        own = iota((CHIPS, rows), 0) == chip
        near = iota((CHIPS, rows), 0) == (chip ^ 1)
        before = hot(iota((rows, rows), 0) < iota((rows, rows), 1))
        ahead = dot(hot(own), before)
        count = jnp.sum(jnp.where(own, 1.0, 0.0), 1, keepdims=True)
        position = jnp.sum(jnp.where(own, ahead, 0.0), 0, keepdims=True).astype(I32)
        beside = jnp.sum(jnp.where(near, count, 0.0), 0, keepdims=True).astype(I32)
        spilled = position >= SEATS
        seat = jnp.where(spilled, beside + position - SEATS, position)
        late = jnp.max(jnp.where(seat >= SEATS, 1.0, 0.0), 1, keepdims=True)
        goes = jnp.where(seat < SEATS, jnp.where(spilled, chip ^ 1, chip), -1)
        line = seat + jnp.where(spilled, 32, 0)
        slot[...] = jnp.where(goes >= 0, goes * BLOCK + seat, -1)
        place[...] = jnp.where(iota(place.shape, 0) == 0, chip, line)
        entries = (
            number,
            group,
            order >> 8,
            order & 255,
            jnp.ones_like(order),
            jnp.where(spilled, 1, 0),
            (line + (me[0] & 7) * BLOCK) & (EXTRA - 1),
            jnp.broadcast_to(me[0], order.shape),
        )
        there = iota((CHIPS, rows), 0) == goes
        tables = [jnp.where(there, entry.astype(F32), 0.0).astype(BF16) for entry in entries]
        seats = hot(iota((EXTRA, rows), 0) == seat)
        fields = dot(jnp.concatenate(tables, 0), seats, COLS)
        lane = iota((CHIPS, EXTRA), 1)
        for at in range(len(entries)):
            field = fields[CHIPS * at : CHIPS * (at + 1), :]
            if at == 0:
                field = jnp.where(lane == EXTRA - 1, late, field)
            ends[:, EXTRA * at : EXTRA * (at + 1)] = field

    pick = hot(iota((block, rows), 0) == slot[...] - step * block)
    moved = dot(pick, unit[...])
    senders = block // BLOCK
    end = ends[pl.ds(pl.multiple_of(step * senders, 8), senders), :]
    last = iota((8, width), 0) == 7
    pieces = []
    for at in range(block // BLOCK):
        top = at * BLOCK
        pieces.append(moved[top : top + 16, :])
        pieces.append(jnp.where(last, end[at : at + 1, :], moved[top + 16 : top + 24, :]))
    out[...] = jnp.concatenate(pieces, 0).astype(BF16)


def gather(spot, count, taken, rows, fields):
    pick = hot(iota((count, CHUNK), 0) == spot)
    return dot(pick, taken[rows, :]), dot(pick, fields, COLS)


def read_kernel(taken, spill, spots, fields, info, pile, ends, strange):
    chunks = taken.shape[0] // CHUNK
    width = taken.shape[1]
    upto = hot(iota((CHUNK, CHUNK), 0) <= iota((CHUNK, CHUNK), 1))
    place = iota((EXTRA, CHUNK), 1)
    sender = jnp.zeros(place.shape, I32)
    for at in range(1, 8):
        sender = sender + jnp.where(place >= at * BLOCK, 1, 0)
    spread = hot(place - sender * BLOCK == iota((EXTRA, CHUNK), 0))
    mine = (iota((64, CHUNK), 0) & 7) == sender[:64, :]
    spots[...] = jnp.full(spots.shape, -1, I32)
    for at in range(CHIPS):
        last = at * BLOCK + SEATS
        top = (last // 16) * 16
        tile = taken[top : top + 16, :].astype(F32)
        ends[at : at + 1, :] = tile[last - top : last - top + 1, :]
    late = jnp.max(ends[:, EXTRA - 1 : EXTRA])
    stack = [
        ends[8 * at : 8 * at + 8, EXTRA * f : EXTRA * (f + 1)]
        for at in range(chunks)
        for f in range(8)
    ]
    wide = dot(jnp.concatenate(stack, 0).astype(BF16), spread)
    natives, foreigns = [], []
    for at in range(chunks):
        part = jnp.where(mine, wide[64 * at : 64 * at + 64, :], 0.0)
        found = [jnp.sum(part[8 * f : 8 * f + 8, :], 0, keepdims=True) for f in range(8)]
        table = jnp.concatenate(found + [jnp.zeros((EXTRA - 8, CHUNK), F32)], 0)
        fields[at] = table.astype(BF16)
        natives.append(found[4] - found[5])
        foreigns.append(found[5])
    both = jnp.concatenate(natives + foreigns, 0)
    running = dot(both.astype(BF16), upto).astype(I32)
    start, start_strange = jnp.int32(0), jnp.int32(0)
    for at in range(chunks):
        native, foreign = natives[at], foreigns[at]
        spots[at : at + 1, 0:CHUNK] = jnp.where(
            native > 0, running[at : at + 1, :] + (start - 1), -1
        )
        strange[at : at + 1, :] = jnp.where(
            foreign > 0, running[chunks + at : chunks + at + 1, :] + (start_strange - 1), -1
        )
        info[at] = (start >> 4) << 4
        start = start + jnp.sum(native).astype(I32)
        start_strange = start_strange + jnp.sum(foreign).astype(I32)
    info[16] = (start + TILE - 1) // TILE
    info[17] = jnp.where((start_strange > SPILL) | (late > 0), 1, 0)
    info[18] = start
    pile[...] = jnp.zeros(pile.shape, F32)

    @pl.when(start_strange > 0)
    def _():
        def step(at, carry):
            rows = pl.ds(pl.multiple_of(at * CHUNK, CHUNK), CHUNK)
            rows_in, side = gather(strange[pl.ds(at, 1), :], SPILL, taken, rows, fields[at])
            pile[:, :width] += rows_in
            pile[:, width:] += side
            return carry

        lax.fori_loop(0, chunks, step, 0)

    spill[...] = pile[...].astype(BF16)


def pack_kernel(info, taken, spots, fields, packed):
    width = taken.shape[1]
    tiles = info[16]
    packed[0:16, :] = jnp.zeros((16, packed.shape[1]), BF16)
    first = jnp.int32(0)
    for at in range(taken.shape[0] // CHUNK):
        first = pl.multiple_of(jnp.minimum(info[at], PACKED - WINDOW), 16)
        spot = spots[at : at + 1, 0:CHUNK] - first
        rows_in, side = gather(spot, WINDOW, taken, pl.ds(at * CHUNK, CHUNK), fields[at])
        here = pl.ds(first, 16)
        after = pl.ds(pl.multiple_of(first + 16, 16), WINDOW - 16)
        for span, value in ((pl.ds(0, width), rows_in), (pl.ds(width, EXTRA), side)):
            packed[here, span] = (packed[here, span].astype(F32) + value[:16]).astype(BF16)
            packed[after, span] = value[16:].astype(BF16)
    clear(packed, (first + WINDOW) // 16, tiles * (TILE // 16))


def clear(rows, low, high):
    def step(at, carry):
        rows[pl.ds(pl.multiple_of(at * 16, 16), 16), :] = jnp.zeros((16, rows.shape[1]), BF16)
        return carry

    lax.fori_loop(low, high, step, 0)


def append_kernel(info, near, packed_in, packed, info_out):
    for at in range(20):
        info_out[at] = info[at]
    total, tiles = info[18], info[16]
    count = jnp.sum(near[:, packed.shape[1] - EXTRA :].astype(F32)[:, 4:5]).astype(I32)
    begin = jnp.minimum((total >> 4) << 4, PACKED - SPILL - 16)
    fits = total + count <= PACKED

    @pl.when((count > 0) & jnp.logical_not(fits))
    def _():
        info_out[17] = 1

    @pl.when((count > 0) & fits)
    def _():
        more = (total + count + TILE - 1) // TILE
        info_out[16] = more
        clear(packed, tiles * (TILE // 16), more * (TILE // 16))
        shift = iota((SPILL + 16, SPILL), 0) - iota((SPILL + 16, SPILL), 1)
        moved = dot(hot(shift == total - begin), near[...])
        keep = iota(moved.shape, 0) < total - begin
        here = pl.ds(pl.multiple_of(begin, 16), SPILL + 16)
        packed[here, :] = jnp.where(keep, packed[here, :].astype(F32), moved).astype(BF16)


def score(queries, query_tiles, keys, key_tiles, best, marks, bounds):
    width = queries.shape[1] - EXTRA
    fields = fields_of(queries[:, width:]).astype(I32)
    bounds[0:1, :] = (fields[1:2, :] * 128 + fields[0:1, :] + fields[4:5, :]) * 65536
    bounds[1:2, :] = fields[2:3, :] * 256 + fields[3:4, :] + LOWEST

    def mark_step(at, carry):
        span = pl.ds(pl.multiple_of(at * TILE, TILE), TILE)
        side = keys[span, width:].astype(F32).astype(I32)
        mark = (side[:, 1:2] * 128 + side[:, 0:1] + side[:, 4:5]) * 65536
        mark = mark + side[:, 2:3] * 256 + side[:, 3:4] + LOWEST
        marks[span, :] = jnp.broadcast_to(mark, (TILE, EXTRA))
        return carry

    lax.fori_loop(0, key_tiles, mark_step, 0)

    def against(size):
        def query_step(at, carry):
            rows = pl.ds(pl.multiple_of(at * TILE, TILE), TILE)
            mark = marks[:size, :]
            mark = jnp.concatenate([mark] * (TILE // EXTRA), 1)
            scores = dot(keys[:size, :width], queries[rows, :width], COLS)
            earlier = mark - bounds[0:1, rows] < bounds[1:2, rows]
            found = jnp.max(jnp.where(earlier, scores, -1.0), 0, keepdims=True)
            best[:, rows] = jnp.maximum(best[:, rows], found)
            return carry

        lax.fori_loop(0, query_tiles, query_step, 0)

    if isinstance(key_tiles, int):
        against(key_tiles * TILE)
        return
    for tiles in range(1, keys.shape[0] // TILE + 1):
        pl.when(key_tiles == tiles)(functools.partial(against, tiles * TILE))


def own_kernel(info, packed, best, marks, bounds):
    best[...] = jnp.full(best.shape, -1.0, F32)
    score(packed, info[16], packed, info[16], best, marks, bounds)


def other_kernel(
    info, other_info, mine, theirs, near, best_in, spots, back, best, split, marks, bounds
):
    best[:, :PACKED] = best_in[...]
    best[:, PACKED:] = jnp.full((1, best.shape[1] - PACKED), -1.0, F32)
    score(mine, info[16], theirs, other_info[16], best, marks, bounds)
    flag = jnp.maximum(info[17], other_info[17]).astype(F32)
    reach = 384
    row = iota((16, best.shape[1]), 0)
    stack = jnp.zeros(row.shape, F32)
    for at, part in enumerate(thirds(best[...])):
        stack = jnp.where(row == at, part.astype(F32), stack)
    split[...] = stack.astype(BF16)

    def stacked(first, count):
        return split[:, pl.ds(pl.multiple_of(first, 128), count)]

    sub, lane = iota((8, EXTRA), 0), iota((8, EXTRA), 1)
    lower = (lane >= sub * BLOCK) & (lane < sub * BLOCK + BLOCK)
    upper = (lane + EXTRA >= sub * BLOCK) & (lane + EXTRA < sub * BLOCK + BLOCK)
    empty = jnp.where(((lane - sub * BLOCK) & (EXTRA - 1)) >= 64, flag, 0.0)
    for step in range(CHIPS // 8):
        first = (info[step] >> 7) << 7
        pick = hot(iota((reach, 2 * EXTRA), 0) + first == spots[step : step + 1, :])
        value = jnp.sum(dot(stacked(first, reach), pick), 0, keepdims=True)
        line = jnp.where(upper, value[:, EXTRA:], jnp.where(lower, value[:, :EXTRA], empty))
        back[8 * step : 8 * step + 8, :] = line
    fields = fields_of(near[:, mine.shape[1] - EXTRA :]).astype(I32)
    filled = fields[4:5, :] > 0

    @pl.when(jnp.max(fields[4:5, :].astype(F32)) > 0)
    def _():
        total = info[18]
        first = (total >> 7) << 7
        shift = iota((2 * EXTRA, SPILL), 0) - iota((2 * EXTRA, SPILL), 1)
        pick = hot(shift == total - first)
        value = jnp.sum(dot(stacked(first, 2 * EXTRA), pick), 0, keepdims=True)
        source = (iota((CHIPS, SPILL), 0) == fields[7:8, :]) & filled
        line = hot(iota((EXTRA, SPILL), 0) == fields[6:7, :])
        total = back[...]
        for part in thirds(value):
            held = jnp.where(source, part.astype(F32), 0.0).astype(BF16)
            total = total + dot(held, line, COLS)
        back[...] = total


def home_kernel(me, back, place, highest, flag):
    rows = place.shape[1]
    base = (me[0] & 7) * BLOCK
    pick = hot(iota((CHIPS, rows), 0) == place[0:1, :])
    lines = back[...]
    total = jnp.zeros((EXTRA, rows), F32)
    for part in thirds(lines):
        total = total + dot(part, pick, (((0,), (0,)), ((), ())))
    mine = iota((EXTRA, rows), 0) == ((place[1:2, :] + base) & (EXTRA - 1))
    highest[...] = jnp.sum(jnp.where(mine, total, 0.0), 0, keepdims=True)
    marks = ((iota(lines.shape, 1) - base) & (EXTRA - 1)) >= 64
    flag[0] = jnp.max(jnp.where(marks, lines, 0.0)).astype(I32)


def whole(shape):
    return pl.BlockSpec(shape, lambda *_: (0,) * len(shape))


SCALARS = pl.BlockSpec(memory_space=pltpu.SMEM)
HELD = pl.BlockSpec(memory_space=pltpu.VMEM)

LESS = pltpu.CompilerParams(vmem_limit_bytes=28 * 1024 * 1024)


def held(x):
    return pltpu.with_memory_space_constraint(x, pltpu.VMEM)


def array(shape, dtype):
    return jax.ShapeDtypeStruct(shape, dtype)


def exchange(x):
    return lax.all_to_all(
        x, BOTH, split_axis=0, concat_axis=0, tiled=True, axis_index_groups=GROUPS
    )


def direct(attempt, embed, owner, local_id, rank):
    rows, width = embed.shape
    full = width + EXTRA
    lines = CHIPS * BLOCK
    chunks = lines // CHUNK
    me = ((lax.axis_index("grp") >> 1) * 8 + lax.axis_index("blk")).astype(I32).reshape(1)
    sent, place = pl.pallas_call(
        functools.partial(send_kernel, attempt),
        grid=(chunks // 2,),
        in_specs=[SCALARS, whole((rows, width))] + [whole((1, rows))] * 3,
        out_specs=[pl.BlockSpec((2 * CHUNK, width), lambda i: (i, 0)), whole((8, rows))],
        out_shape=[array((lines, width), BF16), array((8, rows), I32)],
        scratch_shapes=[
            pltpu.VMEM((rows, width), BF16),
            pltpu.VMEM((1, rows), I32),
            pltpu.VMEM((CHIPS, width), F32),
        ],
        compiler_params=LESS,
        name="send",
    )(me, embed, owner.reshape(1, rows), local_id.reshape(1, rows), rank.reshape(1, rows))
    taken = exchange(sent.reshape(CHIPS, BLOCK, width)).reshape(lines, width)
    spill, spots, fields, info = pl.pallas_call(
        read_kernel,
        in_specs=[HELD],
        out_specs=[HELD, HELD, HELD, SCALARS],
        out_shape=[
            pltpu.VMEM((SPILL, full), BF16),
            pltpu.VMEM((chunks, 2 * EXTRA), I32),
            pltpu.VMEM((chunks, EXTRA, CHUNK), BF16),
            array((32,), I32),
        ],
        scratch_shapes=[
            pltpu.VMEM((SPILL, full), F32),
            pltpu.VMEM((CHIPS, width), F32),
            pltpu.VMEM((chunks, CHUNK), I32),
        ],
        compiler_params=LESS,
        name="read",
    )(held(taken))
    near = lax.ppermute(spill, BOTH, [(i, i ^ 1) for i in range(2 * CHIPS)])
    packed = pl.pallas_call(
        pack_kernel,
        in_specs=[SCALARS, HELD, HELD, HELD],
        out_specs=HELD,
        out_shape=pltpu.VMEM((PACKED, full), BF16),
        compiler_params=LESS,
        cost_estimate=pl.CostEstimate(
            flops=2 * lines * WINDOW * full, bytes_accessed=4 * lines * full, transcendentals=0
        ),
        name="pack",
    )(info, held(taken), held(spots), held(fields))
    packed, info = pl.pallas_call(
        append_kernel,
        in_specs=[SCALARS, HELD, HELD],
        out_specs=[HELD, SCALARS],
        out_shape=[pltpu.VMEM((PACKED, full), BF16), array((32,), I32)],
        input_output_aliases={2: 0},
        compiler_params=LESS,
        name="append",
    )(info, held(near), held(packed))
    swap = [(i, i ^ 1) for i in range(16)]
    other_info = lax.ppermute(info, "grp", swap)
    other = lax.ppermute(packed, "grp", swap)
    best = pl.pallas_call(
        own_kernel,
        in_specs=[SCALARS, HELD],
        out_specs=HELD,
        out_shape=pltpu.VMEM((1, PACKED), F32),
        scratch_shapes=[pltpu.VMEM((PACKED, EXTRA), I32), pltpu.VMEM((8, PACKED), I32)],
        compiler_params=LESS,
        cost_estimate=pl.CostEstimate(
            flops=2 * 1024 * 1024 * width, bytes_accessed=2 * PACKED * full, transcendentals=0
        ),
        name="own",
    )(info, held(packed))
    back = pl.pallas_call(
        other_kernel,
        in_specs=[SCALARS, SCALARS] + [HELD] * 5,
        out_specs=HELD,
        out_shape=pltpu.VMEM((CHIPS, EXTRA), F32),
        scratch_shapes=[
            pltpu.VMEM((1, PACKED + 2 * TILE), F32),
            pltpu.VMEM((16, PACKED + 2 * TILE), BF16),
            pltpu.VMEM((PACKED, EXTRA), I32),
            pltpu.VMEM((8, PACKED), I32),
        ],
        compiler_params=LESS,
        name="other",
    )(info, other_info, held(packed), held(other), held(near), held(best), held(spots))
    home = exchange(back)
    highest, flag = pl.pallas_call(
        home_kernel,
        in_specs=[SCALARS, whole((CHIPS, EXTRA)), whole((8, rows))],
        out_specs=[whole((1, rows)), SCALARS],
        out_shape=[array((1, rows), F32), array((1,), I32)],
        compiler_params=LESS,
        name="home",
    )(me, home, place)
    return highest.reshape(rows), flag[0]


def group_kernel(queries, keys, best_in, best, marks, bounds):
    best[...] = best_in[...]
    tiles = keys.shape[0] // TILE
    score(queries, tiles, keys, tiles, best, marks, bounds)


def by_group(embed, owner, local_id, rank):
    n_group, n_block = lax.axis_size("grp"), lax.axis_size("blk")
    row_count, columns = embed.shape
    capacity = row_count // 8
    width = n_group * capacity
    full = columns + EXTRA
    wide = embed.astype(F32)
    unit = (wide * lax.rsqrt(jnp.sum(wide * wide, 1, keepdims=True) + EPS)).astype(BF16)
    target = owner[:, 0]
    onehot = (target[:, None] == jnp.arange(n_group, dtype=I32)[None, :]).astype(I32)
    position = jnp.sum((jnp.cumsum(onehot, 0) - 1) * onehot, 1)
    slot_index = target * capacity + position
    fields = jnp.stack([local_id, target, rank >> 8, rank & 255, jnp.ones_like(rank)], 1)
    fields = jnp.pad(fields, ((0, 0), (0, EXTRA - 5))).astype(BF16)
    sent = jnp.zeros((width, full), BF16).at[slot_index].set(jnp.concatenate([unit, fields], 1))
    routed = lax.all_to_all(
        sent.reshape(n_group, capacity, full), "grp", split_axis=0, concat_axis=0, tiled=True
    ).reshape(width, full)
    best = jnp.full((1, width), -1.0, F32)
    for by in range(n_block):
        turn = [(i, (i + by) % n_block) for i in range(n_block)]
        best = pl.pallas_call(
            group_kernel,
            in_specs=[whole((width, full))] * 2 + [whole((1, width))],
            out_specs=whole((1, width)),
            out_shape=array((1, width), F32),
            scratch_shapes=[pltpu.VMEM((width, EXTRA), I32), pltpu.VMEM((8, width), I32)],
            compiler_params=LESS,
            name="group",
        )(routed, lax.ppermute(routed, "blk", turn) if by else routed, best)
    home = lax.all_to_all(
        best.reshape(n_group, capacity), "grp", split_axis=0, concat_axis=0, tiled=True
    )
    return home.reshape(width)[slot_index]


def per_device(*arrays):
    highest, flag = direct(0, *arrays)

    def again():
        second, still = direct(1, *arrays)
        return lax.cond(still > 0, lambda: by_group(*arrays), lambda: second)

    return lax.cond(flag > 0, again, lambda: highest)


def solution(mesh):
    in_specs = (
        P(("grp", "blk"), None),
        P(("grp", "blk"), None),
        P(("grp", "blk")),
        P(("grp", "blk")),
    )
    out_specs = P(("grp", "blk"))
    return jax.shard_map(
        per_device, mesh=mesh, in_specs=in_specs, out_specs=out_specs, check_vma=False
    )
```

```python
import functools

import jax
import jax.numpy as jnp
from jax import lax
from jax.experimental import pallas as pl
from jax.experimental.pallas import tpu as pltpu
from jax.sharding import PartitionSpec as P

EPS = 1e-06
BOTH = ("grp", "blk")
CHIPS = 64
BLOCK = 24
SEATS = 23
EXTRA = 128
CHUNK = 8 * BLOCK
WINDOW = CHUNK + 16
TILE = 256
TILES = 6
PACKED = TILE * TILES
SIZES = (256, 512, 768, 1024, 1152, 1280, 1408, 1536)
SPILL = 128
GROUPS = [[g * 8 + b for g in range(core, 16, 2) for b in range(8)] for core in range(2)]
COLS = (((1,), (1,)), ((), ()))
F32 = jnp.float32
BF16 = jnp.bfloat16
I32 = jnp.int32
LOWEST = -(2**31)


def iota(shape, dim):
    return lax.broadcasted_iota(I32, shape, dim)


def hot(mask):
    return jnp.where(mask, jnp.float32(1), jnp.float32(0)).astype(BF16)


def dot(a, b, dims=(((1,), (0,)), ((), ()))):
    return lax.dot_general(a, b, dims, preferred_element_type=F32)


def thirds(x):
    high = x.astype(BF16)
    rest = x - high.astype(F32)
    middle = rest.astype(BF16)
    return high, middle, (rest - middle.astype(F32)).astype(BF16)


def fields_of(extra):
    return dot(hot(iota((16, EXTRA), 0) == iota((16, EXTRA), 1)), extra, COLS)


def chip_of(group, number, attempt):
    if attempt == 0:
        return (number >> 1) ^ (group * 4)
    turned = ((number >> 3) | (number << 4)) & (CHIPS - 1)
    return turned ^ (((group * 5 + 2) & 15) * 4)


def send_kernel(attempt, me, hop, embed, owner, local, rank, out, place, unit, slot, ends):
    rows, width = embed.shape
    step = pl.program_id(0)
    block = out.shape[0]

    @pl.when(step == 0)
    def _():
        wide = embed[...].astype(F32)
        scale = lax.rsqrt(jnp.sum(wide * wide, 1, keepdims=True) + EPS)
        unit[...] = (wide * scale).astype(BF16)
        group, number, order = owner[...], local[...], rank[...]
        chip = chip_of(group, number, attempt)
        own = iota((CHIPS, rows), 0) == chip
        beyond = chip ^ hop[0]
        near = iota((CHIPS, rows), 0) == beyond
        before = hot(iota((rows, rows), 0) < iota((rows, rows), 1))
        ahead = dot(hot(own), before)
        count = jnp.sum(jnp.where(own, 1.0, 0.0), 1, keepdims=True)
        position = jnp.sum(jnp.where(own, ahead, 0.0), 0, keepdims=True).astype(I32)
        beside = jnp.sum(jnp.where(near, count, 0.0), 0, keepdims=True).astype(I32)
        spilled = position >= SEATS
        seat = jnp.where(spilled, beside + position - SEATS, position)
        late = jnp.max(jnp.where(seat >= SEATS, 1.0, 0.0), 1, keepdims=True)
        goes = jnp.where(seat < SEATS, jnp.where(spilled, beyond, chip), -1)
        line = seat + jnp.where(spilled, 32, 0)
        slot[...] = jnp.where(goes >= 0, goes * BLOCK + seat, -1)
        place[...] = jnp.where(iota(place.shape, 0) == 0, chip, line)
        entries = (
            number,
            group,
            order >> 8,
            order & 255,
            jnp.ones_like(order),
            jnp.where(spilled, 1, 0),
            (line + (me[0] & 7) * BLOCK) & (EXTRA - 1),
            jnp.broadcast_to(me[0], order.shape),
        )
        there = iota((CHIPS, rows), 0) == goes
        tables = [jnp.where(there, entry.astype(F32), 0.0).astype(BF16) for entry in entries]
        seats = hot(iota((EXTRA, rows), 0) == seat)
        fields = dot(jnp.concatenate(tables, 0), seats, COLS)
        lane = iota((CHIPS, EXTRA), 1)
        for at in range(len(entries)):
            field = fields[CHIPS * at : CHIPS * (at + 1), :]
            if at == 0:
                field = jnp.where(lane == EXTRA - 1, late, field)
            ends[:, EXTRA * at : EXTRA * (at + 1)] = field

    pick = hot(iota((block, rows), 0) == slot[...] - step * block)
    moved = dot(pick, unit[...])
    senders = block // BLOCK
    end = ends[pl.ds(pl.multiple_of(step * senders, 8), senders), :]
    last = iota((8, width), 0) == 7
    pieces = []
    for at in range(block // BLOCK):
        top = at * BLOCK
        pieces.append(moved[top : top + 16, :])
        pieces.append(jnp.where(last, end[at : at + 1, :], moved[top + 16 : top + 24, :]))
    out[...] = jnp.concatenate(pieces, 0).astype(BF16)


def gather(spot, count, taken, rows, fields):
    pick = hot(iota((count, CHUNK), 0) == spot)
    return dot(pick, taken[rows, :]), dot(pick, fields, COLS)


def read_kernel(taken, spill, spots, fields, info, pile, ends, strange):
    chunks = taken.shape[0] // CHUNK
    width = taken.shape[1]
    upto = hot(iota((CHUNK, CHUNK), 0) <= iota((CHUNK, CHUNK), 1))
    place = iota((EXTRA, CHUNK), 1)
    sender = jnp.zeros(place.shape, I32)
    for at in range(1, 8):
        sender = sender + jnp.where(place >= at * BLOCK, 1, 0)
    spread = hot(place - sender * BLOCK == iota((EXTRA, CHUNK), 0))
    mine = (iota((64, CHUNK), 0) & 7) == sender[:64, :]
    spots[...] = jnp.full(spots.shape, -1, I32)
    for at in range(CHIPS):
        last = at * BLOCK + SEATS
        top = (last // 16) * 16
        tile = taken[top : top + 16, :].astype(F32)
        ends[at : at + 1, :] = tile[last - top : last - top + 1, :]
    late = jnp.max(ends[:, EXTRA - 1 : EXTRA])
    stack = [
        ends[8 * at : 8 * at + 8, EXTRA * f : EXTRA * (f + 1)]
        for at in range(chunks)
        for f in range(8)
    ]
    wide = dot(jnp.concatenate(stack, 0).astype(BF16), spread)
    natives, foreigns = [], []
    for at in range(chunks):
        part = jnp.where(mine, wide[64 * at : 64 * at + 64, :], 0.0)
        found = [jnp.sum(part[8 * f : 8 * f + 8, :], 0, keepdims=True) for f in range(8)]
        table = jnp.concatenate(found + [jnp.zeros((EXTRA - 8, CHUNK), F32)], 0)
        fields[at] = table.astype(BF16)
        natives.append(found[4] - found[5])
        foreigns.append(found[5])
    both = jnp.concatenate(natives + foreigns, 0)
    running = dot(both.astype(BF16), upto).astype(I32)
    start, start_strange = jnp.int32(0), jnp.int32(0)
    for at in range(chunks):
        native, foreign = natives[at], foreigns[at]
        spots[at : at + 1, 0:CHUNK] = jnp.where(
            native > 0, running[at : at + 1, :] + (start - 1), -1
        )
        strange[at : at + 1, :] = jnp.where(
            foreign > 0, running[chunks + at : chunks + at + 1, :] + (start_strange - 1), -1
        )
        info[at] = (start >> 4) << 4
        start = start + jnp.sum(native).astype(I32)
        start_strange = start_strange + jnp.sum(foreign).astype(I32)
    info[16] = (start + TILE - 1) // TILE
    info[17] = jnp.where((start_strange > SPILL) | (late > 0), 1, 0)
    info[18] = start
    info[19] = start
    pile[...] = jnp.zeros(pile.shape, F32)

    @pl.when(start_strange > 0)
    def _():
        def step(at, carry):
            rows = pl.ds(pl.multiple_of(at * CHUNK, CHUNK), CHUNK)
            rows_in, side = gather(strange[pl.ds(at, 1), :], SPILL, taken, rows, fields[at])
            pile[:, :width] += rows_in
            pile[:, width:] += side
            return carry

        lax.fori_loop(0, chunks, step, 0)

    spill[...] = pile[...].astype(BF16)


def pack_kernel(info, taken, spots, fields, packed):
    width = taken.shape[1]
    tiles = info[16]
    packed[0:16, :] = jnp.zeros((16, packed.shape[1]), BF16)
    first = jnp.int32(0)
    for at in range(taken.shape[0] // CHUNK):
        first = pl.multiple_of(jnp.minimum(info[at], PACKED - WINDOW), 16)
        spot = spots[at : at + 1, 0:CHUNK] - first
        rows_in, side = gather(spot, WINDOW, taken, pl.ds(at * CHUNK, CHUNK), fields[at])
        here = pl.ds(first, 16)
        after = pl.ds(pl.multiple_of(first + 16, 16), WINDOW - 16)
        for span, value in ((pl.ds(0, width), rows_in), (pl.ds(width, EXTRA), side)):
            packed[here, span] = (packed[here, span].astype(F32) + value[:16]).astype(BF16)
            packed[after, span] = value[16:].astype(BF16)
    clear(packed, (first + WINDOW) // 16, tiles * (TILE // 16))


def clear(rows, low, high):
    def step(at, carry):
        rows[pl.ds(pl.multiple_of(at * 16, 16), 16), :] = jnp.zeros((16, rows.shape[1]), BF16)
        return carry

    lax.fori_loop(low, high, step, 0)


def append_kernel(info, near, packed_in, packed, info_out):
    for at in range(20):
        info_out[at] = info[at]
    total, tiles = info[18], info[16]
    count = jnp.sum(near[:, packed.shape[1] - EXTRA :].astype(F32)[:, 4:5]).astype(I32)
    begin = jnp.minimum((total >> 4) << 4, PACKED - SPILL - 16)
    fits = total + count <= PACKED

    @pl.when((count > 0) & jnp.logical_not(fits))
    def _():
        info_out[17] = 1

    @pl.when((count > 0) & fits)
    def _():
        more = (total + count + TILE - 1) // TILE
        info_out[16] = more
        info_out[19] = total + count
        clear(packed, tiles * (TILE // 16), more * (TILE // 16))
        shift = iota((SPILL + 16, SPILL), 0) - iota((SPILL + 16, SPILL), 1)
        moved = dot(hot(shift == total - begin), near[...])
        keep = iota(moved.shape, 0) < total - begin
        here = pl.ds(pl.multiple_of(begin, 16), SPILL + 16)
        packed[here, :] = jnp.where(keep, packed[here, :].astype(F32), moved).astype(BF16)


def score(queries, query_rows, keys, key_rows, best, marks, bounds):
    width = queries.shape[1] - EXTRA
    fields = fields_of(queries[:, width:]).astype(I32)
    bounds[0:1, :] = (fields[1:2, :] * 128 + fields[0:1, :] + fields[4:5, :]) * 65536
    bounds[1:2, :] = fields[2:3, :] * 256 + fields[3:4, :] + LOWEST

    def mark_step(at, carry):
        span = pl.ds(pl.multiple_of(at * TILE, TILE), TILE)
        side = keys[span, width:].astype(F32).astype(I32)
        mark = (side[:, 1:2] * 128 + side[:, 0:1] + side[:, 4:5]) * 65536
        mark = mark + side[:, 2:3] * 256 + side[:, 3:4] + LOWEST
        marks[span, :] = jnp.broadcast_to(mark, (TILE, EXTRA))
        return carry

    query_tiles, key_tiles = (query_rows + TILE - 1) // TILE, (key_rows + TILE - 1) // TILE
    lax.fori_loop(0, key_tiles, mark_step, 0)

    def against(size):
        def query_step(at, carry):
            rows = pl.ds(pl.multiple_of(at * TILE, TILE), TILE)
            mark = marks[:size, :]
            mark = jnp.concatenate([mark] * (TILE // EXTRA), 1)
            scores = dot(keys[:size, :width], queries[rows, :width], COLS)
            earlier = mark - bounds[0:1, rows] < bounds[1:2, rows]
            found = jnp.max(jnp.where(earlier, scores, -1.0), 0, keepdims=True)
            best[:, rows] = jnp.maximum(best[:, rows], found)
            return carry

        lax.fori_loop(0, query_tiles, query_step, 0)

    if isinstance(key_rows, int):
        against(key_rows)
        return
    low = 0
    for size in SIZES:
        pl.when((key_rows > low) & (key_rows <= size))(functools.partial(against, size))
        low = size


def own_kernel(info, packed, best, marks, bounds):
    best[...] = jnp.full(best.shape, -1.0, F32)
    score(packed, info[19], packed, info[19], best, marks, bounds)


def other_kernel(
    info, other_info, mine, theirs, near, best_in, spots, back, best, split, marks, bounds
):
    best[:, :PACKED] = best_in[...]
    best[:, PACKED:] = jnp.full((1, best.shape[1] - PACKED), -1.0, F32)
    score(mine, info[19], theirs, other_info[19], best, marks, bounds)
    flag = jnp.maximum(info[17], other_info[17]).astype(F32)
    reach = 384
    row = iota((16, best.shape[1]), 0)
    stack = jnp.zeros(row.shape, F32)
    for at, part in enumerate(thirds(best[...])):
        stack = jnp.where(row == at, part.astype(F32), stack)
    split[...] = stack.astype(BF16)

    def stacked(first, count):
        return split[:, pl.ds(pl.multiple_of(first, 128), count)]

    sub, lane = iota((8, EXTRA), 0), iota((8, EXTRA), 1)
    lower = (lane >= sub * BLOCK) & (lane < sub * BLOCK + BLOCK)
    upper = (lane + EXTRA >= sub * BLOCK) & (lane + EXTRA < sub * BLOCK + BLOCK)
    empty = jnp.where(((lane - sub * BLOCK) & (EXTRA - 1)) >= 64, flag, 0.0)
    for step in range(CHIPS // 8):
        first = (info[step] >> 7) << 7
        pick = hot(iota((reach, 2 * EXTRA), 0) + first == spots[step : step + 1, :])
        value = jnp.sum(dot(stacked(first, reach), pick), 0, keepdims=True)
        line = jnp.where(upper, value[:, EXTRA:], jnp.where(lower, value[:, :EXTRA], empty))
        back[8 * step : 8 * step + 8, :] = line
    fields = fields_of(near[:, mine.shape[1] - EXTRA :]).astype(I32)
    filled = fields[4:5, :] > 0

    @pl.when(jnp.max(fields[4:5, :].astype(F32)) > 0)
    def _():
        total = info[18]
        first = (total >> 7) << 7
        shift = iota((2 * EXTRA, SPILL), 0) - iota((2 * EXTRA, SPILL), 1)
        pick = hot(shift == total - first)
        value = jnp.sum(dot(stacked(first, 2 * EXTRA), pick), 0, keepdims=True)
        source = (iota((CHIPS, SPILL), 0) == fields[7:8, :]) & filled
        line = hot(iota((EXTRA, SPILL), 0) == fields[6:7, :])
        total = back[...]
        for part in thirds(value):
            held = jnp.where(source, part.astype(F32), 0.0).astype(BF16)
            total = total + dot(held, line, COLS)
        back[...] = total


def home_kernel(me, back, place, highest, flag):
    rows = place.shape[1]
    base = (me[0] & 7) * BLOCK
    pick = hot(iota((CHIPS, rows), 0) == place[0:1, :])
    lines = back[...]
    total = jnp.zeros((EXTRA, rows), F32)
    for part in thirds(lines):
        total = total + dot(part, pick, (((0,), (0,)), ((), ())))
    mine = iota((EXTRA, rows), 0) == ((place[1:2, :] + base) & (EXTRA - 1))
    highest[...] = jnp.sum(jnp.where(mine, total, 0.0), 0, keepdims=True)
    marks = ((iota(lines.shape, 1) - base) & (EXTRA - 1)) >= 64
    flag[0] = jnp.max(jnp.where(marks, lines, 0.0)).astype(I32)


def whole(shape):
    return pl.BlockSpec(shape, lambda *_: (0,) * len(shape))


SCALARS = pl.BlockSpec(memory_space=pltpu.SMEM)
HELD = pl.BlockSpec(memory_space=pltpu.VMEM)

LESS = pltpu.CompilerParams(vmem_limit_bytes=28 * 1024 * 1024)


def held(x):
    return pltpu.with_memory_space_constraint(x, pltpu.VMEM)


def array(shape, dtype):
    return jax.ShapeDtypeStruct(shape, dtype)


def exchange(x):
    return lax.all_to_all(
        x, BOTH, split_axis=0, concat_axis=0, tiled=True, axis_index_groups=GROUPS
    )


def direct(attempt, embed, owner, local_id, rank):
    rows, width = embed.shape
    full = width + EXTRA
    lines = CHIPS * BLOCK
    chunks = lines // CHUNK
    group = lax.axis_index("grp")
    core = group & 1
    me = ((group >> 1) * 8 + lax.axis_index("blk")).astype(I32).reshape(1)
    hop = (core * 2 + 1).astype(I32).reshape(1)
    sent, place = pl.pallas_call(
        functools.partial(send_kernel, attempt),
        grid=(chunks // 2,),
        in_specs=[SCALARS, SCALARS, whole((rows, width))] + [whole((1, rows))] * 3,
        out_specs=[pl.BlockSpec((2 * CHUNK, width), lambda i: (i, 0)), whole((8, rows))],
        out_shape=[array((lines, width), BF16), array((8, rows), I32)],
        scratch_shapes=[
            pltpu.VMEM((rows, width), BF16),
            pltpu.VMEM((1, rows), I32),
            pltpu.VMEM((CHIPS, width), F32),
        ],
        compiler_params=LESS,
        name="send",
    )(me, hop, embed, owner.reshape(1, rows), local_id.reshape(1, rows), rank.reshape(1, rows))
    taken = exchange(sent.reshape(CHIPS, BLOCK, width)).reshape(lines, width)
    spill, spots, fields, info = pl.pallas_call(
        read_kernel,
        in_specs=[HELD],
        out_specs=[HELD, HELD, HELD, SCALARS],
        out_shape=[
            pltpu.VMEM((SPILL, full), BF16),
            pltpu.VMEM((chunks, 2 * EXTRA), I32),
            pltpu.VMEM((chunks, EXTRA, CHUNK), BF16),
            array((32,), I32),
        ],
        scratch_shapes=[
            pltpu.VMEM((SPILL, full), F32),
            pltpu.VMEM((CHIPS, width), F32),
            pltpu.VMEM((chunks, CHUNK), I32),
        ],
        compiler_params=LESS,
        name="read",
    )(held(taken))
    beside = [(i, i ^ (1 + (i >> 3 & 1) * 2)) for i in range(2 * CHIPS)]
    near = lax.ppermute(spill, BOTH, beside)
    packed = pl.pallas_call(
        pack_kernel,
        in_specs=[SCALARS, HELD, HELD, HELD],
        out_specs=HELD,
        out_shape=pltpu.VMEM((PACKED, full), BF16),
        compiler_params=LESS,
        cost_estimate=pl.CostEstimate(
            flops=2 * lines * WINDOW * full, bytes_accessed=4 * lines * full, transcendentals=0
        ),
        name="pack",
    )(info, held(taken), held(spots), held(fields))
    packed, info = pl.pallas_call(
        append_kernel,
        in_specs=[SCALARS, HELD, HELD],
        out_specs=[HELD, SCALARS],
        out_shape=[pltpu.VMEM((PACKED, full), BF16), array((32,), I32)],
        input_output_aliases={2: 0},
        compiler_params=LESS,
        name="append",
    )(info, held(near), held(packed))
    swap = [(i, i ^ 1) for i in range(16)]
    other_info = lax.ppermute(info, "grp", swap)
    other = lax.ppermute(packed, "grp", swap)
    best = pl.pallas_call(
        own_kernel,
        in_specs=[SCALARS, HELD],
        out_specs=HELD,
        out_shape=pltpu.VMEM((1, PACKED), F32),
        scratch_shapes=[pltpu.VMEM((PACKED, EXTRA), I32), pltpu.VMEM((8, PACKED), I32)],
        compiler_params=LESS,
        cost_estimate=pl.CostEstimate(
            flops=2 * 1024 * 1024 * width, bytes_accessed=2 * PACKED * full, transcendentals=0
        ),
        name="own",
    )(info, held(packed))
    back = pl.pallas_call(
        other_kernel,
        in_specs=[SCALARS, SCALARS] + [HELD] * 5,
        out_specs=HELD,
        out_shape=pltpu.VMEM((CHIPS, EXTRA), F32),
        scratch_shapes=[
            pltpu.VMEM((1, PACKED + 2 * TILE), F32),
            pltpu.VMEM((16, PACKED + 2 * TILE), BF16),
            pltpu.VMEM((PACKED, EXTRA), I32),
            pltpu.VMEM((8, PACKED), I32),
        ],
        compiler_params=LESS,
        name="other",
    )(info, other_info, held(packed), held(other), held(near), held(best), held(spots))
    home = exchange(back)
    highest, flag = pl.pallas_call(
        home_kernel,
        in_specs=[SCALARS, whole((CHIPS, EXTRA)), whole((8, rows))],
        out_specs=[whole((1, rows)), SCALARS],
        out_shape=[array((1, rows), F32), array((1,), I32)],
        compiler_params=LESS,
        name="home",
    )(me, home, place)
    return highest.reshape(rows), flag[0]


def group_kernel(queries, keys, best_in, best, marks, bounds):
    best[...] = best_in[...]
    rows = keys.shape[0]
    score(queries, rows, keys, rows, best, marks, bounds)


def by_group(embed, owner, local_id, rank):
    n_group, n_block = lax.axis_size("grp"), lax.axis_size("blk")
    row_count, columns = embed.shape
    capacity = row_count // 8
    width = n_group * capacity
    full = columns + EXTRA
    wide = embed.astype(F32)
    unit = (wide * lax.rsqrt(jnp.sum(wide * wide, 1, keepdims=True) + EPS)).astype(BF16)
    target = owner[:, 0]
    onehot = (target[:, None] == jnp.arange(n_group, dtype=I32)[None, :]).astype(I32)
    position = jnp.sum((jnp.cumsum(onehot, 0) - 1) * onehot, 1)
    slot_index = target * capacity + position
    fields = jnp.stack([local_id, target, rank >> 8, rank & 255, jnp.ones_like(rank)], 1)
    fields = jnp.pad(fields, ((0, 0), (0, EXTRA - 5))).astype(BF16)
    sent = jnp.zeros((width, full), BF16).at[slot_index].set(jnp.concatenate([unit, fields], 1))
    routed = lax.all_to_all(
        sent.reshape(n_group, capacity, full), "grp", split_axis=0, concat_axis=0, tiled=True
    ).reshape(width, full)
    best = jnp.full((1, width), -1.0, F32)
    for by in range(n_block):
        turn = [(i, (i + by) % n_block) for i in range(n_block)]
        best = pl.pallas_call(
            group_kernel,
            in_specs=[whole((width, full))] * 2 + [whole((1, width))],
            out_specs=whole((1, width)),
            out_shape=array((1, width), F32),
            scratch_shapes=[pltpu.VMEM((width, EXTRA), I32), pltpu.VMEM((8, width), I32)],
            compiler_params=LESS,
            name="group",
        )(routed, lax.ppermute(routed, "blk", turn) if by else routed, best)
    home = lax.all_to_all(
        best.reshape(n_group, capacity), "grp", split_axis=0, concat_axis=0, tiled=True
    )
    return home.reshape(width)[slot_index]


def per_device(*arrays):
    highest, flag = direct(0, *arrays)

    def again():
        second, still = direct(1, *arrays)
        return lax.cond(still > 0, lambda: by_group(*arrays), lambda: second)

    return lax.cond(flag > 0, again, lambda: highest)


def solution(mesh):
    in_specs = (
        P(("grp", "blk"), None),
        P(("grp", "blk"), None),
        P(("grp", "blk")),
        P(("grp", "blk")),
    )
    out_specs = P(("grp", "blk"))
    return jax.shard_map(
        per_device, mesh=mesh, in_specs=in_specs, out_specs=out_specs, check_vma=False
    )
```

```python
import functools

import jax
import jax.numpy as jnp
from jax import lax
from jax.experimental import pallas as pl
from jax.experimental.pallas import tpu as pltpu
from jax.sharding import PartitionSpec as P

EPS = 1e-06
BOTH = ("grp", "blk")
CHIPS = 64
BLOCK = 24
SEATS = 23
EXTRA = 128
CHUNK = 8 * BLOCK
WINDOW = CHUNK + 16
TILE = 256
TILES = 6
PACKED = TILE * TILES
SIZES = (256, 512, 768, 1024, 1152, 1280, 1408, 1536)
SPILL = 128
GROUPS = [[g * 8 + b for g in range(core, 16, 2) for b in range(8)] for core in range(2)]
COLS = (((1,), (1,)), ((), ()))
F32 = jnp.float32
BF16 = jnp.bfloat16
I32 = jnp.int32
LOWEST = -(2**31)


def iota(shape, dim):
    return lax.broadcasted_iota(I32, shape, dim)


def hot(mask):
    return jnp.where(mask, jnp.float32(1), jnp.float32(0)).astype(BF16)


def dot(a, b, dims=(((1,), (0,)), ((), ()))):
    return lax.dot_general(a, b, dims, preferred_element_type=F32)


def thirds(x):
    high = x.astype(BF16)
    rest = x - high.astype(F32)
    middle = rest.astype(BF16)
    return high, middle, (rest - middle.astype(F32)).astype(BF16)


def fields_of(extra):
    return dot(hot(iota((16, EXTRA), 0) == iota((16, EXTRA), 1)), extra, COLS)


def chip_of(group, number, attempt):
    if attempt == 0:
        return (number >> 1) ^ (group * 4)
    turned = ((number >> 3) | (number << 4)) & (CHIPS - 1)
    return turned ^ (((group * 5 + 2) & 15) * 4)


def send_kernel(attempt, me, hop, embed, owner, local, rank, out, place, unit, slot, ends):
    rows, width = embed.shape
    step = pl.program_id(0)
    block = out.shape[0]

    @pl.when(step == 0)
    def _():
        wide = embed[...].astype(F32)
        scale = lax.rsqrt(jnp.sum(wide * wide, 1, keepdims=True) + EPS)
        unit[...] = (wide * scale).astype(BF16)
        group, number, order = owner[...], local[...], rank[...]
        chip = chip_of(group, number, attempt)
        own = iota((CHIPS, rows), 0) == chip
        beyond = chip ^ hop[0]
        near = iota((CHIPS, rows), 0) == beyond
        before = hot(iota((rows, rows), 0) < iota((rows, rows), 1))
        ahead = dot(hot(own), before)
        count = jnp.sum(jnp.where(own, 1.0, 0.0), 1, keepdims=True)
        position = jnp.sum(jnp.where(own, ahead, 0.0), 0, keepdims=True).astype(I32)
        beside = jnp.sum(jnp.where(near, count, 0.0), 0, keepdims=True).astype(I32)
        spilled = position >= SEATS
        seat = jnp.where(spilled, beside + position - SEATS, position)
        late = jnp.max(jnp.where(seat >= SEATS, 1.0, 0.0), 1, keepdims=True)
        goes = jnp.where(seat < SEATS, jnp.where(spilled, beyond, chip), -1)
        line = seat + jnp.where(spilled, 32, 0)
        slot[...] = jnp.where(goes >= 0, goes * BLOCK + seat, -1)
        place[...] = jnp.where(iota(place.shape, 0) == 0, chip, line)
        entries = (
            number,
            group,
            order >> 8,
            order & 255,
            jnp.ones_like(order),
            jnp.where(spilled, 1, 0),
            (line + (me[0] & 7) * BLOCK) & (EXTRA - 1),
            jnp.broadcast_to(me[0], order.shape),
        )
        there = iota((CHIPS, rows), 0) == goes
        tables = [jnp.where(there, entry.astype(F32), 0.0).astype(BF16) for entry in entries]
        seats = hot(iota((EXTRA, rows), 0) == seat)
        fields = dot(jnp.concatenate(tables, 0), seats, COLS)
        lane = iota((CHIPS, EXTRA), 1)
        for at in range(len(entries)):
            field = fields[CHIPS * at : CHIPS * (at + 1), :]
            if at == 0:
                field = jnp.where(lane == EXTRA - 1, late, field)
            ends[:, EXTRA * at : EXTRA * (at + 1)] = field

    pick = hot(iota((block, rows), 0) == slot[...] - step * block)
    moved = dot(pick, unit[...])
    senders = block // BLOCK
    end = ends[pl.ds(pl.multiple_of(step * senders, 8), senders), :]
    last = iota((8, width), 0) == 7
    pieces = []
    for at in range(block // BLOCK):
        top = at * BLOCK
        pieces.append(moved[top : top + 16, :])
        pieces.append(jnp.where(last, end[at : at + 1, :], moved[top + 16 : top + 24, :]))
    out[...] = jnp.concatenate(pieces, 0).astype(BF16)


def gather(spot, count, taken, rows, fields):
    pick = hot(iota((count, CHUNK), 0) == spot)
    return dot(pick, taken[rows, :]), dot(pick, fields, COLS)


def read_kernel(taken, spill, spots, fields, info, pile, ends, strange):
    chunks = taken.shape[0] // CHUNK
    width = taken.shape[1]
    upto = hot(iota((CHUNK, CHUNK), 0) <= iota((CHUNK, CHUNK), 1))
    place = iota((EXTRA, CHUNK), 1)
    sender = jnp.zeros(place.shape, I32)
    for at in range(1, 8):
        sender = sender + jnp.where(place >= at * BLOCK, 1, 0)
    spread = hot(place - sender * BLOCK == iota((EXTRA, CHUNK), 0))
    mine = (iota((64, CHUNK), 0) & 7) == sender[:64, :]
    spots[...] = jnp.full(spots.shape, -1, I32)
    for at in range(CHIPS):
        last = at * BLOCK + SEATS
        top = (last // 16) * 16
        tile = taken[top : top + 16, :].astype(F32)
        ends[at : at + 1, :] = tile[last - top : last - top + 1, :]
    late = jnp.max(ends[:, EXTRA - 1 : EXTRA])
    stack = [
        ends[8 * at : 8 * at + 8, EXTRA * f : EXTRA * (f + 1)]
        for at in range(chunks)
        for f in range(8)
    ]
    wide = dot(jnp.concatenate(stack, 0).astype(BF16), spread)
    natives, foreigns = [], []
    for at in range(chunks):
        part = jnp.where(mine, wide[64 * at : 64 * at + 64, :], 0.0)
        found = [jnp.sum(part[8 * f : 8 * f + 8, :], 0, keepdims=True) for f in range(8)]
        table = jnp.concatenate(found + [jnp.zeros((EXTRA - 8, CHUNK), F32)], 0)
        fields[at] = table.astype(BF16)
        natives.append(found[4] - found[5])
        foreigns.append(found[5])
    both = jnp.concatenate(natives + foreigns, 0)
    running = dot(both.astype(BF16), upto).astype(I32)
    start, start_strange = jnp.int32(0), jnp.int32(0)
    for at in range(chunks):
        native, foreign = natives[at], foreigns[at]
        spots[at : at + 1, 0:CHUNK] = jnp.where(
            native > 0, running[at : at + 1, :] + (start - 1), -1
        )
        strange[at : at + 1, :] = jnp.where(
            foreign > 0, running[chunks + at : chunks + at + 1, :] + (start_strange - 1), -1
        )
        info[at] = (start >> 4) << 4
        start = start + jnp.sum(native).astype(I32)
        start_strange = start_strange + jnp.sum(foreign).astype(I32)
    info[16] = (start + TILE - 1) // TILE
    info[17] = jnp.where((start_strange > SPILL) | (late > 0), 1, 0)
    info[18] = start
    info[19] = start
    pile[...] = jnp.zeros(pile.shape, F32)

    @pl.when(start_strange > 0)
    def _():
        def step(at, carry):
            rows = pl.ds(pl.multiple_of(at * CHUNK, CHUNK), CHUNK)
            rows_in, side = gather(strange[pl.ds(at, 1), :], SPILL, taken, rows, fields[at])
            pile[:, :width] += rows_in
            pile[:, width:] += side
            return carry

        lax.fori_loop(0, chunks, step, 0)

    spill[...] = pile[...].astype(BF16)


def pack_kernel(info, taken, spots, fields, packed):
    width = taken.shape[1]
    tiles = info[16]
    packed[0:16, :] = jnp.zeros((16, packed.shape[1]), BF16)
    first = jnp.int32(0)
    for at in range(taken.shape[0] // CHUNK):
        first = pl.multiple_of(jnp.minimum(info[at], PACKED - WINDOW), 16)
        spot = spots[at : at + 1, 0:CHUNK] - first
        rows_in, side = gather(spot, WINDOW, taken, pl.ds(at * CHUNK, CHUNK), fields[at])
        here = pl.ds(first, 16)
        after = pl.ds(pl.multiple_of(first + 16, 16), WINDOW - 16)
        for span, value in ((pl.ds(0, width), rows_in), (pl.ds(width, EXTRA), side)):
            packed[here, span] = (packed[here, span].astype(F32) + value[:16]).astype(BF16)
            packed[after, span] = value[16:].astype(BF16)
    clear(packed, (first + WINDOW) // 16, tiles * (TILE // 16))


def clear(rows, low, high):
    def step(at, carry):
        rows[pl.ds(pl.multiple_of(at * 16, 16), 16), :] = jnp.zeros((16, rows.shape[1]), BF16)
        return carry

    lax.fori_loop(low, high, step, 0)


def append_kernel(info, near, packed_in, packed, info_out):
    for at in range(20):
        info_out[at] = info[at]
    total, tiles = info[18], info[16]
    count = jnp.sum(near[:, packed.shape[1] - EXTRA :].astype(F32)[:, 4:5]).astype(I32)
    begin = jnp.minimum((total >> 4) << 4, PACKED - SPILL - 16)
    fits = total + count <= PACKED

    @pl.when((count > 0) & jnp.logical_not(fits))
    def _():
        info_out[17] = 1

    @pl.when((count > 0) & fits)
    def _():
        more = (total + count + TILE - 1) // TILE
        info_out[16] = more
        info_out[19] = total + count
        clear(packed, tiles * (TILE // 16), more * (TILE // 16))
        shift = iota((SPILL + 16, SPILL), 0) - iota((SPILL + 16, SPILL), 1)
        moved = dot(hot(shift == total - begin), near[...])
        keep = iota(moved.shape, 0) < total - begin
        here = pl.ds(pl.multiple_of(begin, 16), SPILL + 16)
        packed[here, :] = jnp.where(keep, packed[here, :].astype(F32), moved).astype(BF16)


def score(queries, query_rows, keys, key_rows, best, marks, bounds):
    width = queries.shape[1] - EXTRA
    fields = fields_of(queries[:, width:]).astype(I32)
    bounds[0:1, :] = (fields[1:2, :] * 128 + fields[0:1, :] + fields[4:5, :]) * 65536
    bounds[1:2, :] = fields[2:3, :] * 256 + fields[3:4, :] + LOWEST

    def mark_step(at, carry):
        span = pl.ds(pl.multiple_of(at * TILE, TILE), TILE)
        side = keys[span, width:].astype(F32).astype(I32)
        mark = (side[:, 1:2] * 128 + side[:, 0:1] + side[:, 4:5]) * 65536
        mark = mark + side[:, 2:3] * 256 + side[:, 3:4] + LOWEST
        marks[span, :] = jnp.broadcast_to(mark, (TILE, EXTRA))
        return carry

    query_tiles, key_tiles = (query_rows + TILE - 1) // TILE, (key_rows + TILE - 1) // TILE
    lax.fori_loop(0, key_tiles, mark_step, 0)

    def against(size):
        def query_step(at, carry):
            rows = pl.ds(pl.multiple_of(at * TILE, TILE), TILE)
            mark = marks[:size, :]
            mark = jnp.concatenate([mark] * (TILE // EXTRA), 1)
            scores = dot(keys[:size, :width], queries[rows, :width], COLS)
            earlier = mark - bounds[0:1, rows] < bounds[1:2, rows]
            found = jnp.max(jnp.where(earlier, scores, -1.0), 0, keepdims=True)
            best[:, rows] = jnp.maximum(best[:, rows], found)
            return carry

        lax.fori_loop(0, query_tiles, query_step, 0)

    if isinstance(key_rows, int):
        against(key_rows)
        return
    low = 0
    for size in SIZES:
        pl.when((key_rows > low) & (key_rows <= size))(functools.partial(against, size))
        low = size


def own_kernel(info, packed, best, marks, bounds):
    best[...] = jnp.full(best.shape, -1.0, F32)
    score(packed, info[19], packed, info[19], best, marks, bounds)


def other_kernel(
    info, other_info, mine, theirs, near, best_in, spots, back, best, split, marks, bounds
):
    best[:, :PACKED] = best_in[...]
    best[:, PACKED:] = jnp.full((1, best.shape[1] - PACKED), -1.0, F32)
    score(mine, info[19], theirs, other_info[19], best, marks, bounds)
    flag = jnp.maximum(info[17], other_info[17]).astype(F32)
    reach = 384
    row = iota((16, best.shape[1]), 0)
    stack = jnp.zeros(row.shape, F32)
    for at, part in enumerate(thirds(best[...])):
        stack = jnp.where(row == at, part.astype(F32), stack)
    split[...] = stack.astype(BF16)

    def stacked(first, count):
        return split[:, pl.ds(pl.multiple_of(first, 128), count)]

    sub, lane = iota((8, EXTRA), 0), iota((8, EXTRA), 1)
    lower = (lane >= sub * BLOCK) & (lane < sub * BLOCK + BLOCK)
    upper = (lane + EXTRA >= sub * BLOCK) & (lane + EXTRA < sub * BLOCK + BLOCK)
    empty = jnp.where(((lane - sub * BLOCK) & (EXTRA - 1)) >= 64, flag, 0.0)
    for step in range(CHIPS // 8):
        first = (info[step] >> 7) << 7
        pick = hot(iota((reach, 2 * EXTRA), 0) + first == spots[step : step + 1, :])
        value = jnp.sum(dot(stacked(first, reach), pick), 0, keepdims=True)
        line = jnp.where(upper, value[:, EXTRA:], jnp.where(lower, value[:, :EXTRA], empty))
        back[8 * step : 8 * step + 8, :] = line
    fields = fields_of(near[:, mine.shape[1] - EXTRA :]).astype(I32)
    filled = fields[4:5, :] > 0

    @pl.when(jnp.max(fields[4:5, :].astype(F32)) > 0)
    def _():
        total = info[18]
        first = (total >> 7) << 7
        shift = iota((2 * EXTRA, SPILL), 0) - iota((2 * EXTRA, SPILL), 1)
        pick = hot(shift == total - first)
        value = jnp.sum(dot(stacked(first, 2 * EXTRA), pick), 0, keepdims=True)
        source = (iota((CHIPS, SPILL), 0) == fields[7:8, :]) & filled
        line = hot(iota((EXTRA, SPILL), 0) == fields[6:7, :])
        total = back[...]
        for part in thirds(value):
            held = jnp.where(source, part.astype(F32), 0.0).astype(BF16)
            total = total + dot(held, line, COLS)
        back[...] = total


def home_kernel(me, back, place, highest, flag):
    rows = place.shape[1]
    base = (me[0] & 7) * BLOCK
    pick = hot(iota((CHIPS, rows), 0) == place[0:1, :])
    lines = back[...]
    total = jnp.zeros((EXTRA, rows), F32)
    for part in thirds(lines):
        total = total + dot(part, pick, (((0,), (0,)), ((), ())))
    mine = iota((EXTRA, rows), 0) == ((place[1:2, :] + base) & (EXTRA - 1))
    highest[...] = jnp.sum(jnp.where(mine, total, 0.0), 0, keepdims=True)
    marks = ((iota(lines.shape, 1) - base) & (EXTRA - 1)) >= 64
    flag[0] = jnp.max(jnp.where(marks, lines, 0.0)).astype(I32)


def whole(shape):
    return pl.BlockSpec(shape, lambda *_: (0,) * len(shape))


SCALARS = pl.BlockSpec(memory_space=pltpu.SMEM)
HELD = pl.BlockSpec(memory_space=pltpu.VMEM)

LESS = pltpu.CompilerParams(vmem_limit_bytes=28 * 1024 * 1024)


def held(x):
    return pltpu.with_memory_space_constraint(x, pltpu.VMEM)


def array(shape, dtype):
    return jax.ShapeDtypeStruct(shape, dtype)


def exchange(x):
    return lax.all_to_all(
        x, BOTH, split_axis=0, concat_axis=0, tiled=True, axis_index_groups=GROUPS
    )


def direct(attempt, embed, owner, local_id, rank):
    rows, width = embed.shape
    full = width + EXTRA
    lines = CHIPS * BLOCK
    chunks = lines // CHUNK
    group = lax.axis_index("grp")
    core = group & 1
    me = ((group >> 1) * 8 + lax.axis_index("blk")).astype(I32).reshape(1)
    hop = (core * 2 + 1).astype(I32).reshape(1)
    sent, place = pl.pallas_call(
        functools.partial(send_kernel, attempt),
        grid=(chunks // 4,),
        in_specs=[SCALARS, SCALARS, whole((rows, width))] + [whole((1, rows))] * 3,
        out_specs=[pl.BlockSpec((4 * CHUNK, width), lambda i: (i, 0)), whole((8, rows))],
        out_shape=[array((lines, width), BF16), array((8, rows), I32)],
        scratch_shapes=[
            pltpu.VMEM((rows, width), BF16),
            pltpu.VMEM((1, rows), I32),
            pltpu.VMEM((CHIPS, width), F32),
        ],
        compiler_params=LESS,
        name="send",
    )(me, hop, embed, owner.reshape(1, rows), local_id.reshape(1, rows), rank.reshape(1, rows))
    taken = exchange(sent.reshape(CHIPS, BLOCK, width)).reshape(lines, width)
    spill, spots, fields, info = pl.pallas_call(
        read_kernel,
        in_specs=[HELD],
        out_specs=[HELD, HELD, HELD, SCALARS],
        out_shape=[
            pltpu.VMEM((SPILL, full), BF16),
            pltpu.VMEM((chunks, 2 * EXTRA), I32),
            pltpu.VMEM((chunks, EXTRA, CHUNK), BF16),
            array((32,), I32),
        ],
        scratch_shapes=[
            pltpu.VMEM((SPILL, full), F32),
            pltpu.VMEM((CHIPS, width), F32),
            pltpu.VMEM((chunks, CHUNK), I32),
        ],
        compiler_params=LESS,
        name="read",
    )(held(taken))
    beside = [(i, i ^ (1 + (i >> 3 & 1) * 2)) for i in range(2 * CHIPS)]
    near = lax.ppermute(spill, BOTH, beside)
    packed = pl.pallas_call(
        pack_kernel,
        in_specs=[SCALARS, HELD, HELD, HELD],
        out_specs=HELD,
        out_shape=pltpu.VMEM((PACKED, full), BF16),
        compiler_params=LESS,
        cost_estimate=pl.CostEstimate(
            flops=2 * lines * WINDOW * full, bytes_accessed=4 * lines * full, transcendentals=0
        ),
        name="pack",
    )(info, held(taken), held(spots), held(fields))
    packed, info = pl.pallas_call(
        append_kernel,
        in_specs=[SCALARS, HELD, HELD],
        out_specs=[HELD, SCALARS],
        out_shape=[pltpu.VMEM((PACKED, full), BF16), array((32,), I32)],
        input_output_aliases={2: 0},
        compiler_params=LESS,
        name="append",
    )(info, held(near), held(packed))
    swap = [(i, i ^ 1) for i in range(16)]
    other_info = lax.ppermute(info, "grp", swap)
    other = lax.ppermute(packed, "grp", swap)
    best = pl.pallas_call(
        own_kernel,
        in_specs=[SCALARS, HELD],
        out_specs=HELD,
        out_shape=pltpu.VMEM((1, PACKED), F32),
        scratch_shapes=[pltpu.VMEM((PACKED, EXTRA), I32), pltpu.VMEM((8, PACKED), I32)],
        compiler_params=LESS,
        cost_estimate=pl.CostEstimate(
            flops=2 * 1024 * 1024 * width, bytes_accessed=2 * PACKED * full, transcendentals=0
        ),
        name="own",
    )(info, held(packed))
    back = pl.pallas_call(
        other_kernel,
        in_specs=[SCALARS, SCALARS] + [HELD] * 5,
        out_specs=HELD,
        out_shape=pltpu.VMEM((CHIPS, EXTRA), F32),
        scratch_shapes=[
            pltpu.VMEM((1, PACKED + 2 * TILE), F32),
            pltpu.VMEM((16, PACKED + 2 * TILE), BF16),
            pltpu.VMEM((PACKED, EXTRA), I32),
            pltpu.VMEM((8, PACKED), I32),
        ],
        compiler_params=LESS,
        name="other",
    )(info, other_info, held(packed), held(other), held(near), held(best), held(spots))
    home = exchange(back)
    highest, flag = pl.pallas_call(
        home_kernel,
        in_specs=[SCALARS, whole((CHIPS, EXTRA)), whole((8, rows))],
        out_specs=[whole((1, rows)), SCALARS],
        out_shape=[array((1, rows), F32), array((1,), I32)],
        compiler_params=LESS,
        name="home",
    )(me, home, place)
    return highest.reshape(rows), flag[0]


def group_kernel(queries, keys, best_in, best, marks, bounds):
    best[...] = best_in[...]
    rows = keys.shape[0]
    score(queries, rows, keys, rows, best, marks, bounds)


def by_group(embed, owner, local_id, rank):
    n_group, n_block = lax.axis_size("grp"), lax.axis_size("blk")
    row_count, columns = embed.shape
    capacity = row_count // 8
    width = n_group * capacity
    full = columns + EXTRA
    wide = embed.astype(F32)
    unit = (wide * lax.rsqrt(jnp.sum(wide * wide, 1, keepdims=True) + EPS)).astype(BF16)
    target = owner[:, 0]
    onehot = (target[:, None] == jnp.arange(n_group, dtype=I32)[None, :]).astype(I32)
    position = jnp.sum((jnp.cumsum(onehot, 0) - 1) * onehot, 1)
    slot_index = target * capacity + position
    fields = jnp.stack([local_id, target, rank >> 8, rank & 255, jnp.ones_like(rank)], 1)
    fields = jnp.pad(fields, ((0, 0), (0, EXTRA - 5))).astype(BF16)
    sent = jnp.zeros((width, full), BF16).at[slot_index].set(jnp.concatenate([unit, fields], 1))
    routed = lax.all_to_all(
        sent.reshape(n_group, capacity, full), "grp", split_axis=0, concat_axis=0, tiled=True
    ).reshape(width, full)
    best = jnp.full((1, width), -1.0, F32)
    for by in range(n_block):
        turn = [(i, (i + by) % n_block) for i in range(n_block)]
        best = pl.pallas_call(
            group_kernel,
            in_specs=[whole((width, full))] * 2 + [whole((1, width))],
            out_specs=whole((1, width)),
            out_shape=array((1, width), F32),
            scratch_shapes=[pltpu.VMEM((width, EXTRA), I32), pltpu.VMEM((8, width), I32)],
            compiler_params=LESS,
            name="group",
        )(routed, lax.ppermute(routed, "blk", turn) if by else routed, best)
    home = lax.all_to_all(
        best.reshape(n_group, capacity), "grp", split_axis=0, concat_axis=0, tiled=True
    )
    return home.reshape(width)[slot_index]


def per_device(*arrays):
    highest, flag = direct(0, *arrays)

    def again():
        second, still = direct(1, *arrays)
        return lax.cond(still > 0, lambda: by_group(*arrays), lambda: second)

    return lax.cond(flag > 0, again, lambda: highest)


def solution(mesh):
    in_specs = (
        P(("grp", "blk"), None),
        P(("grp", "blk"), None),
        P(("grp", "blk")),
        P(("grp", "blk")),
    )
    out_specs = P(("grp", "blk"))
    return jax.shard_map(
        per_device, mesh=mesh, in_specs=in_specs, out_specs=out_specs, check_vma=False
    )
```
